128 devices in a mesh: row: 8 (over y_hi, z), col: 16 (over x, y_lo, core).
Axes of the slice: x: 4, y: 4 (y_hi: 2, y_lo: 2; y = y_hi * 2 + y_lo), z: 4, core: 2. Of those that a mesh axis runs over, the one named last changes fastest.
Arguments:
- tokens: float32 [16384, 1024], P(('row', 'col')), may hold values from -6 to 6
- cotangent: float32 [16384, 1024], P(('row', 'col')), may hold values from -6 to 6
- timestep: int32 [16], replicated, may hold values from 0 to 999
- class_label: int32 [16], replicated, may hold values from 0 to 1000
- class_table: bfloat16 [1001, 1024], P(None, 'row'), may hold values from -6 to 6
- ada_weight: bfloat16 [2, 1024, 6144], P(None, 'row', 'col'), may hold values from -0.1875 to 0.1875
- ada_bias: float32 [2, 6144], replicated, may hold values from -2 to 2
- qkv_weight: bfloat16 [2, 1024, 3072], P(None, 'row', 'col'), may hold values from -0.1875 to 0.1875
- qv_bias: float32 [2, 2, 1024], P(None, None, 'col'), may hold values from -3 to 3
- proj_weight: bfloat16 [2, 1024, 1024], P(None, 'col', 'row'), may hold values from -0.75 to 0.75
- proj_bias: float32 [2, 1024], replicated, may hold values from -2 to 2
- fc1_weight: bfloat16 [2, 1024, 4096], P(None, 'row', 'col'), may hold values from -0.1875 to 0.1875
- fc1_bias: float32 [2, 4096], P(None, 'col'), may hold values from -3 to 3
- fc2_weight: bfloat16 [2, 4096, 1024], P(None, 'col', 'row'), may hold values from -0.09375 to 0.09375
- fc2_bias: float32 [2, 1024], replicated, may hold values from -2 to 2
Outputs:
- mixed: float32 [16384, 1024], P(('row', 'col'))
- tokens_grad: float32 [16384, 1024], P(('row', 'col'))
- cond_grad: float32 [16, 1024], P(None, 'row')
- table_grad: float32 [1001, 1024], P(None, 'row')
- ada_weight_grad: float32 [2, 1024, 6144], P(None, 'row', 'col')
- ada_bias_grad: float32 [2, 6144], replicated
- qkv_weight_grad: float32 [2, 1024, 3072], P(None, 'row', 'col')
- qv_bias_grad: float32 [2, 2, 1024], P(None, None, 'col')
- proj_weight_grad: float32 [2, 1024, 1024], P(None, 'col', 'row')
- proj_bias_grad: float32 [2, 1024], replicated
- fc1_weight_grad: float32 [2, 1024, 4096], P(None, 'row', 'col')
- fc1_bias_grad: float32 [2, 4096], P(None, 'col')
- fc2_weight_grad: float32 [2, 4096, 1024], P(None, 'col', 'row')
- fc2_bias_grad: float32 [2, 1024], replicated
The draws below stay inside these ranges and needn't reach their ends.
All inputs are finite; a program needn't handle non-finite values.
Results may differ from the reference program's by a relative error of at most 0.02.
Values may be sent and summed in bfloat16 or wider, within the bound.
A program may use at most 192 MiB of HBM per device.

```python
import math
import jax
import jax.numpy as jnp
from jax import lax

D = 1024
HEADS = 16
FF = 4096
CLASSES = 1001
HEAD_DIM = 64
SEQ_LEN = 1024
LAYERS = 2
SEQS = 16
TOKENS = 16384


def set_ends(values, key, low, largest):
    shape = values.shape
    place = [jax.random.randint(jax.random.fold_in(key, axis), (), 0, shape[axis]) for axis in range(len(shape))]
    values = values.at[tuple(place)].set(low)
    longest = shape.index(max(shape))
    place[longest] = (place[longest] + 1) % shape[longest]
    return values.at[tuple(place)].set(largest)


def shard_levels(key, dims, pieces, smallest, top_value):
    level = 1.0
    for axis_at, parts in pieces:
        heights = jax.random.uniform(jax.random.fold_in(jax.random.fold_in(key, 6), axis_at), (parts,), jnp.float32, smallest / len(pieces), top_value / len(pieces))
        level = level * jnp.repeat(jnp.exp(heights), dims[axis_at] // parts).reshape((-1,) + (1,) * (len(dims) - 1 - axis_at))
    return level


def centred(own_key, dims, deviation, limit, cuts=(), kind=jnp.bfloat16):
    entries = deviation * jax.random.normal(own_key, dims, jnp.float32)
    if cuts:
        entries = entries * shard_levels(own_key, dims, cuts, -0.22, 0.18)
    return jnp.clip(entries, -limit, limit).astype(kind)


def setup_inputs(seed: int = 0) -> dict:
    key_of = jax.random.split(jax.random.key(seed), 16)
    tokens = centred(key_of[0], (TOKENS, D), 1.0, 6.0, ((0, 128),), jnp.float32)
    cotangent = centred(key_of[1], (TOKENS, D), 1.0, 6.0, ((0, 128),), jnp.float32)
    timestep = set_ends(jax.random.randint(key_of[2], (SEQS,), 0, 1000), jax.random.fold_in(key_of[2], 1), 0, 999).astype(jnp.int32)
    class_label = set_ends(jax.random.randint(key_of[3], (SEQS,), 0, CLASSES), jax.random.fold_in(key_of[3], 1), 0, CLASSES - 1).astype(jnp.int32)
    class_table = centred(key_of[4], (CLASSES, D), 1.0, 6.0, ((1, 8),))
    ada_weight = centred(key_of[5], (LAYERS, D, 6 * D), D ** -0.5, 0.1875, ((1, 8), (2, 16)))
    ada_bias = centred(key_of[6], (LAYERS, 6 * D), 0.3, 2.0, (), jnp.float32)
    qkv_weight = centred(key_of[7], (LAYERS, D, 3 * D), D ** -0.5, 0.1875, ((1, 8), (2, 16)))
    qv_bias = centred(key_of[8], (LAYERS, 2, D), 0.5, 3.0, ((2, 16),), jnp.float32)
    proj_weight = centred(key_of[9], (LAYERS, D, D), HEAD_DIM ** -0.5, 0.75, ((1, 16), (2, 8)))
    proj_bias = centred(key_of[10], (LAYERS, D), 0.3, 2.0, (), jnp.float32)
    fc1_weight = centred(key_of[11], (LAYERS, D, FF), D ** -0.5, 0.1875, ((1, 8), (2, 16)))
    fc1_bias = centred(key_of[12], (LAYERS, FF), 0.5, 3.0, ((1, 16),), jnp.float32)
    fc2_weight = centred(key_of[13], (LAYERS, FF, D), FF ** -0.5, 0.09375, ((1, 16), (2, 8)))
    fc2_bias = centred(key_of[14], (LAYERS, D), 0.3, 2.0, (), jnp.float32)
    return dict(tokens=tokens, cotangent=cotangent, timestep=timestep, class_label=class_label, class_table=class_table, ada_weight=ada_weight, ada_bias=ada_bias, qkv_weight=qkv_weight, qv_bias=qv_bias, proj_weight=proj_weight, proj_bias=proj_bias, fc1_weight=fc1_weight, fc1_bias=fc1_bias, fc2_weight=fc2_weight, fc2_bias=fc2_bias)


@jax.custom_vjp
def low(v):
    return lax.optimization_barrier(v.astype(jnp.bfloat16)).astype(jnp.float32)

@jax.custom_vjp
def low_back(v):
    return v

def low_keep(v):
    return (low(v), None)

def low_pass(kept, grad):
    return (grad,)

def back_keep(v):
    return (v, None)

def back_low(kept, grad):
    return (low(grad),)
low.defvjp(low_keep, low_pass)
low_back.defvjp(back_keep, back_low)
GELU_COEF = math.sqrt(2.0 / math.pi)

def product(left, right):
    return jnp.dot(left, right, precision=lax.Precision.HIGHEST, preferred_element_type=jnp.float32)

def silu(value):
    return value * jax.nn.sigmoid(value)

def gelu(value):
    return 0.5 * value * (1.0 + jnp.tanh(GELU_COEF * (value + 0.044715 * value * value * value)))

def layer_norm(value):
    average = lax.optimization_barrier(jnp.mean(value, axis=-1, keepdims=True))
    centered = value - average
    variance = lax.optimization_barrier(jnp.mean(centered * centered, axis=-1, keepdims=True))
    return centered * lax.rsqrt(variance + 1e-06)

def timestep_waves(stamps):
    half_width = D // 2
    frequency = jnp.exp(-math.log(10000.0) * jnp.arange(half_width, dtype=jnp.float32) / half_width)
    angles = stamps.astype(jnp.float32)[:, None] * frequency[None, :]
    return jnp.concatenate([jnp.cos(angles), jnp.sin(angles)], axis=1)

def attend(packed):
    heads = packed.reshape(SEQ_LEN, HEADS, 3, HEAD_DIM)
    query_rows = heads[:, :, 0]
    key_rows = heads[:, :, 1]
    value_rows = heads[:, :, 2]
    score_scale = HEAD_DIM ** (-0.5)
    scores = low_back(jnp.einsum('qhd,khd->hqk', query_rows, key_rows, precision=lax.Precision.HIGHEST) * score_scale)
    top = lax.optimization_barrier(jnp.max(scores, axis=2, keepdims=True))
    raised = jnp.exp(scores - top)
    weights = low(raised / lax.optimization_barrier(jnp.sum(raised, axis=2, keepdims=True)))
    output = jnp.einsum('hqk,khd->qhd', weights, value_rows, precision=lax.Precision.HIGHEST)
    return output.reshape(SEQ_LEN, D)

def block_forward(latent, offset, params, stamps, klass):
    class_table, ada_weight, ada_bias, qkv_weight, qv_bias, proj_weight, proj_bias, fc1_weight, fc1_bias, fc2_weight, fc2_bias = params
    condition = timestep_waves(stamps) + class_table[klass] + offset
    hidden = latent
    for block_index in range(LAYERS):
        modulation = product(silu(condition), ada_weight[block_index]) + ada_bias[block_index]
        shift_one, scale_one, gate_one, shift_two, scale_two, gate_two = jnp.split(modulation, 6, axis=1)
        normed = low(layer_norm(hidden) * (1.0 + scale_one) + shift_one)
        pair = qv_bias[block_index].reshape(2, HEADS, HEAD_DIM)
        qkv_bias = jnp.stack([pair[0], jnp.zeros_like(pair[0]), pair[1]], axis=1).reshape(3 * D)
        packed = low(low_back(product(normed, qkv_weight[block_index]) + qkv_bias))
        attended = low(low_back(attend(packed)))
        branch = low_back(product(attended, proj_weight[block_index]) + proj_bias[block_index])
        hidden = hidden + gate_one * branch
        normed_two = low(layer_norm(hidden) * (1.0 + scale_two) + shift_two)
        inner = low_back(product(normed_two, fc1_weight[block_index]) + fc1_bias[block_index])
        active = low(gelu(inner))
        branch = low_back(product(active, fc2_weight[block_index]) + fc2_bias[block_index])
        hidden = hidden + gate_two * branch
    return hidden

def reference(tokens, cotangent, timestep, class_label, class_table, ada_weight, ada_bias, qkv_weight, qv_bias, proj_weight, proj_bias, fc1_weight, fc1_bias, fc2_weight, fc2_bias):
    params = tuple((weight.astype(jnp.float32) for weight in (class_table, ada_weight, ada_bias, qkv_weight, qv_bias, proj_weight, proj_bias, fc1_weight, fc1_bias, fc2_weight, fc2_bias)))
    latents = tokens.astype(jnp.float32).reshape(SEQS, SEQ_LEN, D)
    backs = cotangent.astype(jnp.float32).reshape(SEQS, SEQ_LEN, D)
    zero_grads = tuple((jnp.zeros_like(weight) for weight in params))

    def one_latent(totals, inputs):
        latent, back, stamp, klass = inputs
        offset = jnp.zeros((1, D), jnp.float32)

        def forward(latent_in, offset_in, *weights):
            return block_forward(latent_in, offset_in, weights, stamp[None], klass[None])
        output, pullback = jax.vjp(forward, latent, offset, *params)
        grads = pullback(back)
        totals = tuple((total + grad for total, grad in zip(totals, grads[2:])))
        return (totals, (output, grads[0], grads[1][0]))
    totals, (outputs, latent_grads, cond_grads) = lax.scan(one_latent, zero_grads, (latents, backs, timestep, class_label))
    mixed = outputs.reshape(TOKENS, D)
    tokens_grad = latent_grads.reshape(TOKENS, D)
    return (mixed, tokens_grad, cond_grads, totals[0], totals[1], totals[2], totals[3], totals[4], totals[5], totals[6], totals[7], totals[8], totals[9], totals[10])
```

```python
import functools
import math

import jax
import jax.numpy as jnp
from jax import lax
from jax.experimental import pallas as pl
from jax.experimental.pallas import tpu as pltpu
from jax.sharding import Mesh
from jax.sharding import PartitionSpec as P

MESH = pl.DeviceIdType.MESH
HEAD_DIM = 64
SEQ_LEN = 1024
GELU_COEF = math.sqrt(2.0 / math.pi)
LOG_BASE = math.log(10000.0)
F32 = jnp.float32
BF16 = jnp.bfloat16
TOK = 128
PAIR = 2 * TOK
HALF = TOK // 2
VMEM_LIMIT = 60 * 1024 * 1024


def nn(left, right):
    return lax.dot_general(left, right, (((1,), (0,)), ((), ())), preferred_element_type=F32)


def nt(left, right):
    return lax.dot_general(left, right, (((1,), (1,)), ((), ())), preferred_element_type=F32)


def tn(left, right):
    return lax.dot_general(left, right, (((0,), (0,)), ((), ())), preferred_element_type=F32)


class Group:
    def __init__(self):
        me = lax.axis_index("g")
        self.me = me
        self.core = lax.rem(me, 2)
        chip = lax.div(me, 2)
        x, y = lax.div(chip, 2), lax.rem(chip, 2)
        self.chips = (chip, 2 * x + 1 - y, 2 * (1 - x) + y, 2 * (1 - x) + 1 - y)
        self.peers = tuple(2 * c + self.core for c in self.chips)
        self.others = tuple(2 * c + 1 - self.core for c in self.chips)
        self.sibling = self.others[0]

        self.near = tuple({"g": device} for device in (self.sibling, *self.peers[1:3]))
        self.everyone = self.peers[1:] + self.others


class Owners:
    def __init__(self):
        row, self.x = lax.axis_index("row"), lax.axis_index("xh")
        self.y, self.z = lax.div(row, 4), lax.rem(row, 4)
        self.up, self.across, self.down = (lax.rem(self.z + by, 4) for by in (1, 2, 3))
        self.slot = self.z * 4 + self.y * 2 + self.x
        self.to_x, self.to_y = {"xh": 1 - self.x}, {"row": (1 - self.y) * 4 + self.z}
        self.to_up, self.to_down = {"row": self.y * 4 + self.up}, {"row": self.y * 4 + self.down}
        self.to_across = {"row": self.y * 4 + self.across}
        self.near = (self.to_x, self.to_y, self.to_up, self.to_down)


def greet(devices):
    for device in devices:
        pl.semaphore_signal(pltpu.get_barrier_semaphore(), inc=1, device_id=device, device_id_type=MESH)


def met(devices):
    pl.semaphore_wait(pltpu.get_barrier_semaphore(), len(devices))


def remote(src, dst, send, recv, number, device):
    return pltpu.make_async_remote_copy(
        src_ref=src, dst_ref=dst, send_sem=send.at[number], recv_sem=recv.at[number],
        device_id=device, device_id_type=MESH,
    )


class OwnersGather:
    scratch = (pltpu.SemaphoreType.DMA((6,)), pltpu.SemaphoreType.DMA((6,)))

    def __init__(self, owners, ref, send, recv):
        self.owners, self.ref, self.send, self.recv = owners, ref, send, recv

    def copy(self, number, first, count, device):
        part = self.ref.at[pl.ds(first, count)]
        return remote(part, part, self.send, self.recv, number, device)

    def step(self, step):
        o = self.owners
        pair, four, up, across, down = o.z * 4 + o.y * 2, o.z * 4, o.up * 4, o.across * 4, o.down * 4
        if step == 0:
            self.copy(0, o.slot, 1, o.to_x).start()
        if step == 1:
            self.copy(0, pair + 1 - o.x, 1, o.to_x).wait_recv()
            self.copy(1, pair, 2, o.to_y).start()
        if step == 2:
            self.copy(1, four + (1 - o.y) * 2, 2, o.to_y).wait_recv()
            self.copy(2, four, 4, o.to_up).start()
            self.copy(3, four, 4, o.to_down).start()
        if step == 3:
            self.copy(2, down, 4, o.to_up).wait_recv()
            self.copy(4, down, 2, o.to_up).start()
            self.copy(3, up, 4, o.to_down).wait_recv()
            self.copy(5, up + 2, 2, o.to_down).start()
        if step == 4:
            self.copy(4, across, 2, o.to_up).wait_recv()
            self.copy(5, across + 2, 2, o.to_down).wait_recv()
            self.copy(0, o.slot, 1, o.to_x).wait_send()
            self.copy(1, pair, 2, o.to_y).wait_send()
            self.copy(2, four, 4, o.to_up).wait_send()
            self.copy(3, four, 4, o.to_down).wait_send()
            self.copy(4, down, 2, o.to_up).wait_send()
            self.copy(5, up + 2, 2, o.to_down).wait_send()


class OwnersScatter:
    @staticmethod
    def scratch(rows):
        shapes = ((2, 2), (2, 4), (2, 4), (2,), (2,), (1,), (1,))
        return (
            *(pltpu.VMEM((*shape, rows, 128), BF16) for shape in shapes),
            pltpu.VMEM((4, rows, 128), F32),
            pltpu.SemaphoreType.DMA((6,)),
            pltpu.SemaphoreType.DMA((6,)),
        )

    def __init__(self, owners, parts, out, in0, out1, in1, out2, in2, out3, in3, total, send, recv):
        self.owners, self.parts, self.out, self.total = owners, parts, out, total
        self.out1, self.in0, self.in1 = out1, in0, in1
        self.out2, self.in2, self.out3, self.in3 = out2, in2, out3, in3
        across = owners.across * 4
        self.copies = [
            remote(parts.at[pl.ds(across, 2)], in0.at[0], send, recv, 0, owners.to_up),
            remote(parts.at[pl.ds(across + 2, 2)], in0.at[1], send, recv, 1, owners.to_down),
            remote(out1.at[0], in1.at[0], send, recv, 2, owners.to_up),
            remote(out1.at[1], in1.at[1], send, recv, 3, owners.to_down),
            remote(out2, in2, send, recv, 4, owners.to_y),
            remote(out3, in3, send, recv, 5, owners.to_x),
        ]

    def step(self, step):
        o, copies, parts, total = self.owners, self.copies, self.parts, self.total
        up, down = o.up * 4, o.down * 4
        if step == 0:
            copies[0].start()
            copies[1].start()
        if step == 1:
            copies[0].wait_recv()
            self.out1[0, 0:2] = (parts[pl.ds(up, 2)].astype(F32) + self.in0[0].astype(F32)).astype(BF16)
            self.out1[0, 2:4] = parts[pl.ds(up + 2, 2)]
            copies[2].start()
            copies[1].wait_recv()
            self.out1[1, 0:2] = parts[pl.ds(down, 2)]
            self.out1[1, 2:4] = (parts[pl.ds(down + 2, 2)].astype(F32) + self.in0[1].astype(F32)).astype(BF16)
            copies[3].start()
        if step == 2:
            copies[2].wait_recv()
            copies[3].wait_recv()
            for block in range(4):
                total[block] = (
                    parts[o.z * 4 + block].astype(F32)
                    + self.in1[0, block].astype(F32)
                    + self.in1[1, block].astype(F32)
                )
            self.out2[...] = total[pl.ds((1 - o.y) * 2, 2)].astype(BF16)
            copies[4].start()
        if step == 3:
            copies[4].wait_recv()
            total[0:2] = total[pl.ds(o.y * 2, 2)] + self.in2[...].astype(F32)
            self.out3[...] = total[pl.ds(1 - o.x, 1)].astype(BF16)
            copies[5].start()
        if step == 4:
            copies[5].wait_recv()
            self.out[...] = total[o.x] + self.in3[0].astype(F32)
            for copy in copies:
                copy.wait_send()


def owner_place(slot):
    z, y, half = slot // 4, slot // 2 % 2, slot % 2
    return y * 4 + z, half


def place_attention(land, qkv, proj):
    for slot in range(16):
        part, half = owner_place(slot)
        cols = slice(part * 128, part * 128 + 128)
        for kind in range(3):
            first = kind * 128 + half * 64
            qkv[first : first + 64, cols] = land[slot, kind * 64 : kind * 64 + 64, :]
        proj[half * 64 : half * 64 + 64, cols] = land[slot, 192:256, :]


def place_mlp(land, fc1, fc2):
    units = land.shape[1] // 2
    for slot in range(16):
        part, half = owner_place(slot)
        cols, rows = slice(part * 128, part * 128 + 128), slice(half * units, half * units + units)
        fc1[rows, cols] = land[slot, :units, :]
        fc2[rows, cols] = land[slot, units:, :]


def token_rows(device):
    return pl.ds(pl.multiple_of(device * TOK, TOK), TOK)


def chip_rows(chip):
    return pl.ds(pl.multiple_of(chip * PAIR, PAIR), PAIR)


class Gather:
    def __init__(self, group, full, send, recv):
        self.group, self.full, self.send, self.recv = group, full, send, recv
        self.started = []

    def copy(self, number, owner, device, first=0, count=TOK):
        rows = pl.ds(pl.multiple_of(owner * TOK + first, HALF), count)
        part = self.full.at[rows]
        return remote(part, part, self.send, self.recv, number, {"g": device})

    def go(self, *place):
        copy = self.copy(*place)
        copy.start()
        self.started.append(copy)

    def got(self, *place):
        self.copy(*place).wait_recv()

    def start(self):
        group = self.group
        self.go(2, group.me, group.peers[2])
        self.go(1, group.me, group.peers[1])
        self.go(0, group.me, group.sibling)

    def arrive(self, chip):
        group = self.group
        sibling = group.sibling
        if chip == 0:
            self.got(0, sibling, sibling)
        if chip == 1:
            self.got(1, group.peers[1], sibling)
            self.go(3, group.peers[1], group.peers[2], HALF, HALF)
            self.got(2, group.peers[2], sibling)
            self.go(4, group.peers[2], group.peers[1], 0, HALF)
            self.go(5, group.peers[1], sibling)
            self.go(6, group.peers[2], sibling)
            self.got(5, group.others[1], sibling)
        if chip == 2:
            self.got(6, group.others[2], sibling)
        if chip == 3:
            self.got(4, group.peers[3], sibling, 0, HALF)
            self.go(7, group.peers[3], sibling, 0, HALF)
            self.got(3, group.peers[3], sibling, HALF, HALF)
            self.go(8, group.peers[3], sibling, HALF, HALF)
            self.got(7, group.others[3], sibling, 0, HALF)
            self.got(8, group.others[3], sibling, HALF, HALF)

    def finish(self):
        for copy in self.started:
            copy.wait_send()


class Scatter:
    scratch = (
        pltpu.VMEM((4, TOK, 1024), F32),
        pltpu.VMEM((4, TOK, 1024), BF16),
        pltpu.VMEM((4, TOK, 1024), BF16),
        pltpu.VMEM((3, TOK, 1024), BF16),
        pltpu.VMEM((2, HALF, 1024), BF16),
        pltpu.VMEM((2, TOK, 1024), BF16),
        pltpu.SemaphoreType.DMA((10,)),
        pltpu.SemaphoreType.DMA((10,)),
    )

    def __init__(self, group, keep, near_out, near_in, far_out, mid_in, far_in, send, recv):
        self.group, self.keep, self.far_out = group, keep, far_out
        self.near_out, self.near_in, self.mid_in, self.far_in = near_out, near_in, mid_in, far_in
        y, x = ({"g": group.peers[chip]} for chip in (1, 2))
        low, high = pl.ds(0, HALF), pl.ds(HALF, HALF)
        self.copies = [
            *(remote(near_out.at[n], near_in.at[n], send, recv, n, {"g": group.sibling}) for n in range(4)),
            remote(far_out.at[2, low], mid_in.at[0], send, recv, 4, x),
            remote(far_out.at[2, high], mid_in.at[1], send, recv, 5, y),
            remote(far_out.at[0, high], far_in.at[0, high], send, recv, 6, y),
            remote(far_out.at[0, low], far_in.at[0, low], send, recv, 7, y),
            remote(far_out.at[1, low], far_in.at[1, low], send, recv, 8, x),
            remote(far_out.at[1, high], far_in.at[1, high], send, recv, 9, x),
        ]

    def push(self, chip, term):
        self.near_out[chip] = term(self.group.others[chip]).astype(BF16)
        self.copies[chip].start()
        self.keep[chip] = term(self.group.peers[chip])

    def relay(self, chip):
        self.copies[chip].wait_recv()
        total = self.keep[chip] + self.near_in[chip].astype(F32)
        if chip == 0:
            self.keep[0] = total
        if chip == 1:
            self.keep[1] = total
            self.far_out[0, HALF:] = total[HALF:].astype(BF16)
            self.copies[6].start()
        if chip == 2:
            self.keep[2] = total
            self.far_out[1, :HALF] = total[:HALF].astype(BF16)
            self.copies[8].start()
        if chip == 3:
            self.far_out[2] = total.astype(BF16)
            self.copies[4].start()
            self.copies[5].start()

    def across(self):
        self.copies[4].wait_recv()
        self.far_out[0, :HALF] = (self.keep[1, :HALF] + self.mid_in[0].astype(F32)).astype(BF16)
        self.copies[7].start()
        self.copies[5].wait_recv()
        self.far_out[1, HALF:] = (self.keep[2, HALF:] + self.mid_in[1].astype(F32)).astype(BF16)
        self.copies[9].start()

    def result(self):
        for number in (6, 8, 7, 9):
            self.copies[number].wait_recv()
        return self.keep[0] + self.far_in[0].astype(F32) + self.far_in[1].astype(F32)

    def finish(self):
        for copy in self.copies:
            copy.wait_send()


def norm_parts(value):
    average = jnp.mean(value, axis=-1, keepdims=True)
    centered = value - average
    variance = jnp.mean(centered * centered, axis=-1, keepdims=True)
    inverse = lax.rsqrt(variance + 1e-06)
    return centered * inverse, inverse


def norm_back(normal, inverse, grad):
    first = jnp.mean(grad, axis=-1, keepdims=True)
    second = jnp.mean(grad * normal, axis=-1, keepdims=True)
    return (grad - first - normal * second) * inverse


def store_blocks(ref, half, first, value):
    for part in range(8):
        slot = part % 4 * 4 + part // 4 * 2 + half
        ref[slot, first : first + value.shape[0], :] = value[:, part * 128 : part * 128 + 128].astype(ref.dtype)


def column_sum(value):
    return jnp.sum(value, axis=0, keepdims=True)


def attention_forward_stage(
    group, weights, gather, scatter, start,
    hidden, mods, weight, bias, proj, proj_bias,
    middle, branch, full, packed, attended, logsum,
):
    normal, _ = norm_parts(hidden[...])
    full[token_rows(group.me), :] = (normal * (1.0 + mods[1:2]) + mods[0:1]).astype(BF16)
    start()
    gather.start()
    weights.step(0)
    for chip in range(4):
        gather.arrive(chip)
        rows = chip_rows(group.chips[chip])
        packed[rows, :] = (nt(full[rows, :], weight[...]) + bias[...]).astype(BF16)
        if chip == 1:
            weights.step(1)
    weights.step(2)
    order = (3, 2, 1, 0)
    for place, chip in enumerate(order):
        rows = chip_rows(group.chips[chip])
        for head in range(2):
            query = packed[rows, head * 64 : head * 64 + 64] * BF16(HEAD_DIM**-0.5)
            key = packed[:, 128 + head * 64 : 192 + head * 64]
            value = packed[:, 256 + head * 64 : 320 + head * 64]
            scores = nt(key, query)
            top = jnp.max(scores, axis=0, keepdims=True)
            raised = jnp.exp(scores - top)
            total = jnp.sum(raised, axis=0, keepdims=True)
            output = tn(value, raised.astype(BF16)) * (1.0 / total)
            attended[rows, head * 64 : head * 64 + 64] = output.T.astype(BF16)
            logsum[head : head + 1, rows] = top + jnp.log(total)
        scatter.push(chip, lambda device: nn(attended[token_rows(device), :], proj[...]))
        if place:
            scatter.relay(order[place - 1])
        if place == 2:
            weights.step(3)
    scatter.across()
    scatter.relay(0)
    weights.step(4)
    result = scatter.result() + proj_bias[...]
    branch[...] = result
    middle[...] = hidden[...] + mods[2:3] * result
    gather.finish()
    scatter.finish()


def mlp_forward_stage(
    group, weights, gather, scatter,
    middle, mods, weight, bias, weight_two, bias_two,
    output, branch, full, inner, active,
):
    normal, _ = norm_parts(middle[...])
    full[token_rows(group.me), :] = (normal * (1.0 + mods[4:5]) + mods[3:4]).astype(BF16)
    gather.start()
    weights.step(0)
    for chip in range(4):
        gather.arrive(chip)
        rows = chip_rows(group.chips[chip])
        value = nt(full[rows, :], weight[...]) + bias[...]
        inner[rows, :] = value
        bent = jnp.tanh(GELU_COEF * (value + 0.044715 * value * value * value))
        active[rows, :] = (0.5 * value * (1.0 + bent)).astype(BF16)
        scatter.push(chip, lambda device: nn(active[token_rows(device), :], weight_two[...]))
        if chip:
            scatter.relay(chip - 1)
            weights.step(chip)
    scatter.relay(3)
    scatter.across()
    weights.step(4)
    result = scatter.result() + bias_two[...]
    branch[...] = result
    output[...] = middle[...] + mods[5:6] * result
    gather.finish()
    scatter.finish()


def mlp_backward_stage(
    group, owned_sum, gather, scatter, start,
    grad, mods, middle, branch, branch_one, weight, weight_two, full_two, inner, active,
    grad_middle, grad_attn, sums, weight_grads, bias_grad, full, grad_inner,
):
    grad_mlp = (mods[5:6] * grad[...]).astype(BF16)
    full[token_rows(group.me), :] = grad_mlp
    start()
    gather.start()
    owned_sum.step(0)
    sums[0:1, :] = column_sum(grad[...] * branch[...])
    sums[1:2, :] = column_sum(grad_mlp.astype(F32))
    total = jnp.zeros((1, inner.shape[1]), F32)
    for chip in range(4):
        gather.arrive(chip)
        rows = chip_rows(group.chips[chip])
        grad_active = nt(full[rows, :], weight_two[...])
        value = inner[rows, :]
        bent = jnp.tanh(GELU_COEF * (value + 0.044715 * value * value * value))
        slope = GELU_COEF * (1.0 + (3 * 0.044715) * value * value)
        low = (grad_active * (0.5 * (1.0 + bent) + 0.5 * value * (1.0 - bent * bent) * slope)).astype(BF16)
        grad_inner[rows, :] = low
        total = total + column_sum(low.astype(F32))
        scatter.push(chip, lambda device: nn(grad_inner[token_rows(device), :], weight[...]))
        if chip:
            scatter.relay(chip - 1)
            owned_sum.step(chip)
    scatter.relay(3)
    scatter.across()
    bias_grad[...] = total
    units = weight.shape[0] // 2
    for half in range(2):
        cols = slice(half * units, half * units + units)
        store_blocks(weight_grads, half, 0, tn(grad_inner[:, cols], full_two[...]))
        store_blocks(weight_grads, half, units, tn(active[:, cols], full[...]))
    result = scatter.result()
    normal, inverse = norm_parts(middle[...])
    sums[2:3, :] = column_sum(result)
    sums[3:4, :] = column_sum(result * normal)
    back = grad[...] + norm_back(normal, inverse, (1.0 + mods[4:5]) * result)
    grad_middle[...] = back
    low = (mods[2:3] * back).astype(BF16)
    grad_attn[...] = low
    sums[4:5, :] = column_sum(back * branch_one[...])
    sums[5:6, :] = column_sum(low.astype(F32))
    owned_sum.step(4)
    gather.finish()
    scatter.finish()


def attention_backward_stage(
    group, owned_sum, gather, scatter,
    grad_middle, grad_attn, mods, hidden, weight, proj, full_one, packed, attended, logsum,
    grad_input, sums, weight_grads, bias_grad, full, grad_packed, key_grad, value_grad,
):
    full[token_rows(group.me), :] = grad_attn[...]
    gather.start()
    owned_sum.step(0)
    scale = HEAD_DIM**-0.5
    for chip in range(4):
        gather.arrive(chip)
        rows = chip_rows(group.chips[chip])
        grad_out = nt(full[rows, :], proj[...]).astype(BF16)
        for head in range(2):
            query = packed[rows, head * 64 : head * 64 + 64] * BF16(scale)
            key = packed[:, 128 + head * 64 : 192 + head * 64]
            value = packed[:, 256 + head * 64 : 320 + head * 64]
            part = grad_out[:, head * 64 : head * 64 + 64]
            probs = jnp.exp(nt(key, query) - logsum[head : head + 1, rows])
            grad_probs = nt(value, part)
            delta = jnp.sum(probs * grad_probs, axis=0, keepdims=True)
            grad_scores = (probs * (grad_probs - delta)).astype(BF16)
            grad_packed[rows, head * 64 : head * 64 + 64] = (tn(grad_scores, key) * scale).astype(BF16)
            key_term = nn(grad_scores, query)
            value_term = nn(probs.astype(BF16), part)
            if chip == 0:
                key_grad[head] = key_term
                value_grad[head] = value_term
            else:
                key_grad[head] += key_term
                value_grad[head] += value_term
        if chip in (1, 3):
            owned_sum.step(1 + chip // 2)
    for head in range(2):
        grad_packed[:, 128 + head * 64 : 192 + head * 64] = key_grad[head].astype(BF16)
        grad_packed[:, 256 + head * 64 : 320 + head * 64] = value_grad[head].astype(BF16)
    order = (3, 2, 1, 0)
    for place, chip in enumerate(order):
        scatter.push(chip, lambda device: nn(grad_packed[token_rows(device), :], weight[...]))
        if place:
            scatter.relay(order[place - 1])
    scatter.across()
    scatter.relay(0)
    owned_sum.step(3)
    for part in range(3):
        term = tn(grad_packed[:, part * 128 : part * 128 + 128], full_one[...])
        for half in range(2):
            store_blocks(weight_grads, half, part * 64, term[half * 64 : half * 64 + 64])
    term = tn(attended[...], full[...])
    for half in range(2):
        store_blocks(weight_grads, half, 192, term[half * 64 : half * 64 + 64])
    bias_grad[...] = column_sum(grad_packed[...].astype(F32))
    result = scatter.result()
    normal, inverse = norm_parts(hidden[...])
    sums[6:7, :] = column_sum(result)
    sums[7:8, :] = column_sum(result * normal)
    grad_input[...] = grad_middle[...] + norm_back(normal, inverse, (1.0 + mods[1:2]) * result)
    owned_sum.step(4)
    gather.finish()
    scatter.finish()


class Nothing:
    def step(self, step):
        pass


def forward_kernel(more, *refs):
    hidden, mods, weight, bias, proj, proj_bias, inner_bias, bias_two, mlp_rows, *refs = refs
    if more:
        next_rows, *refs = refs
    middle, branch, full, packed, attended, logsum, fc1, fc2, output, branch_two, full_two, inner, active, *refs = refs
    if more:
        next_qkv, next_proj, *refs = refs
    land, own_send, own_recv, *refs = refs
    if more:
        next_land, next_send, next_recv, *refs = refs
    send, recv, *scatter_refs = refs
    group, owners = Group(), Owners()
    partners = group.near + owners.near
    greet(partners)
    weights = OwnersGather(owners, land, own_send, own_recv)
    land[owners.slot] = mlp_rows[...]
    scatter = Scatter(group, *scatter_refs)
    attention_forward_stage(
        group, weights, Gather(group, full, send, recv), scatter, lambda: met(partners),
        hidden, mods, weight, bias, proj, proj_bias, middle, branch, full, packed, attended, logsum,
    )
    place_mlp(land, fc1, fc2)
    weights = Nothing()
    if more:
        weights = OwnersGather(owners, next_land, next_send, next_recv)
        next_land[owners.slot] = next_rows[...]
    mlp_forward_stage(
        group, weights, Gather(group, full_two, send, recv), scatter,
        middle, mods, fc1, inner_bias, fc2, bias_two, output, branch_two, full_two, inner, active,
    )
    if more:
        place_attention(next_land, next_qkv, next_proj)


def backward_kernel(more, *refs):
    grad, mods, middle, branch_two, branch, fc1, fc2, full_two, inner, active, *refs = refs
    hidden, qkv, proj, full_one, packed, attended, logsum, *refs = refs
    if more:
        parts, *refs = refs
    grad_input, sums, attn_parts, qkv_sum, fc1_sum, mlp_owned, *refs = refs
    if more:
        attn_owned, *refs = refs
    grad_middle, grad_attn, mlp_parts, full, full_attn, grad_inner, grad_packed, key_grad, value_grad, *refs = refs
    mlp_refs, refs = refs[:10], refs[10:]
    if more:
        attn_refs, refs = refs[:10], refs[10:]
    send, recv, *scatter_refs = refs
    group, owners = Group(), Owners()
    partners = group.near + owners.near
    greet(partners)
    scatter = Scatter(group, *scatter_refs)
    owned = OwnersScatter(owners, parts, attn_owned, *attn_refs) if more else Nothing()
    mlp_backward_stage(
        group, owned, Gather(group, full, send, recv), scatter, lambda: met(partners),
        grad, mods, middle, branch_two, branch, fc1, fc2, full_two, inner, active,
        grad_middle, grad_attn, sums, mlp_parts, fc1_sum, full, grad_inner,
    )
    owned = OwnersScatter(owners, mlp_parts, mlp_owned, *mlp_refs)
    attention_backward_stage(
        group, owned, Gather(group, full_attn, send, recv), scatter,
        grad_middle, grad_attn, mods, hidden, qkv, proj, full_one, packed, attended, logsum,
        grad_input, sums, attn_parts, qkv_sum, full_attn, grad_packed, key_grad, value_grad,
    )


def first_kernel(
    rows, terms, bias, qkv, proj, halves, mods,
    land, own_send, own_recv, x_in, y_out, y_in, z_out, z_in, send, recv, all_send, all_recv,
):
    group, owners = Group(), Owners()
    partners = owners.near + (owners.to_across,) + tuple({"g": device} for device in group.everyone)
    greet(partners)
    weights = OwnersGather(owners, land, own_send, own_recv)
    land[owners.slot] = rows[...]
    halves[owners.x] = bias[...]
    met(partners)
    other = 1 - owners.x
    along_x = remote(terms.at[pl.ds(other * 8, 8)], x_in, send, recv, 0, owners.to_x)
    along_x.start()
    bias_there = remote(bias, halves.at[owners.x], send, recv, 1, owners.to_x)
    bias_there.start()
    weights.step(0)
    along_x.wait_recv()
    y_out[owners.x] = terms[pl.ds(owners.x * 8 + (1 - owners.y) * 4, 4)]
    y_out[other] = x_in[pl.ds((1 - owners.y) * 4, 4)]
    along_y = remote(y_out, y_in, send, recv, 2, owners.to_y)
    along_y.start()
    weights.step(1)
    along_y.wait_recv()
    own = terms[pl.ds(owners.x * 8 + owners.y * 4, 4)] + y_in[owners.x]
    far = x_in[pl.ds(owners.y * 4, 4)] + y_in[other]
    for z in range(4):
        z_out[z, owners.x] = own[z]
        z_out[z, other] = far[z]
    along_z = [
        remote(z_out.at[z], z_in.at[number], send, recv, 3 + number, device)
        for number, (z, device) in enumerate(
            ((owners.up, owners.to_up), (owners.across, owners.to_across), (owners.down, owners.to_down))
        )
    ]
    for copy in along_z:
        copy.start()
    weights.step(2)
    total = z_out[owners.z]
    for number, copy in enumerate(along_z):
        copy.wait_recv()
        total = total + z_in[number]
    mods[group.me] = total
    around = [
        remote(mods.at[group.me], mods.at[group.me], all_send, all_recv, number, {"g": device})
        for number, device in enumerate(group.everyone)
    ]
    for copy in around:
        copy.start()
    weights.step(3)
    for number, device in enumerate(group.everyone):
        remote(mods.at[device], mods.at[device], all_send, all_recv, number, {"g": device}).wait_recv()
    remote(bias, halves.at[other], send, recv, 1, owners.to_x).wait_recv()
    weights.step(4)
    place_attention(land, qkv, proj)
    for copy in (along_x, bias_there, along_y, *along_z, *around):
        copy.wait_send()


def last_kernel(
    parts, blocks, own, owned, every, summed, copies,
    *refs,
):
    group, owners = Group(), Owners()
    partners = owners.near + tuple({"g": device} for device in group.everyone)
    greet(partners)
    owned_sum = OwnersScatter(owners, parts, owned, *refs[:10])
    own_send, own_recv, inbox, send, recv, all_send, all_recv = refs[10:]
    gather = OwnersGather(owners, every, own_send, own_recv)
    met(partners)
    around = [
        remote(blocks.at[device], inbox.at[number], send, recv, number, {"g": device})
        for number, device in enumerate(group.everyone)
    ]
    for copy in around:
        copy.start()
    owned_sum.step(0)
    total = blocks[group.me]
    for number, copy in enumerate(around):
        copy.wait_recv()
        total = total + inbox[number]
    rows = blocks.shape[1]
    every[owners.slot, 0:rows] = total
    every[owners.slot, rows:] = own[...]
    gather.step(0)
    gather.step(1)
    owned_sum.step(1)
    gather.step(2)
    gather.step(3)
    owned_sum.step(2)
    gather.step(4)
    total = every[0]
    for slot in range(1, 16):
        total = total + every[slot]
    summed[...] = total
    copies[group.me] = total[0:rows]
    spread = [
        remote(copies.at[group.me], copies.at[group.me], all_send, all_recv, number, {"g": device})
        for number, device in enumerate(group.everyone)
    ]
    for copy in spread:
        copy.start()
    owned_sum.step(3)
    for number, device in enumerate(group.everyone):
        remote(copies.at[device], copies.at[device], all_send, all_recv, number, {"g": device}).wait_recv()
    owned_sum.step(4)
    for copy in (*around, *spread):
        copy.wait_send()


def plain_call(kernel, number, outs, scratch, *operands):
    space = pl.BlockSpec(memory_space=pltpu.VMEM)
    return pl.pallas_call(
        kernel,
        out_shape=[jax.ShapeDtypeStruct(shape, kind) for shape, kind in outs],
        in_specs=[space] * len(operands),
        out_specs=[space] * len(outs),
        scratch_shapes=scratch,
        compiler_params=pltpu.CompilerParams(
            collective_id=number, has_side_effects=True, vmem_limit_bytes=VMEM_LIMIT
        ),
        cost_estimate=pl.CostEstimate(flops=10**10, bytes_accessed=8 << 20, transcendentals=1 << 20),
    )(*operands)


def call(kernel, number, outs, scratch, *operands):
    pair = [pltpu.SemaphoreType.DMA((9,)), pltpu.SemaphoreType.DMA((9,))]
    return plain_call(kernel, number, outs, [*scratch, *pair, *Scatter.scratch], *operands)


def first(rows, terms, bias):
    width = 1024
    outs = [
        ((384, width), BF16), ((128, width), BF16), ((2, *bias.shape), F32), ((8, 2, 8, 128), F32),
    ]
    scratch = [
        pltpu.VMEM((16, *rows.shape), BF16), *OwnersGather.scratch,
        pltpu.VMEM((8, 8, 128), F32), pltpu.VMEM((2, 4, 8, 128), F32), pltpu.VMEM((2, 4, 8, 128), F32),
        pltpu.VMEM((4, 2, 8, 128), F32), pltpu.VMEM((3, 2, 8, 128), F32),
        pltpu.SemaphoreType.DMA((6,)), pltpu.SemaphoreType.DMA((6,)),
        pltpu.SemaphoreType.DMA((7,)), pltpu.SemaphoreType.DMA((7,)),
    ]
    return plain_call(first_kernel, 10, outs, scratch, rows, terms, bias)


def last(parts, blocks, own):
    rows = blocks.shape[1]
    outs = [
        (parts.shape[1:], F32), ((16, rows + own.shape[0], 128), F32), ((rows + own.shape[0], 128), F32),
        (blocks.shape, F32),
    ]
    scratch = [
        *OwnersScatter.scratch(parts.shape[1]), *OwnersGather.scratch, pltpu.VMEM((7, rows, 128), F32),
        *([pltpu.SemaphoreType.DMA((7,))] * 4),
    ]
    return plain_call(last_kernel, 11, outs, scratch, parts, blocks, own)


def forward(operands, rows=None):
    hidden, weight, proj, mlp_rows = operands[0], operands[2], operands[4], operands[8]
    width, units = hidden.shape[1], mlp_rows.shape[0]
    token, whole = ((TOK, width), F32), ((SEQ_LEN, width), BF16)
    outs = [
        token, token, whole, ((SEQ_LEN, weight.shape[0]), BF16), ((SEQ_LEN, proj.shape[0]), BF16), ((2, SEQ_LEN), F32),
        ((units, width), BF16), ((units, width), BF16),
        token, token, whole, ((SEQ_LEN, units), F32), ((SEQ_LEN, units), BF16),
    ]
    scratch = [pltpu.VMEM((16, *mlp_rows.shape), BF16), *OwnersGather.scratch]
    if rows is None:
        return call(functools.partial(forward_kernel, False), 0, outs, scratch, *operands)
    outs += [(weight.shape, BF16), (proj.shape, BF16)]
    scratch += [pltpu.VMEM((16, *rows.shape), BF16), *OwnersGather.scratch]
    return call(functools.partial(forward_kernel, True), 1, outs, scratch, *operands, rows)


def backward(operands, parts=None):
    grad, fc1, qkv = operands[0], operands[5], operands[11]
    width, units = grad.shape[1], fc1.shape[0]
    outs = [
        ((TOK, width), F32), ((8, width), F32), ((16, 256, 128), BF16),
        ((1, qkv.shape[0]), F32), ((1, units), F32), ((units, 128), F32),
    ]
    if parts is not None:
        outs += [(parts.shape[1:], F32)]
    scratch = [
        pltpu.VMEM((TOK, width), F32),
        pltpu.VMEM((TOK, width), BF16),
        pltpu.VMEM((16, units, 128), BF16),
        pltpu.VMEM((SEQ_LEN, width), BF16),
        pltpu.VMEM((SEQ_LEN, width), BF16),
        pltpu.VMEM((SEQ_LEN, units), BF16),
        pltpu.VMEM((SEQ_LEN, qkv.shape[0]), BF16),
        pltpu.VMEM((2, SEQ_LEN, HEAD_DIM), F32),
        pltpu.VMEM((2, SEQ_LEN, HEAD_DIM), F32),
        *OwnersScatter.scratch(units),
    ]
    if parts is None:
        return call(functools.partial(backward_kernel, False), 2, outs, scratch, *operands)
    scratch += OwnersScatter.scratch(parts.shape[1])
    return call(functools.partial(backward_kernel, True), 3, outs, scratch, *operands, parts)


RX = ("row", "xh")
ALL = ("row", "xh", "g")


def highest(left, right):
    return jnp.dot(left, right, precision=lax.Precision.HIGHEST, preferred_element_type=F32)


def highest_tn(left, right):
    return lax.dot_general(
        left, right, (((0,), (0,)), ((), ())), precision=lax.Precision.HIGHEST, preferred_element_type=F32
    )


def highest_nt(left, right):
    return lax.dot_general(
        left, right, (((1,), (1,)), ((), ())), precision=lax.Precision.HIGHEST, preferred_element_type=F32
    )


def on_device(
    tokens, cotangent, timestep, class_label, class_table, ada_weight, ada_bias, qkv_weight, qv_bias,
    proj_weight, proj_bias, fc1_weight, fc1_bias, fc2_weight, fc2_bias,
):
    row_index, half_index, _ = (lax.axis_index(axis) for axis in ALL)
    width = tokens.shape[1]
    width_part = class_table.shape[1]
    latent_count = timestep.shape[0]
    layer_count, _, ada_cols = ada_weight.shape
    units = fc1_weight.shape[2]
    attn_rows = [jnp.concatenate([qkv_weight[l].T, proj_weight[l]]) for l in range(layer_count)]
    mlp_rows = [jnp.concatenate([fc1_weight[l].T, fc2_weight[l]]) for l in range(layer_count)]
    column_ids = row_index * width_part + lax.iota(jnp.int32, width_part)
    half_width = width // 2
    frequency = jnp.exp(-LOG_BASE * (column_ids % half_width).astype(F32) / half_width)
    angles = timestep.astype(F32)[:, None] * frequency[None, :]
    waves = jnp.where(column_ids[None, :] < half_width, jnp.cos(angles), jnp.sin(angles))
    class_hot = (class_label[:, None] == lax.iota(jnp.int32, class_table.shape[0])[None, :]).astype(F32)
    condition = waves + highest(class_hot, class_table.astype(F32))
    cond_act = condition * jax.nn.sigmoid(condition)
    ada_float = ada_weight.astype(F32)
    terms = jnp.stack([highest(cond_act, ada_float[l]) for l in range(layer_count)], axis=1)
    terms = terms.reshape(latent_count // 2, 2, -1, 128).swapaxes(0, 1).reshape(latent_count, -1, 128)
    lines = layer_count * ada_cols // 128
    terms = jnp.pad(terms, ((0, 0), (0, 8 - lines), (0, 0)))
    bias_rows = jnp.concatenate([qv_bias.reshape(layer_count, -1), fc1_bias], axis=1).reshape(-1, 128)
    bias_count = bias_rows.shape[0]
    bias_rows = jnp.pad(bias_rows, ((0, 8 - bias_count), (0, 0)))
    qkv, proj, halves, mod_parts = first(attn_rows[0], terms, bias_rows)
    modulation = mod_parts[:, :, :lines].reshape(8, 2, layer_count, ada_cols).transpose(2, 1, 0, 3)
    modulation = modulation.reshape(layer_count, 6 * width) + ada_bias
    mods = jnp.pad(modulation.reshape(layer_count, 6, width), ((0, 0), (0, 2), (0, 0)))
    halves = halves[:, :bias_count].reshape(2, layer_count, -1)

    saved = []
    hidden = tokens
    for number in range(layer_count):
        query = halves[:, number, :HEAD_DIM].reshape(1, -1)
        value = halves[:, number, HEAD_DIM : 2 * HEAD_DIM].reshape(1, -1)
        qkv_bias = jnp.concatenate([query, jnp.zeros_like(query), value], axis=1)
        inner_bias = halves[:, number, 2 * HEAD_DIM :].reshape(1, -1)
        mod = mods[number]
        later = None if number + 1 == layer_count else attn_rows[number + 1]
        operands = (
            hidden, mod, qkv, qkv_bias, proj, proj_bias[number : number + 1], inner_bias, fc2_bias[number : number + 1],
            mlp_rows[number],
        )
        (
            middle, branch, full, packed, attended, logsum, fc1, fc2, output, branch_two, full_two, inner, active, *later
        ) = forward(operands, later)
        saved.append(
            (middle, branch_two, branch, fc1, fc2, full_two, inner, active, hidden, qkv, proj, full, packed, attended, logsum)
        )
        hidden = output
        if later:
            qkv, proj = later
    mixed = hidden
    grad = cotangent
    small = [None] * layer_count
    attn_grads, mlp_grads = [None] * layer_count, [None] * layer_count
    attn_parts = None
    for number in reversed(range(layer_count)):
        mod = mods[number]
        grad, sums, attn_parts, qkv_sum, fc1_sum, mlp_grads[number], *owned = backward(
            (grad, mod, *saved[number]), attn_parts
        )
        if owned:
            attn_grads[number + 1] = owned[0]
        mod_grad = jnp.concatenate([sums[6:8], sums[4:5], sums[2:4], sums[0:1]])
        small[number] = (mod_grad, sums[5], sums[1], qkv_sum, fc1_sum)
    tokens_grad = grad

    mod_grad, proj_sum, fc2_sum, qkv_sum, fc1_sum = (jnp.stack(parts) for parts in zip(*small))
    mod_send = mod_grad.reshape(layer_count, 2, 8, ada_cols).transpose(2, 1, 0, 3).reshape(8, -1)
    bias_send = jnp.concatenate([proj_sum, fc2_sum]).reshape(2 * layer_count, 8, -1).swapaxes(0, 1).reshape(8, -1)
    mod_size = mod_send.shape[1]
    send = jnp.concatenate([mod_send, bias_send], axis=1).reshape(8, -1, 128)
    qv_sum = qkv_sum.reshape(layer_count, 3, 2, HEAD_DIM)[:, ::2].transpose(2, 0, 1, 3).reshape(2, -1)
    fc1_half = fc1_sum.reshape(layer_count, 2, units).swapaxes(0, 1).reshape(2, -1)
    own = jnp.concatenate([qv_sum, fc1_half], axis=1).reshape(-1, 128)
    own_count = own.shape[0]
    own = jnp.pad(own, ((0, 16 - own_count), (0, 0)))
    attn_grads[0], every, summed, copies = last(attn_parts, send, own)
    every = every[:, : mod_size // 128].reshape(4, 2, 2, 2, layer_count, ada_cols)
    mod_cols = lax.dynamic_index_in_dim(every, half_index, axis=3, keepdims=False)
    mod_cols = mod_cols.transpose(1, 0, 2, 3, 4).reshape(latent_count, layer_count, ada_cols)
    copies = copies.reshape(8, -1)
    ada_bias_grad = copies[:, :mod_size].reshape(8, 2, layer_count, ada_cols).transpose(2, 1, 0, 3)
    ada_bias_grad = ada_bias_grad.reshape(layer_count, 6 * width)
    bias_total = copies[:, mod_size:].reshape(8, 2 * layer_count, -1).swapaxes(0, 1).reshape(2, layer_count, width)
    own_total = summed[send.shape[1] :][:own_count].reshape(2, -1)
    own_total = lax.dynamic_index_in_dim(own_total, half_index, keepdims=False)
    qv_bias_grad = own_total[: layer_count * 2 * HEAD_DIM].reshape(layer_count, 2, HEAD_DIM)
    fc1_bias_grad = own_total[layer_count * 2 * HEAD_DIM :].reshape(layer_count, units)
    ada_weight_grad = jnp.stack([highest_tn(cond_act, mod_cols[:, l]) for l in range(layer_count)])
    cond_part = sum(highest_nt(mod_cols[:, l], ada_float[l]) for l in range(layer_count))
    act_grad = lax.all_gather(cond_part, ("xh", "g"), axis=0).sum(axis=0)
    gate = jax.nn.sigmoid(condition)
    cond_grad = act_grad * (gate * (1.0 + condition * (1.0 - gate)))
    table_grad = highest_tn(class_hot, cond_grad)
    attn_grads, mlp_grads = jnp.stack(attn_grads), jnp.stack(mlp_grads)
    return (
        mixed,
        tokens_grad,
        cond_grad,
        table_grad,
        ada_weight_grad,
        ada_bias_grad,
        attn_grads[:, :192].swapaxes(1, 2),
        qv_bias_grad,
        attn_grads[:, 192:],
        bias_total[0],
        mlp_grads[:, :units].swapaxes(1, 2),
        fc1_bias_grad,
        mlp_grads[:, units:],
        bias_total[1],
    )


def solution(mesh):
    split = Mesh(mesh.devices.reshape(mesh.shape["row"], 2, 8), ALL)
    col = ("xh", "g")
    in_specs = (
        P(ALL, None), P(ALL, None), P(), P(), P(None, "row"), P(None, "row", col), P(),
        P(None, "row", col), P(None, None, col), P(None, col, "row"), P(), P(None, "row", col),
        P(None, col), P(None, col, "row"), P(),
    )
    out_specs = (
        P(ALL, None), P(ALL, None), P(None, "row"), P(None, "row"), P(None, "row", col), P(),
        P(None, "row", col), P(None, None, col), P(None, col, "row"), P(), P(None, "row", col),
        P(None, col), P(None, col, "row"), P(),
    )
    return jax.shard_map(on_device, mesh=split, in_specs=in_specs, out_specs=out_specs, check_vma=False)
```

```python
import functools
import math

import jax
import jax.numpy as jnp
from jax import lax
from jax.experimental import pallas as pl
from jax.experimental.pallas import tpu as pltpu
from jax.sharding import Mesh
from jax.sharding import PartitionSpec as P

MESH = pl.DeviceIdType.MESH
HEAD_DIM = 64
SEQ_LEN = 1024
GELU_COEF = math.sqrt(2.0 / math.pi)
LOG_BASE = math.log(10000.0)
F32 = jnp.float32
BF16 = jnp.bfloat16
TOK = 128
PAIR = 2 * TOK
HALF = TOK // 2
VMEM_LIMIT = 60 * 1024 * 1024


def nn(left, right):
    return lax.dot_general(left, right, (((1,), (0,)), ((), ())), preferred_element_type=F32)


def nt(left, right):
    return lax.dot_general(left, right, (((1,), (1,)), ((), ())), preferred_element_type=F32)


def tn(left, right):
    return lax.dot_general(left, right, (((0,), (0,)), ((), ())), preferred_element_type=F32)


class Group:
    def __init__(self):
        me = lax.axis_index("g")
        self.me = me
        self.core = lax.rem(me, 2)
        chip = lax.div(me, 2)
        x, y = lax.div(chip, 2), lax.rem(chip, 2)
        self.chips = (chip, 2 * x + 1 - y, 2 * (1 - x) + y, 2 * (1 - x) + 1 - y)
        self.peers = tuple(2 * c + self.core for c in self.chips)
        self.others = tuple(2 * c + 1 - self.core for c in self.chips)
        self.sibling = self.others[0]

        self.near = tuple({"g": device} for device in (self.sibling, *self.peers[1:3]))
        self.everyone = self.peers[1:] + self.others


class Owners:
    def __init__(self):
        row, self.x = lax.axis_index("row"), lax.axis_index("xh")
        self.y, self.z = lax.div(row, 4), lax.rem(row, 4)
        self.up, self.across, self.down = (lax.rem(self.z + by, 4) for by in (1, 2, 3))
        self.slot = self.z * 4 + self.y * 2 + self.x
        self.to_x, self.to_y = {"xh": 1 - self.x}, {"row": (1 - self.y) * 4 + self.z}
        self.to_up, self.to_down = {"row": self.y * 4 + self.up}, {"row": self.y * 4 + self.down}
        self.to_across = {"row": self.y * 4 + self.across}
        self.near = (self.to_x, self.to_y, self.to_up, self.to_down)


def greet(devices):
    for device in devices:
        pl.semaphore_signal(pltpu.get_barrier_semaphore(), inc=1, device_id=device, device_id_type=MESH)


def met(devices):
    pl.semaphore_wait(pltpu.get_barrier_semaphore(), len(devices))


def remote(src, dst, send, recv, number, device):
    return pltpu.make_async_remote_copy(
        src_ref=src, dst_ref=dst, send_sem=send.at[number], recv_sem=recv.at[number],
        device_id=device, device_id_type=MESH,
    )


class OwnersGather:
    scratch = (pltpu.SemaphoreType.DMA((6,)), pltpu.SemaphoreType.DMA((6,)))

    def __init__(self, owners, ref, send, recv):
        self.owners, self.ref, self.send, self.recv = owners, ref, send, recv

    def copy(self, number, first, count, device):
        part = self.ref.at[pl.ds(first, count)]
        return remote(part, part, self.send, self.recv, number, device)

    def step(self, step):
        o = self.owners
        pair, four, up, across, down = o.z * 4 + o.y * 2, o.z * 4, o.up * 4, o.across * 4, o.down * 4
        if step == 0:
            self.copy(0, o.slot, 1, o.to_x).start()
        if step == 1:
            self.copy(0, pair + 1 - o.x, 1, o.to_x).wait_recv()
            self.copy(1, pair, 2, o.to_y).start()
        if step == 2:
            self.copy(1, four + (1 - o.y) * 2, 2, o.to_y).wait_recv()
            self.copy(2, four, 4, o.to_up).start()
            self.copy(3, four, 4, o.to_down).start()
        if step == 3:
            self.copy(2, down, 4, o.to_up).wait_recv()
            self.copy(4, down, 2, o.to_up).start()
            self.copy(3, up, 4, o.to_down).wait_recv()
            self.copy(5, up + 2, 2, o.to_down).start()
        if step == 4:
            self.copy(4, across, 2, o.to_up).wait_recv()
            self.copy(5, across + 2, 2, o.to_down).wait_recv()
            self.copy(0, o.slot, 1, o.to_x).wait_send()
            self.copy(1, pair, 2, o.to_y).wait_send()
            self.copy(2, four, 4, o.to_up).wait_send()
            self.copy(3, four, 4, o.to_down).wait_send()
            self.copy(4, down, 2, o.to_up).wait_send()
            self.copy(5, up + 2, 2, o.to_down).wait_send()


class OwnersScatter:
    @staticmethod
    def scratch(rows):
        shapes = ((2, 2), (2, 4), (2, 4), (2,), (2,), (1,), (1,))
        return (
            *(pltpu.VMEM((*shape, rows, 128), BF16) for shape in shapes),
            pltpu.VMEM((4, rows, 128), F32),
            pltpu.SemaphoreType.DMA((6,)),
            pltpu.SemaphoreType.DMA((6,)),
        )

    def __init__(self, owners, parts, out, in0, out1, in1, out2, in2, out3, in3, total, send, recv):
        self.owners, self.parts, self.out, self.total = owners, parts, out, total
        self.out1, self.in0, self.in1 = out1, in0, in1
        self.out2, self.in2, self.out3, self.in3 = out2, in2, out3, in3
        across = owners.across * 4
        self.copies = [
            remote(parts.at[pl.ds(across, 2)], in0.at[0], send, recv, 0, owners.to_up),
            remote(parts.at[pl.ds(across + 2, 2)], in0.at[1], send, recv, 1, owners.to_down),
            remote(out1.at[0], in1.at[0], send, recv, 2, owners.to_up),
            remote(out1.at[1], in1.at[1], send, recv, 3, owners.to_down),
            remote(out2, in2, send, recv, 4, owners.to_y),
            remote(out3, in3, send, recv, 5, owners.to_x),
        ]

    def step(self, step):
        o, copies, parts, total = self.owners, self.copies, self.parts, self.total
        up, down = o.up * 4, o.down * 4
        if step == 0:
            copies[0].start()
            copies[1].start()
        if step == 1:
            copies[0].wait_recv()
            self.out1[0, 0:2] = (parts[pl.ds(up, 2)].astype(F32) + self.in0[0].astype(F32)).astype(BF16)
            self.out1[0, 2:4] = parts[pl.ds(up + 2, 2)]
            copies[2].start()
            copies[1].wait_recv()
            self.out1[1, 0:2] = parts[pl.ds(down, 2)]
            self.out1[1, 2:4] = (parts[pl.ds(down + 2, 2)].astype(F32) + self.in0[1].astype(F32)).astype(BF16)
            copies[3].start()
        if step == 2:
            copies[2].wait_recv()
            copies[3].wait_recv()
            for block in range(4):
                total[block] = (
                    parts[o.z * 4 + block].astype(F32)
                    + self.in1[0, block].astype(F32)
                    + self.in1[1, block].astype(F32)
                )
            self.out2[...] = total[pl.ds((1 - o.y) * 2, 2)].astype(BF16)
            copies[4].start()
        if step == 3:
            copies[4].wait_recv()
            total[0:2] = total[pl.ds(o.y * 2, 2)] + self.in2[...].astype(F32)
            self.out3[...] = total[pl.ds(1 - o.x, 1)].astype(BF16)
            copies[5].start()
        if step == 4:
            copies[5].wait_recv()
            self.out[...] = total[o.x] + self.in3[0].astype(F32)
            for copy in copies:
                copy.wait_send()


def owner_place(slot):
    z, y, half = slot // 4, slot // 2 % 2, slot % 2
    return y * 4 + z, half


def place_attention(land, qkv, proj):
    for slot in range(16):
        part, half = owner_place(slot)
        cols = slice(part * 128, part * 128 + 128)
        for kind in range(3):
            first = kind * 128 + half * 64
            qkv[first : first + 64, cols] = land[slot, kind * 64 : kind * 64 + 64, :]
        proj[half * 64 : half * 64 + 64, cols] = land[slot, 192:256, :]


def place_mlp(land, fc1, fc2):
    units = land.shape[1] // 2
    for slot in range(16):
        part, half = owner_place(slot)
        cols, rows = slice(part * 128, part * 128 + 128), slice(half * units, half * units + units)
        fc1[rows, cols] = land[slot, :units, :]
        fc2[rows, cols] = land[slot, units:, :]


def token_rows(device):
    return pl.ds(pl.multiple_of(device * TOK, TOK), TOK)


def chip_rows(chip):
    return pl.ds(pl.multiple_of(chip * PAIR, PAIR), PAIR)


class Gather:
    def __init__(self, group, full, send, recv):
        self.group, self.full, self.send, self.recv = group, full, send, recv
        self.started = []

    def copy(self, number, owner, device, first=0, count=TOK):
        rows = pl.ds(pl.multiple_of(owner * TOK + first, HALF), count)
        part = self.full.at[rows]
        return remote(part, part, self.send, self.recv, number, {"g": device})

    def go(self, *place):
        copy = self.copy(*place)
        copy.start()
        self.started.append(copy)

    def got(self, *place):
        self.copy(*place).wait_recv()

    def start(self):
        group = self.group
        self.go(2, group.me, group.peers[2])
        self.go(1, group.me, group.peers[1])
        self.go(0, group.me, group.sibling)

    def arrive(self, chip):
        group = self.group
        sibling = group.sibling
        if chip == 0:
            self.got(0, sibling, sibling)
        if chip == 1:
            self.got(1, group.peers[1], sibling)
            self.go(3, group.peers[1], group.peers[2], HALF, HALF)
            self.got(2, group.peers[2], sibling)
            self.go(4, group.peers[2], group.peers[1], 0, HALF)
            self.go(5, group.peers[1], sibling)
            self.go(6, group.peers[2], sibling)
            self.got(5, group.others[1], sibling)
        if chip == 2:
            self.got(6, group.others[2], sibling)
        if chip == 3:
            self.got(4, group.peers[3], sibling, 0, HALF)
            self.go(7, group.peers[3], sibling, 0, HALF)
            self.got(3, group.peers[3], sibling, HALF, HALF)
            self.go(8, group.peers[3], sibling, HALF, HALF)
            self.got(7, group.others[3], sibling, 0, HALF)
            self.got(8, group.others[3], sibling, HALF, HALF)

    def finish(self):
        for copy in self.started:
            copy.wait_send()


class Scatter:
    scratch = (
        pltpu.VMEM((4, TOK, 1024), F32),
        pltpu.VMEM((4, TOK, 1024), BF16),
        pltpu.VMEM((4, TOK, 1024), BF16),
        pltpu.VMEM((3, TOK, 1024), BF16),
        pltpu.VMEM((2, HALF, 1024), BF16),
        pltpu.VMEM((2, TOK, 1024), BF16),
        pltpu.SemaphoreType.DMA((10,)),
        pltpu.SemaphoreType.DMA((10,)),
    )

    def __init__(self, group, keep, near_out, near_in, far_out, mid_in, far_in, send, recv):
        self.group, self.keep, self.far_out = group, keep, far_out
        self.near_out, self.near_in, self.mid_in, self.far_in = near_out, near_in, mid_in, far_in
        y, x = ({"g": group.peers[chip]} for chip in (1, 2))
        low, high = pl.ds(0, HALF), pl.ds(HALF, HALF)
        self.copies = [
            *(remote(near_out.at[n], near_in.at[n], send, recv, n, {"g": group.sibling}) for n in range(4)),
            remote(far_out.at[2, low], mid_in.at[0], send, recv, 4, x),
            remote(far_out.at[2, high], mid_in.at[1], send, recv, 5, y),
            remote(far_out.at[0, high], far_in.at[0, high], send, recv, 6, y),
            remote(far_out.at[0, low], far_in.at[0, low], send, recv, 7, y),
            remote(far_out.at[1, low], far_in.at[1, low], send, recv, 8, x),
            remote(far_out.at[1, high], far_in.at[1, high], send, recv, 9, x),
        ]

    def push(self, chip, term):
        self.near_out[chip] = term(self.group.others[chip]).astype(BF16)
        self.copies[chip].start()
        self.keep[chip] = term(self.group.peers[chip])

    def relay(self, chip):
        self.copies[chip].wait_recv()
        total = self.keep[chip] + self.near_in[chip].astype(F32)
        if chip == 0:
            self.keep[0] = total
        if chip == 1:
            self.keep[1] = total
            self.far_out[0, HALF:] = total[HALF:].astype(BF16)
            self.copies[6].start()
        if chip == 2:
            self.keep[2] = total
            self.far_out[1, :HALF] = total[:HALF].astype(BF16)
            self.copies[8].start()
        if chip == 3:
            self.far_out[2] = total.astype(BF16)
            self.copies[4].start()
            self.copies[5].start()

    def across(self):
        self.copies[4].wait_recv()
        self.far_out[0, :HALF] = (self.keep[1, :HALF] + self.mid_in[0].astype(F32)).astype(BF16)
        self.copies[7].start()
        self.copies[5].wait_recv()
        self.far_out[1, HALF:] = (self.keep[2, HALF:] + self.mid_in[1].astype(F32)).astype(BF16)
        self.copies[9].start()

    def result(self):
        for number in (6, 8, 7, 9):
            self.copies[number].wait_recv()
        return self.keep[0] + self.far_in[0].astype(F32) + self.far_in[1].astype(F32)

    def finish(self):
        for copy in self.copies:
            copy.wait_send()


def norm_parts(value):
    average = jnp.mean(value, axis=-1, keepdims=True)
    centered = value - average
    variance = jnp.mean(centered * centered, axis=-1, keepdims=True)
    inverse = lax.rsqrt(variance + 1e-06)
    return centered * inverse, inverse


def norm_back(normal, inverse, grad):
    first = jnp.mean(grad, axis=-1, keepdims=True)
    second = jnp.mean(grad * normal, axis=-1, keepdims=True)
    return (grad - first - normal * second) * inverse


def store_blocks(ref, half, first, value):
    for part in range(8):
        slot = part % 4 * 4 + part // 4 * 2 + half
        ref[slot, first : first + value.shape[0], :] = value[:, part * 128 : part * 128 + 128].astype(ref.dtype)


def column_sum(value):
    return jnp.sum(value, axis=0, keepdims=True)


def attention_forward_stage(
    group, weights, gather, scatter, start,
    hidden, mods, weight, bias, proj, proj_bias,
    middle, branch, full, packed, attended, logsum,
):
    normal, _ = norm_parts(hidden[...])
    full[token_rows(group.me), :] = (normal * (1.0 + mods[1:2]) + mods[0:1]).astype(BF16)
    start()
    gather.start()
    weights.step(0)
    for chip in range(4):
        gather.arrive(chip)
        rows = chip_rows(group.chips[chip])
        packed[rows, :] = (nt(full[rows, :], weight[...]) + bias[...]).astype(BF16)
        if chip == 1:
            weights.step(1)
    weights.step(2)
    order = (3, 2, 1, 0)
    for place, chip in enumerate(order):
        rows = chip_rows(group.chips[chip])
        for head in range(2):
            query = packed[rows, head * 64 : head * 64 + 64] * BF16(HEAD_DIM**-0.5)
            key = packed[:, 128 + head * 64 : 192 + head * 64]
            value = packed[:, 256 + head * 64 : 320 + head * 64]
            scores = nt(key, query)
            top = jnp.max(scores, axis=0, keepdims=True)
            raised = jnp.exp(scores - top)
            total = jnp.sum(raised, axis=0, keepdims=True)
            output = tn(value, raised.astype(BF16)) * (1.0 / total)
            attended[rows, head * 64 : head * 64 + 64] = output.T.astype(BF16)
            logsum[head : head + 1, rows] = top + jnp.log(total)
        scatter.push(chip, lambda device: nn(attended[token_rows(device), :], proj[...]))
        if place:
            scatter.relay(order[place - 1])
        if place == 2:
            weights.step(3)
    scatter.across()
    scatter.relay(0)
    weights.step(4)
    result = scatter.result() + proj_bias[...]
    branch[...] = result
    middle[...] = hidden[...] + mods[2:3] * result
    gather.finish()
    scatter.finish()


def mlp_forward_stage(
    group, weights, gather, scatter,
    middle, mods, weight, bias, weight_two, bias_two,
    output, branch, full, inner, active,
):
    normal, _ = norm_parts(middle[...])
    full[token_rows(group.me), :] = (normal * (1.0 + mods[4:5]) + mods[3:4]).astype(BF16)
    gather.start()
    weights.step(0)
    for chip in range(4):
        gather.arrive(chip)
        rows = chip_rows(group.chips[chip])
        value = nt(full[rows, :], weight[...]) + bias[...]
        inner[rows, :] = value
        bent = jnp.tanh(GELU_COEF * (value + 0.044715 * value * value * value))
        active[rows, :] = (0.5 * value * (1.0 + bent)).astype(BF16)
        scatter.push(chip, lambda device: nn(active[token_rows(device), :], weight_two[...]))
        if chip:
            scatter.relay(chip - 1)
            weights.step(chip)
    scatter.relay(3)
    scatter.across()
    weights.step(4)

    def end():
        result = scatter.result() + bias_two[...]
        branch[...] = result
        output[...] = middle[...] + mods[5:6] * result
        gather.finish()
        scatter.finish()

    return end


def mlp_backward_stage(
    group, owned_sum, gather, scatter, start, start_result,
    grad, mods, middle, branch, branch_one, weight, weight_two, full_two, inner, active,
    grad_middle, grad_attn, sums, weight_grads, bias_grad, full, grad_inner,
):
    if gather:
        full[token_rows(group.me), :] = (mods[5:6] * grad[...]).astype(BF16)
        start()
        gather.start()
    owned_sum.step(0)
    sums[1:2, :] = column_sum(full[token_rows(group.me), :].astype(F32))
    total = jnp.zeros((1, inner.shape[1]), F32)
    for chip in range(4):
        if gather:
            gather.arrive(chip)
        rows = chip_rows(group.chips[chip])
        grad_active = nt(full[rows, :], weight_two[...])
        value = inner[rows, :]
        bent = jnp.tanh(GELU_COEF * (value + 0.044715 * value * value * value))
        slope = GELU_COEF * (1.0 + (3 * 0.044715) * value * value)
        low = (grad_active * (0.5 * (1.0 + bent) + 0.5 * value * (1.0 - bent * bent) * slope)).astype(BF16)
        grad_inner[rows, :] = low
        total = total + column_sum(low.astype(F32))
        scatter.push(chip, lambda device: nn(grad_inner[token_rows(device), :], weight[...]))
        if chip:
            scatter.relay(chip - 1)
            owned_sum.step(chip)
    scatter.relay(3)
    scatter.across()
    bias_grad[...] = total
    units = weight.shape[0] // 2
    for half in range(2):
        cols = slice(half * units, half * units + units)
        store_blocks(weight_grads, half, 0, tn(grad_inner[:, cols], full_two[...]))
        store_blocks(weight_grads, half, units, tn(active[:, cols], full[...]))
    start_result()
    sums[0:1, :] = column_sum(grad[...] * branch[...])
    result = scatter.result()
    normal, inverse = norm_parts(middle[...])
    sums[2:3, :] = column_sum(result)
    sums[3:4, :] = column_sum(result * normal)
    back = grad[...] + norm_back(normal, inverse, (1.0 + mods[4:5]) * result)
    grad_middle[...] = back
    low = (mods[2:3] * back).astype(BF16)
    grad_attn[...] = low
    sums[4:5, :] = column_sum(back * branch_one[...])
    sums[5:6, :] = column_sum(low.astype(F32))
    owned_sum.step(4)
    if gather:
        gather.finish()
    scatter.finish()


def attention_backward_stage(
    group, owned_sum, gather, scatter,
    grad_middle, grad_attn, mods, hidden, weight, proj, full_one, packed, attended, logsum,
    grad_input, sums, weight_grads, bias_grad, full, grad_packed, key_grad, value_grad,
):
    full[token_rows(group.me), :] = grad_attn[...]
    gather.start()
    owned_sum.step(0)
    scale = HEAD_DIM**-0.5
    for chip in range(4):
        gather.arrive(chip)
        rows = chip_rows(group.chips[chip])
        grad_out = nt(full[rows, :], proj[...]).astype(BF16)
        for head in range(2):
            query = packed[rows, head * 64 : head * 64 + 64] * BF16(scale)
            key = packed[:, 128 + head * 64 : 192 + head * 64]
            value = packed[:, 256 + head * 64 : 320 + head * 64]
            part = grad_out[:, head * 64 : head * 64 + 64]
            probs = jnp.exp(nt(key, query) - logsum[head : head + 1, rows])
            grad_probs = nt(value, part)
            delta = jnp.sum(probs * grad_probs, axis=0, keepdims=True)
            grad_scores = (probs * (grad_probs - delta)).astype(BF16)
            grad_packed[rows, head * 64 : head * 64 + 64] = (tn(grad_scores, key) * scale).astype(BF16)
            key_term = nn(grad_scores, query)
            value_term = nn(probs.astype(BF16), part)
            if chip == 0:
                key_grad[head] = key_term
                value_grad[head] = value_term
            else:
                key_grad[head] += key_term
                value_grad[head] += value_term
        if chip in (1, 3):
            owned_sum.step(1 + chip // 2)
    for head in range(2):
        grad_packed[:, 128 + head * 64 : 192 + head * 64] = key_grad[head].astype(BF16)
        grad_packed[:, 256 + head * 64 : 320 + head * 64] = value_grad[head].astype(BF16)
    order = (3, 2, 1, 0)
    for place, chip in enumerate(order):
        scatter.push(chip, lambda device: nn(grad_packed[token_rows(device), :], weight[...]))
        if place:
            scatter.relay(order[place - 1])
    scatter.across()
    scatter.relay(0)
    owned_sum.step(3)
    for part in range(3):
        term = tn(grad_packed[:, part * 128 : part * 128 + 128], full_one[...])
        for half in range(2):
            store_blocks(weight_grads, half, part * 64, term[half * 64 : half * 64 + 64])
    term = tn(attended[...], full[...])
    for half in range(2):
        store_blocks(weight_grads, half, 192, term[half * 64 : half * 64 + 64])
    bias_grad[...] = column_sum(grad_packed[...].astype(F32))
    result = scatter.result()
    normal, inverse = norm_parts(hidden[...])
    sums[6:7, :] = column_sum(result)
    sums[7:8, :] = column_sum(result * normal)
    grad_input[...] = grad_middle[...] + norm_back(normal, inverse, (1.0 + mods[1:2]) * result)
    owned_sum.step(4)
    gather.finish()
    scatter.finish()


class Nothing:
    def step(self, step):
        pass


def forward_kernel(more, *refs):
    hidden, mods, weight, bias, proj, proj_bias, inner_bias, bias_two, mlp_rows, *refs = refs
    if more:
        next_rows, *refs = refs
    middle, branch, full, packed, attended, logsum, fc1, fc2, output, branch_two, full_two, inner, active, *refs = refs
    if more:
        next_qkv, next_proj, *refs = refs
    land, own_send, own_recv, *refs = refs
    if more:
        next_land, next_send, next_recv, *refs = refs
    send, recv, *scatter_refs = refs
    group, owners = Group(), Owners()
    partners = group.near + owners.near
    greet(partners)
    weights = OwnersGather(owners, land, own_send, own_recv)
    land[owners.slot] = mlp_rows[...]
    scatter = Scatter(group, *scatter_refs)
    attention_forward_stage(
        group, weights, Gather(group, full, send, recv), scatter, lambda: met(partners),
        hidden, mods, weight, bias, proj, proj_bias, middle, branch, full, packed, attended, logsum,
    )
    place_mlp(land, fc1, fc2)
    weights = Nothing()
    if more:
        weights = OwnersGather(owners, next_land, next_send, next_recv)
        next_land[owners.slot] = next_rows[...]
    mlp_forward_stage(
        group, weights, Gather(group, full_two, send, recv), scatter,
        middle, mods, fc1, inner_bias, fc2, bias_two, output, branch_two, full_two, inner, active,
    )()
    if more:
        place_attention(next_land, next_qkv, next_proj)


def backward_kernel(more, *refs):
    grad, mods, middle, branch_two, branch, fc1, fc2, full_two, inner, active, *refs = refs
    hidden, qkv, proj, full_one, packed, attended, logsum, *refs = refs
    if more:
        parts, *refs = refs
    grad_input, sums, attn_parts, qkv_sum, fc1_sum, mlp_owned, *refs = refs
    if more:
        attn_owned, *refs = refs
    grad_middle, grad_attn, mlp_parts, full, full_attn, grad_inner, grad_packed, key_grad, value_grad, *refs = refs
    mlp_refs, refs = refs[:10], refs[10:]
    if more:
        attn_refs, refs = refs[:10], refs[10:]
    send, recv, *scatter_refs = refs
    group, owners = Group(), Owners()
    partners = group.near + owners.near
    greet(partners)
    scatter = Scatter(group, *scatter_refs)
    owned = OwnersScatter(owners, parts, attn_owned, *attn_refs) if more else Nothing()
    mlp_backward_stage(
        group, owned, Gather(group, full, send, recv), scatter, lambda: met(partners), lambda: None,
        grad, mods, middle, branch_two, branch, fc1, fc2, full_two, inner, active,
        grad_middle, grad_attn, sums, mlp_parts, fc1_sum, full, grad_inner,
    )
    owned = OwnersScatter(owners, mlp_parts, mlp_owned, *mlp_refs)
    attention_backward_stage(
        group, owned, Gather(group, full_attn, send, recv), scatter,
        grad_middle, grad_attn, mods, hidden, qkv, proj, full_one, packed, attended, logsum,
        grad_input, sums, attn_parts, qkv_sum, full_attn, grad_packed, key_grad, value_grad,
    )


class Beside:
    def __init__(self, weights, gather):
        self.weights, self.gather = weights, gather

    def step(self, step):
        self.weights.step(step)
        if step == 2:
            self.gather.start()
            self.gather.arrive(0)
        if step == 3:
            self.gather.arrive(1)
            self.gather.arrive(2)
        if step == 4:
            self.gather.arrive(3)
            self.gather.finish()


def turn_kernel(
    hidden, mods, qkv, qkv_bias, proj, proj_bias, inner_bias, bias_two, mlp_rows, grad,
    output, grad_input, sums, attn_parts, qkv_sum, fc1_sum, mlp_owned,
    middle, branch, branch_two, full, packed, attended, logsum, fc1, fc2, full_two, inner, active,
    land, own_send, own_recv,
    grad_middle, grad_attn, mlp_parts, full_grad, full_attn, grad_inner, grad_packed, key_grad, value_grad, *refs,
):
    mlp_refs, refs = refs[:10], refs[10:]
    back_refs, refs = refs[:8], refs[8:]
    grad_send, grad_recv, send, recv, *scatter_refs = refs
    group, owners = Group(), Owners()
    partners = group.near + owners.near
    greet(partners)
    weights = OwnersGather(owners, land, own_send, own_recv)
    land[owners.slot] = mlp_rows[...]
    full_grad[token_rows(group.me), :] = (mods[5:6] * grad[...]).astype(BF16)
    beside = Beside(weights, Gather(group, full_grad, grad_send, grad_recv))
    scatter, back = Scatter(group, *scatter_refs), Scatter(group, *back_refs)
    attention_forward_stage(
        group, beside, Gather(group, full, send, recv), scatter, lambda: met(partners),
        hidden, mods, qkv, qkv_bias, proj, proj_bias, middle, branch, full, packed, attended, logsum,
    )
    place_mlp(land, fc1, fc2)
    end = mlp_forward_stage(
        group, Nothing(), Gather(group, full_two, send, recv), scatter,
        middle, mods, fc1, inner_bias, fc2, bias_two, output, branch_two, full_two, inner, active,
    )
    mlp_backward_stage(
        group, Nothing(), None, back, None, end,
        grad, mods, middle, branch_two, branch, fc1, fc2, full_two, inner, active,
        grad_middle, grad_attn, sums, mlp_parts, fc1_sum, full_grad, grad_inner,
    )
    owned = OwnersScatter(owners, mlp_parts, mlp_owned, *mlp_refs)
    attention_backward_stage(
        group, owned, Gather(group, full_attn, send, recv), back,
        grad_middle, grad_attn, mods, hidden, qkv, proj, full, packed, attended, logsum,
        grad_input, sums, attn_parts, qkv_sum, full_attn, grad_packed, key_grad, value_grad,
    )


def first_kernel(
    rows, terms, bias, qkv, proj, halves, mods,
    land, own_send, own_recv, x_in, y_out, y_in, z_out, z_in, send, recv, all_send, all_recv,
):
    group, owners = Group(), Owners()
    partners = owners.near + (owners.to_across,) + tuple({"g": device} for device in group.everyone)
    greet(partners)
    weights = OwnersGather(owners, land, own_send, own_recv)
    land[owners.slot] = rows[...]
    halves[owners.x] = bias[...]
    met(partners)
    other = 1 - owners.x
    along_x = remote(terms.at[pl.ds(other * 8, 8)], x_in, send, recv, 0, owners.to_x)
    along_x.start()
    bias_there = remote(bias, halves.at[owners.x], send, recv, 1, owners.to_x)
    bias_there.start()
    weights.step(0)
    along_x.wait_recv()
    y_out[owners.x] = terms[pl.ds(owners.x * 8 + (1 - owners.y) * 4, 4)]
    y_out[other] = x_in[pl.ds((1 - owners.y) * 4, 4)]
    along_y = remote(y_out, y_in, send, recv, 2, owners.to_y)
    along_y.start()
    weights.step(1)
    along_y.wait_recv()
    own = terms[pl.ds(owners.x * 8 + owners.y * 4, 4)] + y_in[owners.x]
    far = x_in[pl.ds(owners.y * 4, 4)] + y_in[other]
    for z in range(4):
        z_out[z, owners.x] = own[z]
        z_out[z, other] = far[z]
    along_z = [
        remote(z_out.at[z], z_in.at[number], send, recv, 3 + number, device)
        for number, (z, device) in enumerate(
            ((owners.up, owners.to_up), (owners.across, owners.to_across), (owners.down, owners.to_down))
        )
    ]
    for copy in along_z:
        copy.start()
    weights.step(2)
    total = z_out[owners.z]
    for number, copy in enumerate(along_z):
        copy.wait_recv()
        total = total + z_in[number]
    mods[group.me] = total
    around = [
        remote(mods.at[group.me], mods.at[group.me], all_send, all_recv, number, {"g": device})
        for number, device in enumerate(group.everyone)
    ]
    for copy in around:
        copy.start()
    weights.step(3)
    for number, device in enumerate(group.everyone):
        remote(mods.at[device], mods.at[device], all_send, all_recv, number, {"g": device}).wait_recv()
    remote(bias, halves.at[other], send, recv, 1, owners.to_x).wait_recv()
    weights.step(4)
    place_attention(land, qkv, proj)
    for copy in (along_x, bias_there, along_y, *along_z, *around):
        copy.wait_send()


def last_kernel(
    parts, blocks, own, ada, owned, every, summed, copies, act_grad,
    *refs,
):
    group, owners = Group(), Owners()
    partners = owners.near + tuple({"g": device} for device in group.everyone)
    greet(partners)
    owned_sum = OwnersScatter(owners, parts, owned, *refs[:10])
    own_send, own_recv, inbox, send, recv, all_send, all_recv, *refs = refs[10:]
    act_all, act_out, act_in, act_send, act_recv, x_send, x_recv = refs
    gather = OwnersGather(owners, every, own_send, own_recv)
    met(partners)
    around = [
        remote(blocks.at[device], inbox.at[number], send, recv, number, {"g": device})
        for number, device in enumerate(group.everyone)
    ]
    for copy in around:
        copy.start()
    owned_sum.step(0)
    total = blocks[group.me]
    for number, copy in enumerate(around):
        copy.wait_recv()
        total = total + inbox[number]
    rows = blocks.shape[1]
    every[owners.slot, 0:rows] = total
    every[owners.slot, rows:] = own[...]
    gather.step(0)
    gather.step(1)
    owned_sum.step(1)
    gather.step(2)
    gather.step(3)
    owned_sum.step(2)
    gather.step(4)
    act = jnp.zeros(act_out.shape, F32)
    lines = ada.shape[2] // 128
    for layer in range(ada.shape[0]):
        for line in range(lines):
            place = layer * lines + line
            left = jnp.where(owners.x == 0, every[:, place, :], every[:, ada.shape[0] * lines + place, :])
            right = ada[layer, :, line * 128 : line * 128 + 128].astype(F32)
            act = act + lax.dot_general(
                left, right, (((1,), (1,)), ((), ())), precision=lax.Precision.HIGHEST, preferred_element_type=F32
            )
    act_all[group.me] = act
    acts = [
        remote(act_all.at[group.me], act_all.at[group.me], act_send, act_recv, number, {"g": device})
        for number, device in enumerate(group.everyone)
    ]
    for copy in acts:
        copy.start()
    total = every[0]
    for slot in range(1, 16):
        total = total + every[slot]
    summed[...] = total
    copies[group.me] = total[0:rows]
    spread = [
        remote(copies.at[group.me], copies.at[group.me], all_send, all_recv, number, {"g": device})
        for number, device in enumerate(group.everyone)
    ]
    for copy in spread:
        copy.start()
    for number, device in enumerate(group.everyone):
        remote(act_all.at[device], act_all.at[device], act_send, act_recv, number, {"g": device}).wait_recv()
    act = act_all[0]
    for device in range(1, 8):
        act = act + act_all[device]
    act_out[...] = act
    over = remote(act_out, act_in, x_send, x_recv, 0, owners.to_x)
    over.start()
    owned_sum.step(3)
    for number, device in enumerate(group.everyone):
        remote(copies.at[device], copies.at[device], all_send, all_recv, number, {"g": device}).wait_recv()
    over.wait_recv()
    act_grad[...] = act_out[...] + act_in[...]
    owned_sum.step(4)
    for copy in (*around, *spread, *acts, over):
        copy.wait_send()


def plain_call(kernel, number, outs, scratch, *operands):
    space = pl.BlockSpec(memory_space=pltpu.VMEM)
    return pl.pallas_call(
        kernel,
        out_shape=[jax.ShapeDtypeStruct(shape, kind) for shape, kind in outs],
        in_specs=[space] * len(operands),
        out_specs=[space] * len(outs),
        scratch_shapes=scratch,
        compiler_params=pltpu.CompilerParams(
            collective_id=number, has_side_effects=True, vmem_limit_bytes=VMEM_LIMIT
        ),
        cost_estimate=pl.CostEstimate(flops=10**10, bytes_accessed=8 << 20, transcendentals=1 << 20),
    )(*operands)


def call(kernel, number, outs, scratch, *operands):
    pair = [pltpu.SemaphoreType.DMA((9,)), pltpu.SemaphoreType.DMA((9,))]
    return plain_call(kernel, number, outs, [*scratch, *pair, *Scatter.scratch], *operands)


def first(rows, terms, bias):
    width = 1024
    outs = [
        ((384, width), BF16), ((128, width), BF16), ((2, *bias.shape), F32), ((8, 2, 8, 128), F32),
    ]
    scratch = [
        pltpu.VMEM((16, *rows.shape), BF16), *OwnersGather.scratch,
        pltpu.VMEM((8, 8, 128), F32), pltpu.VMEM((2, 4, 8, 128), F32), pltpu.VMEM((2, 4, 8, 128), F32),
        pltpu.VMEM((4, 2, 8, 128), F32), pltpu.VMEM((3, 2, 8, 128), F32),
        pltpu.SemaphoreType.DMA((6,)), pltpu.SemaphoreType.DMA((6,)),
        pltpu.SemaphoreType.DMA((7,)), pltpu.SemaphoreType.DMA((7,)),
    ]
    return plain_call(first_kernel, 10, outs, scratch, rows, terms, bias)


def last(parts, blocks, own, ada):
    rows = blocks.shape[1]
    outs = [
        (parts.shape[1:], F32), ((16, rows + own.shape[0], 128), F32), ((rows + own.shape[0], 128), F32),
        (blocks.shape, F32), ((16, 128), F32),
    ]
    scratch = [
        *OwnersScatter.scratch(parts.shape[1]), *OwnersGather.scratch, pltpu.VMEM((7, rows, 128), F32),
        *([pltpu.SemaphoreType.DMA((7,))] * 4),
        pltpu.VMEM((8, 16, 128), F32), pltpu.VMEM((16, 128), F32), pltpu.VMEM((16, 128), F32),
        *([pltpu.SemaphoreType.DMA((7,))] * 2), *([pltpu.SemaphoreType.DMA((1,))] * 2),
    ]
    return plain_call(last_kernel, 11, outs, scratch, parts, blocks, own, ada)


def forward(operands, rows=None):
    hidden, weight, proj, mlp_rows = operands[0], operands[2], operands[4], operands[8]
    width, units = hidden.shape[1], mlp_rows.shape[0]
    token, whole = ((TOK, width), F32), ((SEQ_LEN, width), BF16)
    outs = [
        token, token, whole, ((SEQ_LEN, weight.shape[0]), BF16), ((SEQ_LEN, proj.shape[0]), BF16), ((2, SEQ_LEN), F32),
        ((units, width), BF16), ((units, width), BF16),
        token, token, whole, ((SEQ_LEN, units), F32), ((SEQ_LEN, units), BF16),
    ]
    scratch = [pltpu.VMEM((16, *mlp_rows.shape), BF16), *OwnersGather.scratch]
    if rows is None:
        return call(functools.partial(forward_kernel, False), 0, outs, scratch, *operands)
    outs += [(weight.shape, BF16), (proj.shape, BF16)]
    scratch += [pltpu.VMEM((16, *rows.shape), BF16), *OwnersGather.scratch]
    return call(functools.partial(forward_kernel, True), 1, outs, scratch, *operands, rows)


def backward(operands, parts=None):
    grad, fc1, qkv = operands[0], operands[5], operands[11]
    width, units = grad.shape[1], fc1.shape[0]
    outs = [
        ((TOK, width), F32), ((8, width), F32), ((16, 256, 128), BF16),
        ((1, qkv.shape[0]), F32), ((1, units), F32), ((units, 128), F32),
    ]
    if parts is not None:
        outs += [(parts.shape[1:], F32)]
    scratch = [
        pltpu.VMEM((TOK, width), F32),
        pltpu.VMEM((TOK, width), BF16),
        pltpu.VMEM((16, units, 128), BF16),
        pltpu.VMEM((SEQ_LEN, width), BF16),
        pltpu.VMEM((SEQ_LEN, width), BF16),
        pltpu.VMEM((SEQ_LEN, units), BF16),
        pltpu.VMEM((SEQ_LEN, qkv.shape[0]), BF16),
        pltpu.VMEM((2, SEQ_LEN, HEAD_DIM), F32),
        pltpu.VMEM((2, SEQ_LEN, HEAD_DIM), F32),
        *OwnersScatter.scratch(units),
    ]
    if parts is None:
        return call(functools.partial(backward_kernel, False), 2, outs, scratch, *operands)
    scratch += OwnersScatter.scratch(parts.shape[1])
    return call(functools.partial(backward_kernel, True), 3, outs, scratch, *operands, parts)


def turn(*operands):
    hidden, qkv, proj, mlp_rows = operands[0], operands[2], operands[4], operands[8]
    width, units, cols = hidden.shape[1], mlp_rows.shape[0], qkv.shape[0]
    outs = [
        ((TOK, width), F32), ((TOK, width), F32), ((8, width), F32), ((16, 256, 128), BF16),
        ((1, cols), F32), ((1, units), F32), ((units, 128), F32),
    ]
    token, whole = pltpu.VMEM((TOK, width), F32), pltpu.VMEM((SEQ_LEN, width), BF16)
    head = pltpu.VMEM((2, SEQ_LEN, HEAD_DIM), F32)
    scratch = [
        token, token, token, whole, pltpu.VMEM((SEQ_LEN, cols), BF16), pltpu.VMEM((SEQ_LEN, proj.shape[0]), BF16),
        pltpu.VMEM((2, SEQ_LEN), F32), pltpu.VMEM((units, width), BF16), pltpu.VMEM((units, width), BF16),
        whole, pltpu.VMEM((SEQ_LEN, units), F32), pltpu.VMEM((SEQ_LEN, units), BF16),
        pltpu.VMEM((16, units, 128), BF16), *OwnersGather.scratch,
        token, pltpu.VMEM((TOK, width), BF16), pltpu.VMEM((16, units, 128), BF16), whole, whole,
        pltpu.VMEM((SEQ_LEN, units), BF16), pltpu.VMEM((SEQ_LEN, cols), BF16), head, head,
        *OwnersScatter.scratch(units), *Scatter.scratch,
        pltpu.SemaphoreType.DMA((9,)), pltpu.SemaphoreType.DMA((9,)),
    ]
    return call(turn_kernel, 4, outs, scratch, *operands)


RX = ("row", "xh")
ALL = ("row", "xh", "g")


def highest(left, right):
    return jnp.dot(left, right, precision=lax.Precision.HIGHEST, preferred_element_type=F32)


def highest_tn(left, right):
    return lax.dot_general(
        left, right, (((0,), (0,)), ((), ())), precision=lax.Precision.HIGHEST, preferred_element_type=F32
    )


def highest_nt(left, right):
    return lax.dot_general(
        left, right, (((1,), (1,)), ((), ())), precision=lax.Precision.HIGHEST, preferred_element_type=F32
    )


def small_sums(sums, qkv_sum, fc1_sum):
    mod_grad = jnp.concatenate([sums[6:8], sums[4:5], sums[2:4], sums[0:1]])
    return mod_grad, sums[5], sums[1], qkv_sum, fc1_sum


def on_device(
    tokens, cotangent, timestep, class_label, class_table, ada_weight, ada_bias, qkv_weight, qv_bias,
    proj_weight, proj_bias, fc1_weight, fc1_bias, fc2_weight, fc2_bias,
):
    row_index, half_index, _ = (lax.axis_index(axis) for axis in ALL)
    width = tokens.shape[1]
    width_part = class_table.shape[1]
    latent_count = timestep.shape[0]
    layer_count, _, ada_cols = ada_weight.shape
    units = fc1_weight.shape[2]
    attn_rows = [jnp.concatenate([qkv_weight[l].T, proj_weight[l]]) for l in range(layer_count)]
    mlp_rows = [jnp.concatenate([fc1_weight[l].T, fc2_weight[l]]) for l in range(layer_count)]
    column_ids = row_index * width_part + lax.iota(jnp.int32, width_part)
    half_width = width // 2
    frequency = jnp.exp(-LOG_BASE * (column_ids % half_width).astype(F32) / half_width)
    angles = timestep.astype(F32)[:, None] * frequency[None, :]
    waves = jnp.where(column_ids[None, :] < half_width, jnp.cos(angles), jnp.sin(angles))
    class_hot = (class_label[:, None] == lax.iota(jnp.int32, class_table.shape[0])[None, :]).astype(F32)
    condition = waves + highest(class_hot, class_table.astype(F32))
    cond_act = condition * jax.nn.sigmoid(condition)
    ada_float = ada_weight.astype(F32)
    terms = jnp.stack([highest(cond_act, ada_float[l]) for l in range(layer_count)], axis=1)
    terms = terms.reshape(latent_count // 2, 2, -1, 128).swapaxes(0, 1).reshape(latent_count, -1, 128)
    lines = layer_count * ada_cols // 128
    terms = jnp.pad(terms, ((0, 0), (0, 8 - lines), (0, 0)))
    bias_rows = jnp.concatenate([qv_bias.reshape(layer_count, -1), fc1_bias], axis=1).reshape(-1, 128)
    bias_count = bias_rows.shape[0]
    bias_rows = jnp.pad(bias_rows, ((0, 8 - bias_count), (0, 0)))
    qkv, proj, halves, mod_parts = first(attn_rows[0], terms, bias_rows)
    modulation = mod_parts[:, :, :lines].reshape(8, 2, layer_count, ada_cols).transpose(2, 1, 0, 3)
    modulation = modulation.reshape(layer_count, 6 * width) + ada_bias
    mods = jnp.pad(modulation.reshape(layer_count, 6, width), ((0, 0), (0, 2), (0, 0)))
    halves = halves[:, :bias_count].reshape(2, layer_count, -1)

    saved = []
    hidden = tokens
    small = [None] * layer_count
    attn_grads, mlp_grads = [None] * layer_count, [None] * layer_count
    for number in range(layer_count):
        query = halves[:, number, :HEAD_DIM].reshape(1, -1)
        value = halves[:, number, HEAD_DIM : 2 * HEAD_DIM].reshape(1, -1)
        qkv_bias = jnp.concatenate([query, jnp.zeros_like(query), value], axis=1)
        inner_bias = halves[:, number, 2 * HEAD_DIM :].reshape(1, -1)
        operands = (
            hidden, mods[number], qkv, qkv_bias, proj, proj_bias[number : number + 1], inner_bias,
            fc2_bias[number : number + 1], mlp_rows[number],
        )
        if number + 1 < layer_count:
            (
                middle, branch, full, packed, attended, logsum, fc1, fc2, output, branch_two, full_two, inner, active, *later
            ) = forward(operands, attn_rows[number + 1])
            saved.append(
                (middle, branch_two, branch, fc1, fc2, full_two, inner, active, hidden, qkv, proj, full, packed, attended, logsum)
            )
            hidden = output
            qkv, proj = later
        else:
            mixed, grad, sums, attn_parts, qkv_sum, fc1_sum, mlp_grads[number] = turn(*operands, cotangent)
            small[number] = small_sums(sums, qkv_sum, fc1_sum)
    for number in reversed(range(layer_count - 1)):
        grad, sums, attn_parts, qkv_sum, fc1_sum, mlp_grads[number], attn_grads[number + 1] = backward(
            (grad, mods[number], *saved[number]), attn_parts
        )
        small[number] = small_sums(sums, qkv_sum, fc1_sum)
    tokens_grad = grad

    mod_grad, proj_sum, fc2_sum, qkv_sum, fc1_sum = (jnp.stack(parts) for parts in zip(*small))
    mod_send = mod_grad.reshape(layer_count, 2, 8, ada_cols).transpose(2, 1, 0, 3).reshape(8, -1)
    bias_send = jnp.concatenate([proj_sum, fc2_sum]).reshape(2 * layer_count, 8, -1).swapaxes(0, 1).reshape(8, -1)
    mod_size = mod_send.shape[1]
    send = jnp.concatenate([mod_send, bias_send], axis=1).reshape(8, -1, 128)
    qv_sum = qkv_sum.reshape(layer_count, 3, 2, HEAD_DIM)[:, ::2].transpose(2, 0, 1, 3).reshape(2, -1)
    fc1_half = fc1_sum.reshape(layer_count, 2, units).swapaxes(0, 1).reshape(2, -1)
    own = jnp.concatenate([qv_sum, fc1_half], axis=1).reshape(-1, 128)
    own_count = own.shape[0]
    own = jnp.pad(own, ((0, 16 - own_count), (0, 0)))
    attn_grads[0], every, summed, copies, act_grad = last(attn_parts, send, own, ada_weight)
    every = every[:, : mod_size // 128].reshape(4, 2, 2, 2, layer_count, ada_cols)
    mod_cols = lax.dynamic_index_in_dim(every, half_index, axis=3, keepdims=False)
    mod_cols = mod_cols.transpose(1, 0, 2, 3, 4).reshape(latent_count, layer_count, ada_cols)
    copies = copies.reshape(8, -1)
    ada_bias_grad = copies[:, :mod_size].reshape(8, 2, layer_count, ada_cols).transpose(2, 1, 0, 3)
    ada_bias_grad = ada_bias_grad.reshape(layer_count, 6 * width)
    bias_total = copies[:, mod_size:].reshape(8, 2 * layer_count, -1).swapaxes(0, 1).reshape(2, layer_count, width)
    own_total = summed[send.shape[1] :][:own_count].reshape(2, -1)
    own_total = lax.dynamic_index_in_dim(own_total, half_index, keepdims=False)
    qv_bias_grad = own_total[: layer_count * 2 * HEAD_DIM].reshape(layer_count, 2, HEAD_DIM)
    fc1_bias_grad = own_total[layer_count * 2 * HEAD_DIM :].reshape(layer_count, units)
    ada_weight_grad = jnp.stack([highest_tn(cond_act, mod_cols[:, l]) for l in range(layer_count)])
    act_grad = act_grad.reshape(4, 2, 2, width_part).swapaxes(0, 1).reshape(latent_count, width_part)
    gate = jax.nn.sigmoid(condition)
    cond_grad = act_grad * (gate * (1.0 + condition * (1.0 - gate)))
    table_grad = highest_tn(class_hot, cond_grad)
    attn_grads, mlp_grads = jnp.stack(attn_grads), jnp.stack(mlp_grads)
    return (
        mixed,
        tokens_grad,
        cond_grad,
        table_grad,
        ada_weight_grad,
        ada_bias_grad,
        attn_grads[:, :192].swapaxes(1, 2),
        qv_bias_grad,
        attn_grads[:, 192:],
        bias_total[0],
        mlp_grads[:, :units].swapaxes(1, 2),
        fc1_bias_grad,
        mlp_grads[:, units:],
        bias_total[1],
    )


def solution(mesh):
    split = Mesh(mesh.devices.reshape(mesh.shape["row"], 2, 8), ALL)
    col = ("xh", "g")
    in_specs = (
        P(ALL, None), P(ALL, None), P(), P(), P(None, "row"), P(None, "row", col), P(),
        P(None, "row", col), P(None, None, col), P(None, col, "row"), P(), P(None, "row", col),
        P(None, col), P(None, col, "row"), P(),
    )
    out_specs = (
        P(ALL, None), P(ALL, None), P(None, "row"), P(None, "row"), P(None, "row", col), P(),
        P(None, "row", col), P(None, None, col), P(None, col, "row"), P(), P(None, "row", col),
        P(None, col), P(None, col, "row"), P(),
    )
    return jax.shard_map(on_device, mesh=split, in_specs=in_specs, out_specs=out_specs, check_vma=False)
```

```python
import functools
import math

import jax
import jax.numpy as jnp
from jax import lax
from jax.experimental import pallas as pl
from jax.experimental.pallas import tpu as pltpu
from jax.sharding import Mesh
from jax.sharding import PartitionSpec as P

MESH = pl.DeviceIdType.MESH
HEAD_DIM = 64
SEQ_LEN = 1024
GELU_COEF = math.sqrt(2.0 / math.pi)
LOG_BASE = math.log(10000.0)
F32 = jnp.float32
BF16 = jnp.bfloat16
TOK = 128
PAIR = 2 * TOK
HALF = TOK // 2
VMEM_LIMIT = 60 * 1024 * 1024


def nn(left, right):
    return lax.dot_general(left, right, (((1,), (0,)), ((), ())), preferred_element_type=F32)


def nt(left, right):
    return lax.dot_general(left, right, (((1,), (1,)), ((), ())), preferred_element_type=F32)


def tn(left, right):
    return lax.dot_general(left, right, (((0,), (0,)), ((), ())), preferred_element_type=F32)


class Group:
    def __init__(self):
        me = lax.axis_index("g")
        self.me = me
        self.core = lax.rem(me, 2)
        chip = lax.div(me, 2)
        x, y = lax.div(chip, 2), lax.rem(chip, 2)
        self.chips = (chip, 2 * x + 1 - y, 2 * (1 - x) + y, 2 * (1 - x) + 1 - y)
        self.peers = tuple(2 * c + self.core for c in self.chips)
        self.others = tuple(2 * c + 1 - self.core for c in self.chips)
        self.sibling = self.others[0]

        self.near = tuple({"g": device} for device in (self.sibling, *self.peers[1:3]))
        self.everyone = self.peers[1:] + self.others


class Owners:
    def __init__(self):
        row, self.x = lax.axis_index("row"), lax.axis_index("xh")
        self.y, self.z = lax.div(row, 4), lax.rem(row, 4)
        self.up, self.across, self.down = (lax.rem(self.z + by, 4) for by in (1, 2, 3))
        self.slot = self.z * 4 + self.y * 2 + self.x
        self.to_x, self.to_y = {"xh": 1 - self.x}, {"row": (1 - self.y) * 4 + self.z}
        self.to_up, self.to_down = {"row": self.y * 4 + self.up}, {"row": self.y * 4 + self.down}
        self.to_across = {"row": self.y * 4 + self.across}
        self.near = (self.to_x, self.to_y, self.to_up, self.to_down)


def greet(devices):
    for device in devices:
        pl.semaphore_signal(pltpu.get_barrier_semaphore(), inc=1, device_id=device, device_id_type=MESH)


def met(devices):
    pl.semaphore_wait(pltpu.get_barrier_semaphore(), len(devices))


def remote(src, dst, send, recv, number, device):
    return pltpu.make_async_remote_copy(
        src_ref=src, dst_ref=dst, send_sem=send.at[number], recv_sem=recv.at[number],
        device_id=device, device_id_type=MESH,
    )


class OwnersGather:
    scratch = (pltpu.SemaphoreType.DMA((6,)), pltpu.SemaphoreType.DMA((6,)))

    def __init__(self, owners, ref, send, recv):
        self.owners, self.ref, self.send, self.recv = owners, ref, send, recv

    def copy(self, number, first, count, device):
        part = self.ref.at[pl.ds(first, count)]
        return remote(part, part, self.send, self.recv, number, device)

    def step(self, step):
        o = self.owners
        pair, four, up, across, down = o.z * 4 + o.y * 2, o.z * 4, o.up * 4, o.across * 4, o.down * 4
        if step == 0:
            self.copy(0, o.slot, 1, o.to_x).start()
        if step == 1:
            self.copy(0, pair + 1 - o.x, 1, o.to_x).wait_recv()
            self.copy(1, pair, 2, o.to_y).start()
        if step == 2:
            self.copy(1, four + (1 - o.y) * 2, 2, o.to_y).wait_recv()
            self.copy(2, four, 4, o.to_up).start()
            self.copy(3, four, 4, o.to_down).start()
        if step == 3:
            self.copy(2, down, 4, o.to_up).wait_recv()
            self.copy(4, down, 2, o.to_up).start()
            self.copy(3, up, 4, o.to_down).wait_recv()
            self.copy(5, up + 2, 2, o.to_down).start()
        if step == 4:
            self.copy(4, across, 2, o.to_up).wait_recv()
            self.copy(5, across + 2, 2, o.to_down).wait_recv()
            self.copy(0, o.slot, 1, o.to_x).wait_send()
            self.copy(1, pair, 2, o.to_y).wait_send()
            self.copy(2, four, 4, o.to_up).wait_send()
            self.copy(3, four, 4, o.to_down).wait_send()
            self.copy(4, down, 2, o.to_up).wait_send()
            self.copy(5, up + 2, 2, o.to_down).wait_send()


class OwnersScatter:
    @staticmethod
    def scratch(rows):
        shapes = ((2, 2), (2, 4), (2, 4), (2,), (2,), (1,), (1,))
        return (
            *(pltpu.VMEM((*shape, rows, 128), BF16) for shape in shapes),
            pltpu.VMEM((4, rows, 128), F32),
            pltpu.SemaphoreType.DMA((6,)),
            pltpu.SemaphoreType.DMA((6,)),
        )

    def __init__(self, owners, parts, out, in0, out1, in1, out2, in2, out3, in3, total, send, recv):
        self.owners, self.parts, self.out, self.total = owners, parts, out, total
        self.out1, self.in0, self.in1 = out1, in0, in1
        self.out2, self.in2, self.out3, self.in3 = out2, in2, out3, in3
        across = owners.across * 4
        self.copies = [
            remote(parts.at[pl.ds(across, 2)], in0.at[0], send, recv, 0, owners.to_up),
            remote(parts.at[pl.ds(across + 2, 2)], in0.at[1], send, recv, 1, owners.to_down),
            remote(out1.at[0], in1.at[0], send, recv, 2, owners.to_up),
            remote(out1.at[1], in1.at[1], send, recv, 3, owners.to_down),
            remote(out2, in2, send, recv, 4, owners.to_y),
            remote(out3, in3, send, recv, 5, owners.to_x),
        ]

    def step(self, step):
        o, copies, parts, total = self.owners, self.copies, self.parts, self.total
        up, down = o.up * 4, o.down * 4
        if step == 0:
            copies[0].start()
            copies[1].start()
        if step == 1:
            copies[0].wait_recv()
            self.out1[0, 0:2] = (parts[pl.ds(up, 2)].astype(F32) + self.in0[0].astype(F32)).astype(BF16)
            self.out1[0, 2:4] = parts[pl.ds(up + 2, 2)]
            copies[2].start()
            copies[1].wait_recv()
            self.out1[1, 0:2] = parts[pl.ds(down, 2)]
            self.out1[1, 2:4] = (parts[pl.ds(down + 2, 2)].astype(F32) + self.in0[1].astype(F32)).astype(BF16)
            copies[3].start()
        if step == 2:
            copies[2].wait_recv()
            copies[3].wait_recv()
            for block in range(4):
                total[block] = (
                    parts[o.z * 4 + block].astype(F32)
                    + self.in1[0, block].astype(F32)
                    + self.in1[1, block].astype(F32)
                )
            self.out2[...] = total[pl.ds((1 - o.y) * 2, 2)].astype(BF16)
            copies[4].start()
        if step == 3:
            copies[4].wait_recv()
            total[0:2] = total[pl.ds(o.y * 2, 2)] + self.in2[...].astype(F32)
            self.out3[...] = total[pl.ds(1 - o.x, 1)].astype(BF16)
            copies[5].start()
        if step == 4:
            copies[5].wait_recv()
            self.out[...] = total[o.x] + self.in3[0].astype(F32)
            for copy in copies:
                copy.wait_send()


def owner_place(slot):
    z, y, half = slot // 4, slot // 2 % 2, slot % 2
    return y * 4 + z, half


def place_attention(land, qkv, proj):
    for slot in range(16):
        part, half = owner_place(slot)
        cols = slice(part * 128, part * 128 + 128)
        for kind in range(3):
            first = kind * 128 + half * 64
            qkv[first : first + 64, cols] = land[slot, kind * 64 : kind * 64 + 64, :]
        proj[half * 64 : half * 64 + 64, cols] = land[slot, 192:256, :]


def place_mlp(land, fc1, fc2):
    units = land.shape[1] // 2
    for slot in range(16):
        part, half = owner_place(slot)
        cols, rows = slice(part * 128, part * 128 + 128), slice(half * units, half * units + units)
        fc1[rows, cols] = land[slot, :units, :]
        fc2[rows, cols] = land[slot, units:, :]


def token_rows(device):
    return pl.ds(pl.multiple_of(device * TOK, TOK), TOK)


def chip_rows(chip):
    return pl.ds(pl.multiple_of(chip * PAIR, PAIR), PAIR)


class Gather:
    def __init__(self, group, full, send, recv):
        self.group, self.full, self.send, self.recv = group, full, send, recv
        self.started = []

    def copy(self, number, owner, device, first=0, count=TOK):
        rows = pl.ds(pl.multiple_of(owner * TOK + first, HALF), count)
        part = self.full.at[rows]
        return remote(part, part, self.send, self.recv, number, {"g": device})

    def go(self, *place):
        copy = self.copy(*place)
        copy.start()
        self.started.append(copy)

    def got(self, *place):
        self.copy(*place).wait_recv()

    def start(self):
        group = self.group
        self.go(2, group.me, group.peers[2])
        self.go(1, group.me, group.peers[1])
        self.go(0, group.me, group.sibling)

    def arrive(self, chip):
        group = self.group
        sibling = group.sibling
        if chip == 0:
            self.got(0, sibling, sibling)
        if chip == 1:
            self.got(1, group.peers[1], sibling)
            self.go(3, group.peers[1], group.peers[2], HALF, HALF)
            self.got(2, group.peers[2], sibling)
            self.go(4, group.peers[2], group.peers[1], 0, HALF)
            self.go(5, group.peers[1], sibling)
            self.go(6, group.peers[2], sibling)
            self.got(5, group.others[1], sibling)
        if chip == 2:
            self.got(6, group.others[2], sibling)
        if chip == 3:
            self.got(4, group.peers[3], sibling, 0, HALF)
            self.go(7, group.peers[3], sibling, 0, HALF)
            self.got(3, group.peers[3], sibling, HALF, HALF)
            self.go(8, group.peers[3], sibling, HALF, HALF)
            self.got(7, group.others[3], sibling, 0, HALF)
            self.got(8, group.others[3], sibling, HALF, HALF)

    def finish(self):
        for copy in self.started:
            copy.wait_send()


class Scatter:
    scratch = (
        pltpu.VMEM((4, TOK, 1024), F32),
        pltpu.VMEM((4, TOK, 1024), BF16),
        pltpu.VMEM((4, TOK, 1024), BF16),
        pltpu.VMEM((3, TOK, 1024), BF16),
        pltpu.VMEM((2, HALF, 1024), BF16),
        pltpu.VMEM((2, TOK, 1024), BF16),
        pltpu.SemaphoreType.DMA((10,)),
        pltpu.SemaphoreType.DMA((10,)),
    )

    def __init__(self, group, keep, near_out, near_in, far_out, mid_in, far_in, send, recv):
        self.group, self.keep, self.far_out = group, keep, far_out
        self.near_out, self.near_in, self.mid_in, self.far_in = near_out, near_in, mid_in, far_in
        y, x = ({"g": group.peers[chip]} for chip in (1, 2))
        low, high = pl.ds(0, HALF), pl.ds(HALF, HALF)
        self.copies = [
            *(remote(near_out.at[n], near_in.at[n], send, recv, n, {"g": group.sibling}) for n in range(4)),
            remote(far_out.at[2, low], mid_in.at[0], send, recv, 4, x),
            remote(far_out.at[2, high], mid_in.at[1], send, recv, 5, y),
            remote(far_out.at[0, high], far_in.at[0, high], send, recv, 6, y),
            remote(far_out.at[0, low], far_in.at[0, low], send, recv, 7, y),
            remote(far_out.at[1, low], far_in.at[1, low], send, recv, 8, x),
            remote(far_out.at[1, high], far_in.at[1, high], send, recv, 9, x),
        ]

    def push(self, chip, term):
        self.near_out[chip] = term(self.group.others[chip]).astype(BF16)
        self.copies[chip].start()
        self.keep[chip] = term(self.group.peers[chip])

    def relay(self, chip):
        self.copies[chip].wait_recv()
        total = self.keep[chip] + self.near_in[chip].astype(F32)
        if chip == 0:
            self.keep[0] = total
        if chip == 1:
            self.keep[1] = total
            self.far_out[0, HALF:] = total[HALF:].astype(BF16)
            self.copies[6].start()
        if chip == 2:
            self.keep[2] = total
            self.far_out[1, :HALF] = total[:HALF].astype(BF16)
            self.copies[8].start()
        if chip == 3:
            self.far_out[2] = total.astype(BF16)
            self.copies[4].start()
            self.copies[5].start()

    def across(self):
        self.copies[4].wait_recv()
        self.far_out[0, :HALF] = (self.keep[1, :HALF] + self.mid_in[0].astype(F32)).astype(BF16)
        self.copies[7].start()
        self.copies[5].wait_recv()
        self.far_out[1, HALF:] = (self.keep[2, HALF:] + self.mid_in[1].astype(F32)).astype(BF16)
        self.copies[9].start()

    def result(self):
        for number in (6, 8, 7, 9):
            self.copies[number].wait_recv()
        return self.keep[0] + self.far_in[0].astype(F32) + self.far_in[1].astype(F32)

    def finish(self):
        for copy in self.copies:
            copy.wait_send()


def norm_parts(value):
    average = jnp.mean(value, axis=-1, keepdims=True)
    centered = value - average
    variance = jnp.mean(centered * centered, axis=-1, keepdims=True)
    inverse = lax.rsqrt(variance + 1e-06)
    return centered * inverse, inverse


def norm_back(normal, inverse, grad):
    first = jnp.mean(grad, axis=-1, keepdims=True)
    second = jnp.mean(grad * normal, axis=-1, keepdims=True)
    return (grad - first - normal * second) * inverse


def store_blocks(ref, half, first, value):
    for part in range(8):
        slot = part % 4 * 4 + part // 4 * 2 + half
        ref[slot, first : first + value.shape[0], :] = value[:, part * 128 : part * 128 + 128].astype(ref.dtype)


def column_sum(value):
    return jnp.sum(value, axis=0, keepdims=True)


def attention_forward_stage(
    group, weights, gather, scatter, start,
    hidden, mods, weight, bias, proj, proj_bias,
    middle, branch, full, packed, attended, logsum,
):
    normal, _ = norm_parts(hidden[...])
    full[token_rows(group.me), :] = (normal * (1.0 + mods[1:2]) + mods[0:1]).astype(BF16)
    start()
    gather.start()
    weights.step(0)
    for chip in range(4):
        gather.arrive(chip)
        rows = chip_rows(group.chips[chip])
        packed[rows, :] = (nt(full[rows, :], weight[...]) + bias[...]).astype(BF16)
        if chip == 1:
            weights.step(1)
    weights.step(2)
    order = (3, 2, 1, 0)
    for place, chip in enumerate(order):
        rows = chip_rows(group.chips[chip])
        for head in range(2):
            query = packed[rows, head * 64 : head * 64 + 64] * BF16(HEAD_DIM**-0.5)
            key = packed[:, 128 + head * 64 : 192 + head * 64]
            value = packed[:, 256 + head * 64 : 320 + head * 64]
            scores = nt(key, query)
            top = jnp.max(scores, axis=0, keepdims=True)
            raised = jnp.exp(scores - top)
            total = jnp.sum(raised, axis=0, keepdims=True)
            output = tn(value, raised.astype(BF16)) * (1.0 / total)
            attended[rows, head * 64 : head * 64 + 64] = output.T.astype(BF16)
            logsum[head : head + 1, rows] = top + jnp.log(total)
        scatter.push(chip, lambda device: nn(attended[token_rows(device), :], proj[...]))
        if place:
            scatter.relay(order[place - 1])
    scatter.across()
    scatter.relay(0)
    weights.step(3)
    result = scatter.result() + proj_bias[...]
    branch[...] = result
    middle[...] = hidden[...] + mods[2:3] * result
    gather.finish()
    scatter.finish()


def mlp_forward_stage(
    group, weights, gather, scatter, ready,
    middle, mods, weight, bias, weight_two, bias_two,
    output, branch, full, inner, active,
):
    normal, _ = norm_parts(middle[...])
    full[token_rows(group.me), :] = (normal * (1.0 + mods[4:5]) + mods[3:4]).astype(BF16)
    gather.start()
    ready()
    weights.step(1)
    for chip in range(4):
        gather.arrive(chip)
        rows = chip_rows(group.chips[chip])
        value = nt(full[rows, :], weight[...]) + bias[...]
        inner[rows, :] = value
        bent = jnp.tanh(GELU_COEF * (value + 0.044715 * value * value * value))
        active[rows, :] = (0.5 * value * (1.0 + bent)).astype(BF16)
        scatter.push(chip, lambda device: nn(active[token_rows(device), :], weight_two[...]))
        if chip:
            scatter.relay(chip - 1)
        if chip == 2:
            weights.step(2)
    scatter.relay(3)
    scatter.across()
    weights.step(3)

    def end():
        result = scatter.result() + bias_two[...]
        branch[...] = result
        output[...] = middle[...] + mods[5:6] * result
        gather.finish()
        scatter.finish()

    return end


def mlp_backward_stage(
    group, owned_sum, gather, scatter, start, start_result,
    grad, mods, middle, branch, branch_one, weight, weight_two, full_two, inner, active,
    grad_middle, grad_attn, sums, weight_grads, bias_grad, full, grad_inner,
):
    if gather:
        full[token_rows(group.me), :] = (mods[5:6] * grad[...]).astype(BF16)
        start()
        gather.start()
    owned_sum.step(0)
    sums[1:2, :] = column_sum(full[token_rows(group.me), :].astype(F32))
    total = jnp.zeros((1, inner.shape[1]), F32)
    for chip in range(4):
        if gather:
            gather.arrive(chip)
        rows = chip_rows(group.chips[chip])
        grad_active = nt(full[rows, :], weight_two[...])
        value = inner[rows, :]
        bent = jnp.tanh(GELU_COEF * (value + 0.044715 * value * value * value))
        slope = GELU_COEF * (1.0 + (3 * 0.044715) * value * value)
        low = (grad_active * (0.5 * (1.0 + bent) + 0.5 * value * (1.0 - bent * bent) * slope)).astype(BF16)
        grad_inner[rows, :] = low
        total = total + column_sum(low.astype(F32))
        scatter.push(chip, lambda device: nn(grad_inner[token_rows(device), :], weight[...]))
        if chip:
            scatter.relay(chip - 1)
        if chip == 1:
            owned_sum.step(1)
    scatter.relay(3)
    scatter.across()
    owned_sum.step(2)
    bias_grad[...] = total
    units = weight.shape[0] // 2
    for half in range(2):
        cols = slice(half * units, half * units + units)
        store_blocks(weight_grads, half, 0, tn(grad_inner[:, cols], full_two[...]))
        store_blocks(weight_grads, half, units, tn(active[:, cols], full[...]))
    owned_sum.step(3)
    start_result()
    sums[0:1, :] = column_sum(grad[...] * branch[...])
    result = scatter.result()
    normal, inverse = norm_parts(middle[...])
    sums[2:3, :] = column_sum(result)
    sums[3:4, :] = column_sum(result * normal)
    back = grad[...] + norm_back(normal, inverse, (1.0 + mods[4:5]) * result)
    grad_middle[...] = back
    low = (mods[2:3] * back).astype(BF16)
    grad_attn[...] = low
    sums[4:5, :] = column_sum(back * branch_one[...])
    sums[5:6, :] = column_sum(low.astype(F32))
    owned_sum.step(4)
    if gather:
        gather.finish()
    scatter.finish()


def attention_backward_stage(
    group, owned_sum, gather, scatter,
    grad_middle, grad_attn, mods, hidden, weight, proj, full_one, packed, attended, logsum,
    grad_input, sums, weight_grads, bias_grad, full, grad_packed, key_grad, value_grad,
):
    full[token_rows(group.me), :] = grad_attn[...]
    gather.start()
    owned_sum.step(0)
    scale = HEAD_DIM**-0.5
    for chip in range(4):
        gather.arrive(chip)
        rows = chip_rows(group.chips[chip])
        grad_out = nt(full[rows, :], proj[...]).astype(BF16)
        for head in range(2):
            query = packed[rows, head * 64 : head * 64 + 64] * BF16(scale)
            key = packed[:, 128 + head * 64 : 192 + head * 64]
            value = packed[:, 256 + head * 64 : 320 + head * 64]
            part = grad_out[:, head * 64 : head * 64 + 64]
            probs = jnp.exp(nt(key, query) - logsum[head : head + 1, rows])
            grad_probs = nt(value, part)
            delta = jnp.sum(probs * grad_probs, axis=0, keepdims=True)
            grad_scores = (probs * (grad_probs - delta)).astype(BF16)
            grad_packed[rows, head * 64 : head * 64 + 64] = (tn(grad_scores, key) * scale).astype(BF16)
            key_term = nn(grad_scores, query)
            value_term = nn(probs.astype(BF16), part)
            if chip == 0:
                key_grad[head] = key_term
                value_grad[head] = value_term
            else:
                key_grad[head] += key_term
                value_grad[head] += value_term
        if chip == 1:
            owned_sum.step(1)
    for head in range(2):
        grad_packed[:, 128 + head * 64 : 192 + head * 64] = key_grad[head].astype(BF16)
        grad_packed[:, 256 + head * 64 : 320 + head * 64] = value_grad[head].astype(BF16)
    order = (3, 2, 1, 0)
    for place, chip in enumerate(order):
        scatter.push(chip, lambda device: nn(grad_packed[token_rows(device), :], weight[...]))
        if place:
            scatter.relay(order[place - 1])
    scatter.across()
    scatter.relay(0)
    owned_sum.step(2)
    for part in range(3):
        term = tn(grad_packed[:, part * 128 : part * 128 + 128], full_one[...])
        for half in range(2):
            store_blocks(weight_grads, half, part * 64, term[half * 64 : half * 64 + 64])
    term = tn(attended[...], full[...])
    for half in range(2):
        store_blocks(weight_grads, half, 192, term[half * 64 : half * 64 + 64])
    bias_grad[...] = column_sum(grad_packed[...].astype(F32))
    owned_sum.step(3)
    result = scatter.result()
    normal, inverse = norm_parts(hidden[...])
    sums[6:7, :] = column_sum(result)
    sums[7:8, :] = column_sum(result * normal)
    grad_input[...] = grad_middle[...] + norm_back(normal, inverse, (1.0 + mods[1:2]) * result)
    owned_sum.step(4)
    gather.finish()
    scatter.finish()


class Nothing:
    def step(self, step):
        pass


def forward_kernel(more, *refs):
    hidden, mods, weight, bias, proj, proj_bias, inner_bias, bias_two, mlp_rows, *refs = refs
    if more:
        next_rows, *refs = refs
    middle, branch, full, packed, attended, logsum, fc1, fc2, output, branch_two, full_two, inner, active, *refs = refs
    if more:
        next_qkv, next_proj, *refs = refs
    land, own_send, own_recv, *refs = refs
    if more:
        next_land, next_send, next_recv, *refs = refs
    send, recv, *scatter_refs = refs
    group, owners = Group(), Owners()
    partners = group.near + owners.near
    greet(partners)
    weights = OwnersGather(owners, land, own_send, own_recv)
    land[owners.slot] = mlp_rows[...]
    scatter = Scatter(group, *scatter_refs)
    attention_forward_stage(
        group, weights, Gather(group, full, send, recv), scatter, lambda: met(partners),
        hidden, mods, weight, bias, proj, proj_bias, middle, branch, full, packed, attended, logsum,
    )
    following = Nothing()
    if more:
        following = OwnersGather(owners, next_land, next_send, next_recv)
        next_land[owners.slot] = next_rows[...]
    following.step(0)

    def ready():
        weights.step(4)
        place_mlp(land, fc1, fc2)

    mlp_forward_stage(
        group, following, Gather(group, full_two, send, recv), scatter, ready,
        middle, mods, fc1, inner_bias, fc2, bias_two, output, branch_two, full_two, inner, active,
    )()
    following.step(4)
    if more:
        place_attention(next_land, next_qkv, next_proj)


def backward_kernel(more, *refs):
    grad, mods, middle, branch_two, branch, fc1, fc2, full_two, inner, active, *refs = refs
    hidden, qkv, proj, full_one, packed, attended, logsum, *refs = refs
    if more:
        parts, *refs = refs
    grad_input, sums, attn_parts, qkv_sum, fc1_sum, mlp_owned, *refs = refs
    if more:
        attn_owned, *refs = refs
    grad_middle, grad_attn, mlp_parts, full, full_attn, grad_inner, grad_packed, key_grad, value_grad, *refs = refs
    mlp_refs, refs = refs[:10], refs[10:]
    if more:
        attn_refs, refs = refs[:10], refs[10:]
    send, recv, *scatter_refs = refs
    group, owners = Group(), Owners()
    partners = group.near + owners.near
    greet(partners)
    scatter = Scatter(group, *scatter_refs)
    owned = OwnersScatter(owners, parts, attn_owned, *attn_refs) if more else Nothing()
    mlp_backward_stage(
        group, owned, Gather(group, full, send, recv), scatter, lambda: met(partners), lambda: None,
        grad, mods, middle, branch_two, branch, fc1, fc2, full_two, inner, active,
        grad_middle, grad_attn, sums, mlp_parts, fc1_sum, full, grad_inner,
    )
    owned = OwnersScatter(owners, mlp_parts, mlp_owned, *mlp_refs)
    attention_backward_stage(
        group, owned, Gather(group, full_attn, send, recv), scatter,
        grad_middle, grad_attn, mods, hidden, qkv, proj, full_one, packed, attended, logsum,
        grad_input, sums, attn_parts, qkv_sum, full_attn, grad_packed, key_grad, value_grad,
    )


class Beside:
    def __init__(self, weights, gather):
        self.weights, self.gather = weights, gather

    def step(self, step):
        self.weights.step(step)
        if step == 2:
            self.gather.start()
            self.gather.arrive(0)
        if step == 3:
            self.gather.arrive(1)
            self.gather.arrive(2)
        if step == 4:
            self.gather.arrive(3)
            self.gather.finish()


def turn_kernel(
    hidden, mods, qkv, qkv_bias, proj, proj_bias, inner_bias, bias_two, mlp_rows, grad,
    output, grad_input, sums, attn_parts, qkv_sum, fc1_sum, mlp_owned,
    middle, branch, branch_two, full, packed, attended, logsum, fc1, fc2, full_two, inner, active,
    land, own_send, own_recv,
    grad_middle, grad_attn, mlp_parts, full_grad, full_attn, grad_inner, grad_packed, key_grad, value_grad, *refs,
):
    mlp_refs, refs = refs[:10], refs[10:]
    back_refs, refs = refs[:8], refs[8:]
    grad_send, grad_recv, send, recv, *scatter_refs = refs
    group, owners = Group(), Owners()
    partners = group.near + owners.near
    greet(partners)
    weights = OwnersGather(owners, land, own_send, own_recv)
    land[owners.slot] = mlp_rows[...]
    full_grad[token_rows(group.me), :] = (mods[5:6] * grad[...]).astype(BF16)
    beside = Beside(weights, Gather(group, full_grad, grad_send, grad_recv))
    scatter, back = Scatter(group, *scatter_refs), Scatter(group, *back_refs)
    attention_forward_stage(
        group, beside, Gather(group, full, send, recv), scatter, lambda: met(partners),
        hidden, mods, qkv, qkv_bias, proj, proj_bias, middle, branch, full, packed, attended, logsum,
    )

    def ready():
        beside.step(4)
        place_mlp(land, fc1, fc2)

    end = mlp_forward_stage(
        group, Nothing(), Gather(group, full_two, send, recv), scatter, ready,
        middle, mods, fc1, inner_bias, fc2, bias_two, output, branch_two, full_two, inner, active,
    )
    mlp_backward_stage(
        group, Nothing(), None, back, None, end,
        grad, mods, middle, branch_two, branch, fc1, fc2, full_two, inner, active,
        grad_middle, grad_attn, sums, mlp_parts, fc1_sum, full_grad, grad_inner,
    )
    owned = OwnersScatter(owners, mlp_parts, mlp_owned, *mlp_refs)
    attention_backward_stage(
        group, owned, Gather(group, full_attn, send, recv), back,
        grad_middle, grad_attn, mods, hidden, qkv, proj, full, packed, attended, logsum,
        grad_input, sums, attn_parts, qkv_sum, full_attn, grad_packed, key_grad, value_grad,
    )


def first_kernel(
    rows, terms, bias, qkv, proj, halves, mods,
    land, own_send, own_recv, x_in, y_out, y_in, z_out, z_in, send, recv, all_send, all_recv,
):
    group, owners = Group(), Owners()
    partners = owners.near + (owners.to_across,) + tuple({"g": device} for device in group.everyone)
    greet(partners)
    weights = OwnersGather(owners, land, own_send, own_recv)
    land[owners.slot] = rows[...]
    halves[owners.x] = bias[...]
    met(partners)
    other = 1 - owners.x
    along_x = remote(terms.at[pl.ds(other * 8, 8)], x_in, send, recv, 0, owners.to_x)
    along_x.start()
    bias_there = remote(bias, halves.at[owners.x], send, recv, 1, owners.to_x)
    bias_there.start()
    weights.step(0)
    along_x.wait_recv()
    y_out[owners.x] = terms[pl.ds(owners.x * 8 + (1 - owners.y) * 4, 4)]
    y_out[other] = x_in[pl.ds((1 - owners.y) * 4, 4)]
    along_y = remote(y_out, y_in, send, recv, 2, owners.to_y)
    along_y.start()
    weights.step(1)
    along_y.wait_recv()
    own = terms[pl.ds(owners.x * 8 + owners.y * 4, 4)] + y_in[owners.x]
    far = x_in[pl.ds(owners.y * 4, 4)] + y_in[other]
    for z in range(4):
        z_out[z, owners.x] = own[z]
        z_out[z, other] = far[z]
    along_z = [
        remote(z_out.at[z], z_in.at[number], send, recv, 3 + number, device)
        for number, (z, device) in enumerate(
            ((owners.up, owners.to_up), (owners.across, owners.to_across), (owners.down, owners.to_down))
        )
    ]
    for copy in along_z:
        copy.start()
    weights.step(2)
    total = z_out[owners.z]
    for number, copy in enumerate(along_z):
        copy.wait_recv()
        total = total + z_in[number]
    mods[group.me] = total
    around = [
        remote(mods.at[group.me], mods.at[group.me], all_send, all_recv, number, {"g": device})
        for number, device in enumerate(group.everyone)
    ]
    for copy in around:
        copy.start()
    weights.step(3)
    for number, device in enumerate(group.everyone):
        remote(mods.at[device], mods.at[device], all_send, all_recv, number, {"g": device}).wait_recv()
    remote(bias, halves.at[other], send, recv, 1, owners.to_x).wait_recv()
    weights.step(4)
    place_attention(land, qkv, proj)
    for copy in (along_x, bias_there, along_y, *along_z, *around):
        copy.wait_send()


def last_kernel(
    parts, blocks, own, ada, owned, every, summed, copies, act_grad,
    *refs,
):
    group, owners = Group(), Owners()
    partners = owners.near + tuple({"g": device} for device in group.everyone)
    greet(partners)
    owned_sum = OwnersScatter(owners, parts, owned, *refs[:10])
    own_send, own_recv, inbox, send, recv, all_send, all_recv, *refs = refs[10:]
    act_all, act_out, act_in, act_send, act_recv, x_send, x_recv = refs
    gather = OwnersGather(owners, every, own_send, own_recv)
    met(partners)
    around = [
        remote(blocks.at[device], inbox.at[number], send, recv, number, {"g": device})
        for number, device in enumerate(group.everyone)
    ]
    for copy in around:
        copy.start()
    owned_sum.step(0)
    total = blocks[group.me]
    for number, copy in enumerate(around):
        copy.wait_recv()
        total = total + inbox[number]
    rows = blocks.shape[1]
    every[owners.slot, 0:rows] = total
    every[owners.slot, rows:] = own[...]
    gather.step(0)
    gather.step(1)
    owned_sum.step(1)
    gather.step(2)
    gather.step(3)
    owned_sum.step(2)
    gather.step(4)
    act = jnp.zeros(act_out.shape, F32)
    lines = ada.shape[2] // 128
    for layer in range(ada.shape[0]):
        for line in range(lines):
            place = layer * lines + line
            left = jnp.where(owners.x == 0, every[:, place, :], every[:, ada.shape[0] * lines + place, :])
            right = ada[layer, :, line * 128 : line * 128 + 128].astype(F32)
            act = act + lax.dot_general(
                left, right, (((1,), (1,)), ((), ())), precision=lax.Precision.HIGHEST, preferred_element_type=F32
            )
    act_all[group.me] = act
    acts = [
        remote(act_all.at[group.me], act_all.at[group.me], act_send, act_recv, number, {"g": device})
        for number, device in enumerate(group.everyone)
    ]
    for copy in acts:
        copy.start()
    total = every[0]
    for slot in range(1, 16):
        total = total + every[slot]
    summed[...] = total
    copies[group.me] = total[0:rows]
    spread = [
        remote(copies.at[group.me], copies.at[group.me], all_send, all_recv, number, {"g": device})
        for number, device in enumerate(group.everyone)
    ]
    for copy in spread:
        copy.start()
    for number, device in enumerate(group.everyone):
        remote(act_all.at[device], act_all.at[device], act_send, act_recv, number, {"g": device}).wait_recv()
    act = act_all[0]
    for device in range(1, 8):
        act = act + act_all[device]
    act_out[...] = act
    over = remote(act_out, act_in, x_send, x_recv, 0, owners.to_x)
    over.start()
    owned_sum.step(3)
    for number, device in enumerate(group.everyone):
        remote(copies.at[device], copies.at[device], all_send, all_recv, number, {"g": device}).wait_recv()
    over.wait_recv()
    act_grad[...] = act_out[...] + act_in[...]
    owned_sum.step(4)
    for copy in (*around, *spread, *acts, over):
        copy.wait_send()


def plain_call(kernel, number, outs, scratch, *operands):
    space = pl.BlockSpec(memory_space=pltpu.VMEM)
    return pl.pallas_call(
        kernel,
        out_shape=[jax.ShapeDtypeStruct(shape, kind) for shape, kind in outs],
        in_specs=[space] * len(operands),
        out_specs=[space] * len(outs),
        scratch_shapes=scratch,
        compiler_params=pltpu.CompilerParams(
            collective_id=number, has_side_effects=True, vmem_limit_bytes=VMEM_LIMIT
        ),
        cost_estimate=pl.CostEstimate(flops=10**10, bytes_accessed=8 << 20, transcendentals=1 << 20),
    )(*operands)


def call(kernel, number, outs, scratch, *operands):
    pair = [pltpu.SemaphoreType.DMA((9,)), pltpu.SemaphoreType.DMA((9,))]
    return plain_call(kernel, number, outs, [*scratch, *pair, *Scatter.scratch], *operands)


def first(rows, terms, bias):
    width = 1024
    outs = [
        ((384, width), BF16), ((128, width), BF16), ((2, *bias.shape), F32), ((8, 2, 8, 128), F32),
    ]
    scratch = [
        pltpu.VMEM((16, *rows.shape), BF16), *OwnersGather.scratch,
        pltpu.VMEM((8, 8, 128), F32), pltpu.VMEM((2, 4, 8, 128), F32), pltpu.VMEM((2, 4, 8, 128), F32),
        pltpu.VMEM((4, 2, 8, 128), F32), pltpu.VMEM((3, 2, 8, 128), F32),
        pltpu.SemaphoreType.DMA((6,)), pltpu.SemaphoreType.DMA((6,)),
        pltpu.SemaphoreType.DMA((7,)), pltpu.SemaphoreType.DMA((7,)),
    ]
    return plain_call(first_kernel, 10, outs, scratch, rows, terms, bias)


def last(parts, blocks, own, ada):
    rows = blocks.shape[1]
    outs = [
        (parts.shape[1:], F32), ((16, rows + own.shape[0], 128), F32), ((rows + own.shape[0], 128), F32),
        (blocks.shape, F32), ((16, 128), F32),
    ]
    scratch = [
        *OwnersScatter.scratch(parts.shape[1]), *OwnersGather.scratch, pltpu.VMEM((7, rows, 128), F32),
        *([pltpu.SemaphoreType.DMA((7,))] * 4),
        pltpu.VMEM((8, 16, 128), F32), pltpu.VMEM((16, 128), F32), pltpu.VMEM((16, 128), F32),
        *([pltpu.SemaphoreType.DMA((7,))] * 2), *([pltpu.SemaphoreType.DMA((1,))] * 2),
    ]
    return plain_call(last_kernel, 11, outs, scratch, parts, blocks, own, ada)


def forward(operands, rows=None):
    hidden, weight, proj, mlp_rows = operands[0], operands[2], operands[4], operands[8]
    width, units = hidden.shape[1], mlp_rows.shape[0]
    token, whole = ((TOK, width), F32), ((SEQ_LEN, width), BF16)
    outs = [
        token, token, whole, ((SEQ_LEN, weight.shape[0]), BF16), ((SEQ_LEN, proj.shape[0]), BF16), ((2, SEQ_LEN), F32),
        ((units, width), BF16), ((units, width), BF16),
        token, token, whole, ((SEQ_LEN, units), F32), ((SEQ_LEN, units), BF16),
    ]
    scratch = [pltpu.VMEM((16, *mlp_rows.shape), BF16), *OwnersGather.scratch]
    if rows is None:
        return call(functools.partial(forward_kernel, False), 0, outs, scratch, *operands)
    outs += [(weight.shape, BF16), (proj.shape, BF16)]
    scratch += [pltpu.VMEM((16, *rows.shape), BF16), *OwnersGather.scratch]
    return call(functools.partial(forward_kernel, True), 1, outs, scratch, *operands, rows)


def backward(operands, parts=None):
    grad, fc1, qkv = operands[0], operands[5], operands[11]
    width, units = grad.shape[1], fc1.shape[0]
    outs = [
        ((TOK, width), F32), ((8, width), F32), ((16, 256, 128), BF16),
        ((1, qkv.shape[0]), F32), ((1, units), F32), ((units, 128), F32),
    ]
    if parts is not None:
        outs += [(parts.shape[1:], F32)]
    scratch = [
        pltpu.VMEM((TOK, width), F32),
        pltpu.VMEM((TOK, width), BF16),
        pltpu.VMEM((16, units, 128), BF16),
        pltpu.VMEM((SEQ_LEN, width), BF16),
        pltpu.VMEM((SEQ_LEN, width), BF16),
        pltpu.VMEM((SEQ_LEN, units), BF16),
        pltpu.VMEM((SEQ_LEN, qkv.shape[0]), BF16),
        pltpu.VMEM((2, SEQ_LEN, HEAD_DIM), F32),
        pltpu.VMEM((2, SEQ_LEN, HEAD_DIM), F32),
        *OwnersScatter.scratch(units),
    ]
    if parts is None:
        return call(functools.partial(backward_kernel, False), 2, outs, scratch, *operands)
    scratch += OwnersScatter.scratch(parts.shape[1])
    return call(functools.partial(backward_kernel, True), 3, outs, scratch, *operands, parts)


def turn(*operands):
    hidden, qkv, proj, mlp_rows = operands[0], operands[2], operands[4], operands[8]
    width, units, cols = hidden.shape[1], mlp_rows.shape[0], qkv.shape[0]
    outs = [
        ((TOK, width), F32), ((TOK, width), F32), ((8, width), F32), ((16, 256, 128), BF16),
        ((1, cols), F32), ((1, units), F32), ((units, 128), F32),
    ]
    token, whole = pltpu.VMEM((TOK, width), F32), pltpu.VMEM((SEQ_LEN, width), BF16)
    head = pltpu.VMEM((2, SEQ_LEN, HEAD_DIM), F32)
    scratch = [
        token, token, token, whole, pltpu.VMEM((SEQ_LEN, cols), BF16), pltpu.VMEM((SEQ_LEN, proj.shape[0]), BF16),
        pltpu.VMEM((2, SEQ_LEN), F32), pltpu.VMEM((units, width), BF16), pltpu.VMEM((units, width), BF16),
        whole, pltpu.VMEM((SEQ_LEN, units), F32), pltpu.VMEM((SEQ_LEN, units), BF16),
        pltpu.VMEM((16, units, 128), BF16), *OwnersGather.scratch,
        token, pltpu.VMEM((TOK, width), BF16), pltpu.VMEM((16, units, 128), BF16), whole, whole,
        pltpu.VMEM((SEQ_LEN, units), BF16), pltpu.VMEM((SEQ_LEN, cols), BF16), head, head,
        *OwnersScatter.scratch(units), *Scatter.scratch,
        pltpu.SemaphoreType.DMA((9,)), pltpu.SemaphoreType.DMA((9,)),
    ]
    return call(turn_kernel, 4, outs, scratch, *operands)


RX = ("row", "xh")
ALL = ("row", "xh", "g")


def highest(left, right):
    return jnp.dot(left, right, precision=lax.Precision.HIGHEST, preferred_element_type=F32)


def highest_tn(left, right):
    return lax.dot_general(
        left, right, (((0,), (0,)), ((), ())), precision=lax.Precision.HIGHEST, preferred_element_type=F32
    )


def highest_nt(left, right):
    return lax.dot_general(
        left, right, (((1,), (1,)), ((), ())), precision=lax.Precision.HIGHEST, preferred_element_type=F32
    )


def small_sums(sums, qkv_sum, fc1_sum):
    mod_grad = jnp.concatenate([sums[6:8], sums[4:5], sums[2:4], sums[0:1]])
    return mod_grad, sums[5], sums[1], qkv_sum, fc1_sum


def on_device(
    tokens, cotangent, timestep, class_label, class_table, ada_weight, ada_bias, qkv_weight, qv_bias,
    proj_weight, proj_bias, fc1_weight, fc1_bias, fc2_weight, fc2_bias,
):
    row_index, half_index, _ = (lax.axis_index(axis) for axis in ALL)
    width = tokens.shape[1]
    width_part = class_table.shape[1]
    latent_count = timestep.shape[0]
    layer_count, _, ada_cols = ada_weight.shape
    units = fc1_weight.shape[2]
    attn_rows = [jnp.concatenate([qkv_weight[l].T, proj_weight[l]]) for l in range(layer_count)]
    mlp_rows = [jnp.concatenate([fc1_weight[l].T, fc2_weight[l]]) for l in range(layer_count)]
    column_ids = row_index * width_part + lax.iota(jnp.int32, width_part)
    half_width = width // 2
    frequency = jnp.exp(-LOG_BASE * (column_ids % half_width).astype(F32) / half_width)
    angles = timestep.astype(F32)[:, None] * frequency[None, :]
    waves = jnp.where(column_ids[None, :] < half_width, jnp.cos(angles), jnp.sin(angles))
    class_hot = (class_label[:, None] == lax.iota(jnp.int32, class_table.shape[0])[None, :]).astype(F32)
    condition = waves + highest(class_hot, class_table.astype(F32))
    cond_act = condition * jax.nn.sigmoid(condition)
    ada_float = ada_weight.astype(F32)
    terms = jnp.stack([highest(cond_act, ada_float[l]) for l in range(layer_count)], axis=1)
    terms = terms.reshape(latent_count // 2, 2, -1, 128).swapaxes(0, 1).reshape(latent_count, -1, 128)
    lines = layer_count * ada_cols // 128
    terms = jnp.pad(terms, ((0, 0), (0, 8 - lines), (0, 0)))
    bias_rows = jnp.concatenate([qv_bias.reshape(layer_count, -1), fc1_bias], axis=1).reshape(-1, 128)
    bias_count = bias_rows.shape[0]
    bias_rows = jnp.pad(bias_rows, ((0, 8 - bias_count), (0, 0)))
    qkv, proj, halves, mod_parts = first(attn_rows[0], terms, bias_rows)
    modulation = mod_parts[:, :, :lines].reshape(8, 2, layer_count, ada_cols).transpose(2, 1, 0, 3)
    modulation = modulation.reshape(layer_count, 6 * width) + ada_bias
    mods = jnp.pad(modulation.reshape(layer_count, 6, width), ((0, 0), (0, 2), (0, 0)))
    halves = halves[:, :bias_count].reshape(2, layer_count, -1)

    saved = []
    hidden = tokens
    small = [None] * layer_count
    attn_grads, mlp_grads = [None] * layer_count, [None] * layer_count
    for number in range(layer_count):
        query = halves[:, number, :HEAD_DIM].reshape(1, -1)
        value = halves[:, number, HEAD_DIM : 2 * HEAD_DIM].reshape(1, -1)
        qkv_bias = jnp.concatenate([query, jnp.zeros_like(query), value], axis=1)
        inner_bias = halves[:, number, 2 * HEAD_DIM :].reshape(1, -1)
        operands = (
            hidden, mods[number], qkv, qkv_bias, proj, proj_bias[number : number + 1], inner_bias,
            fc2_bias[number : number + 1], mlp_rows[number],
        )
        if number + 1 < layer_count:
            (
                middle, branch, full, packed, attended, logsum, fc1, fc2, output, branch_two, full_two, inner, active, *later
            ) = forward(operands, attn_rows[number + 1])
            saved.append(
                (middle, branch_two, branch, fc1, fc2, full_two, inner, active, hidden, qkv, proj, full, packed, attended, logsum)
            )
            hidden = output
            qkv, proj = later
        else:
            mixed, grad, sums, attn_parts, qkv_sum, fc1_sum, mlp_grads[number] = turn(*operands, cotangent)
            small[number] = small_sums(sums, qkv_sum, fc1_sum)
    for number in reversed(range(layer_count - 1)):
        grad, sums, attn_parts, qkv_sum, fc1_sum, mlp_grads[number], attn_grads[number + 1] = backward(
            (grad, mods[number], *saved[number]), attn_parts
        )
        small[number] = small_sums(sums, qkv_sum, fc1_sum)
    tokens_grad = grad

    mod_grad, proj_sum, fc2_sum, qkv_sum, fc1_sum = (jnp.stack(parts) for parts in zip(*small))
    mod_send = mod_grad.reshape(layer_count, 2, 8, ada_cols).transpose(2, 1, 0, 3).reshape(8, -1)
    bias_send = jnp.concatenate([proj_sum, fc2_sum]).reshape(2 * layer_count, 8, -1).swapaxes(0, 1).reshape(8, -1)
    mod_size = mod_send.shape[1]
    send = jnp.concatenate([mod_send, bias_send], axis=1).reshape(8, -1, 128)
    qv_sum = qkv_sum.reshape(layer_count, 3, 2, HEAD_DIM)[:, ::2].transpose(2, 0, 1, 3).reshape(2, -1)
    fc1_half = fc1_sum.reshape(layer_count, 2, units).swapaxes(0, 1).reshape(2, -1)
    own = jnp.concatenate([qv_sum, fc1_half], axis=1).reshape(-1, 128)
    own_count = own.shape[0]
    own = jnp.pad(own, ((0, 16 - own_count), (0, 0)))
    attn_grads[0], every, summed, copies, act_grad = last(attn_parts, send, own, ada_weight)
    every = every[:, : mod_size // 128].reshape(4, 2, 2, 2, layer_count, ada_cols)
    mod_cols = lax.dynamic_index_in_dim(every, half_index, axis=3, keepdims=False)
    mod_cols = mod_cols.transpose(1, 0, 2, 3, 4).reshape(latent_count, layer_count, ada_cols)
    copies = copies.reshape(8, -1)
    ada_bias_grad = copies[:, :mod_size].reshape(8, 2, layer_count, ada_cols).transpose(2, 1, 0, 3)
    ada_bias_grad = ada_bias_grad.reshape(layer_count, 6 * width)
    bias_total = copies[:, mod_size:].reshape(8, 2 * layer_count, -1).swapaxes(0, 1).reshape(2, layer_count, width)
    own_total = summed[send.shape[1] :][:own_count].reshape(2, -1)
    own_total = lax.dynamic_index_in_dim(own_total, half_index, keepdims=False)
    qv_bias_grad = own_total[: layer_count * 2 * HEAD_DIM].reshape(layer_count, 2, HEAD_DIM)
    fc1_bias_grad = own_total[layer_count * 2 * HEAD_DIM :].reshape(layer_count, units)
    ada_weight_grad = jnp.stack([highest_tn(cond_act, mod_cols[:, l]) for l in range(layer_count)])
    act_grad = act_grad.reshape(4, 2, 2, width_part).swapaxes(0, 1).reshape(latent_count, width_part)
    gate = jax.nn.sigmoid(condition)
    cond_grad = act_grad * (gate * (1.0 + condition * (1.0 - gate)))
    table_grad = highest_tn(class_hot, cond_grad)
    attn_grads, mlp_grads = jnp.stack(attn_grads), jnp.stack(mlp_grads)
    return (
        mixed,
        tokens_grad,
        cond_grad,
        table_grad,
        ada_weight_grad,
        ada_bias_grad,
        attn_grads[:, :192].swapaxes(1, 2),
        qv_bias_grad,
        attn_grads[:, 192:],
        bias_total[0],
        mlp_grads[:, :units].swapaxes(1, 2),
        fc1_bias_grad,
        mlp_grads[:, units:],
        bias_total[1],
    )


def solution(mesh):
    split = Mesh(mesh.devices.reshape(mesh.shape["row"], 2, 8), ALL)
    col = ("xh", "g")
    in_specs = (
        P(ALL, None), P(ALL, None), P(), P(), P(None, "row"), P(None, "row", col), P(),
        P(None, "row", col), P(None, None, col), P(None, col, "row"), P(), P(None, "row", col),
        P(None, col), P(None, col, "row"), P(),
    )
    out_specs = (
        P(ALL, None), P(ALL, None), P(None, "row"), P(None, "row"), P(None, "row", col), P(),
        P(None, "row", col), P(None, None, col), P(None, col, "row"), P(), P(None, "row", col),
        P(None, col), P(None, col, "row"), P(),
    )
    return jax.shard_map(on_device, mesh=split, in_specs=in_specs, out_specs=out_specs, check_vma=False)
```

```python
import functools
import math

import jax
import jax.numpy as jnp
from jax import lax
from jax.experimental import pallas as pl
from jax.experimental.pallas import tpu as pltpu
from jax.sharding import Mesh
from jax.sharding import PartitionSpec as P

MESH = pl.DeviceIdType.MESH
HEAD_DIM = 64
SEQ_LEN = 1024
GELU_COEF = math.sqrt(2.0 / math.pi)
LOG_BASE = math.log(10000.0)
F32 = jnp.float32
BF16 = jnp.bfloat16
TOK = 128
PAIR = 2 * TOK
HALF = TOK // 2
VMEM_LIMIT = 60 * 1024 * 1024


def nn(left, right):
    return lax.dot_general(left, right, (((1,), (0,)), ((), ())), preferred_element_type=F32)


def nt(left, right):
    return lax.dot_general(left, right, (((1,), (1,)), ((), ())), preferred_element_type=F32)


def tn(left, right):
    return lax.dot_general(left, right, (((0,), (0,)), ((), ())), preferred_element_type=F32)


class Group:
    def __init__(self):
        me = lax.axis_index("g")
        self.me = me
        self.core = lax.rem(me, 2)
        chip = lax.div(me, 2)
        x, y = lax.div(chip, 2), lax.rem(chip, 2)
        self.chips = (chip, 2 * x + 1 - y, 2 * (1 - x) + y, 2 * (1 - x) + 1 - y)
        self.peers = tuple(2 * c + self.core for c in self.chips)
        self.others = tuple(2 * c + 1 - self.core for c in self.chips)
        self.sibling = self.others[0]

        self.near = tuple({"g": device} for device in (self.sibling, *self.peers[1:3]))
        self.everyone = self.peers[1:] + self.others


class Owners:
    def __init__(self):
        row, self.x = lax.axis_index("row"), lax.axis_index("xh")
        self.y, self.z = lax.div(row, 4), lax.rem(row, 4)
        self.up, self.across, self.down = (lax.rem(self.z + by, 4) for by in (1, 2, 3))
        self.slot = self.z * 4 + self.y * 2 + self.x
        self.to_x, self.to_y = {"xh": 1 - self.x}, {"row": (1 - self.y) * 4 + self.z}
        self.to_up, self.to_down = {"row": self.y * 4 + self.up}, {"row": self.y * 4 + self.down}
        self.to_across = {"row": self.y * 4 + self.across}
        self.near = (self.to_x, self.to_y, self.to_up, self.to_down)


def greet(devices):
    for device in devices:
        pl.semaphore_signal(pltpu.get_barrier_semaphore(), inc=1, device_id=device, device_id_type=MESH)


def met(devices):
    pl.semaphore_wait(pltpu.get_barrier_semaphore(), len(devices))


def remote(src, dst, send, recv, number, device):
    return pltpu.make_async_remote_copy(
        src_ref=src, dst_ref=dst, send_sem=send.at[number], recv_sem=recv.at[number],
        device_id=device, device_id_type=MESH,
    )


class OwnersGather:
    scratch = (pltpu.SemaphoreType.DMA((6,)), pltpu.SemaphoreType.DMA((6,)))

    def __init__(self, owners, ref, send, recv):
        self.owners, self.ref, self.send, self.recv = owners, ref, send, recv

    def copy(self, number, first, count, device):
        part = self.ref.at[pl.ds(first, count)]
        return remote(part, part, self.send, self.recv, number, device)

    def step(self, step):
        o = self.owners
        pair, four, up, across, down = o.z * 4 + o.y * 2, o.z * 4, o.up * 4, o.across * 4, o.down * 4
        if step == 0:
            self.copy(0, o.slot, 1, o.to_x).start()
        if step == 1:
            self.copy(0, pair + 1 - o.x, 1, o.to_x).wait_recv()
            self.copy(1, pair, 2, o.to_y).start()
        if step == 2:
            self.copy(1, four + (1 - o.y) * 2, 2, o.to_y).wait_recv()
            self.copy(2, four, 4, o.to_up).start()
            self.copy(3, four, 4, o.to_down).start()
        if step == 3:
            self.copy(2, down, 4, o.to_up).wait_recv()
            self.copy(4, down, 2, o.to_up).start()
            self.copy(3, up, 4, o.to_down).wait_recv()
            self.copy(5, up + 2, 2, o.to_down).start()
        if step == 4:
            self.copy(4, across, 2, o.to_up).wait_recv()
            self.copy(5, across + 2, 2, o.to_down).wait_recv()
            self.copy(0, o.slot, 1, o.to_x).wait_send()
            self.copy(1, pair, 2, o.to_y).wait_send()
            self.copy(2, four, 4, o.to_up).wait_send()
            self.copy(3, four, 4, o.to_down).wait_send()
            self.copy(4, down, 2, o.to_up).wait_send()
            self.copy(5, up + 2, 2, o.to_down).wait_send()


class OwnersScatter:
    @staticmethod
    def scratch(rows):
        shapes = ((2, 2), (2, 4), (2, 4), (2,), (2,), (1,), (1,))
        return (
            *(pltpu.VMEM((*shape, rows, 128), BF16) for shape in shapes),
            pltpu.VMEM((4, rows, 128), F32),
            pltpu.SemaphoreType.DMA((6,)),
            pltpu.SemaphoreType.DMA((6,)),
        )

    def __init__(self, owners, parts, out, in0, out1, in1, out2, in2, out3, in3, total, send, recv):
        self.owners, self.parts, self.out, self.total = owners, parts, out, total
        self.out1, self.in0, self.in1 = out1, in0, in1
        self.out2, self.in2, self.out3, self.in3 = out2, in2, out3, in3
        across = owners.across * 4
        self.copies = [
            remote(parts.at[pl.ds(across, 2)], in0.at[0], send, recv, 0, owners.to_up),
            remote(parts.at[pl.ds(across + 2, 2)], in0.at[1], send, recv, 1, owners.to_down),
            remote(out1.at[0], in1.at[0], send, recv, 2, owners.to_up),
            remote(out1.at[1], in1.at[1], send, recv, 3, owners.to_down),
            remote(out2, in2, send, recv, 4, owners.to_y),
            remote(out3, in3, send, recv, 5, owners.to_x),
        ]

    def step(self, step):
        o, copies, parts, total = self.owners, self.copies, self.parts, self.total
        up, down = o.up * 4, o.down * 4
        if step == 0:
            copies[0].start()
            copies[1].start()
        if step == 1:
            copies[0].wait_recv()
            self.out1[0, 0:2] = (parts[pl.ds(up, 2)].astype(F32) + self.in0[0].astype(F32)).astype(BF16)
            self.out1[0, 2:4] = parts[pl.ds(up + 2, 2)]
            copies[2].start()
            copies[1].wait_recv()
            self.out1[1, 0:2] = parts[pl.ds(down, 2)]
            self.out1[1, 2:4] = (parts[pl.ds(down + 2, 2)].astype(F32) + self.in0[1].astype(F32)).astype(BF16)
            copies[3].start()
        if step == 2:
            copies[2].wait_recv()
            copies[3].wait_recv()
            for block in range(4):
                total[block] = (
                    parts[o.z * 4 + block].astype(F32)
                    + self.in1[0, block].astype(F32)
                    + self.in1[1, block].astype(F32)
                )
            self.out2[...] = total[pl.ds((1 - o.y) * 2, 2)].astype(BF16)
            copies[4].start()
        if step == 3:
            copies[4].wait_recv()
            total[0:2] = total[pl.ds(o.y * 2, 2)] + self.in2[...].astype(F32)
            self.out3[...] = total[pl.ds(1 - o.x, 1)].astype(BF16)
            copies[5].start()
        if step == 4:
            copies[5].wait_recv()
            self.out[...] = total[o.x] + self.in3[0].astype(F32)
            for copy in copies:
                copy.wait_send()


def owner_place(slot):
    z, y, half = slot // 4, slot // 2 % 2, slot % 2
    return y * 4 + z, half


def place_attention(land, qkv, proj):
    for slot in range(16):
        part, half = owner_place(slot)
        cols = slice(part * 128, part * 128 + 128)
        for kind in range(3):
            first = kind * 128 + half * 64
            qkv[first : first + 64, cols] = land[slot, kind * 64 : kind * 64 + 64, :]
        proj[half * 64 : half * 64 + 64, cols] = land[slot, 192:256, :]


def place_mlp(land, fc1, fc2):
    units = land.shape[1] // 2
    for slot in range(16):
        part, half = owner_place(slot)
        cols, rows = slice(part * 128, part * 128 + 128), slice(half * units, half * units + units)
        fc1[rows, cols] = land[slot, :units, :]
        fc2[rows, cols] = land[slot, units:, :]


def token_rows(device):
    return pl.ds(pl.multiple_of(device * TOK, TOK), TOK)


def chip_rows(chip):
    return pl.ds(pl.multiple_of(chip * PAIR, PAIR), PAIR)


class Gather:
    def __init__(self, group, full, send, recv):
        self.group, self.full, self.send, self.recv = group, full, send, recv
        self.started = []

    def copy(self, number, owner, device, first=0, count=TOK):
        rows = pl.ds(pl.multiple_of(owner * TOK + first, HALF), count)
        part = self.full.at[rows]
        return remote(part, part, self.send, self.recv, number, {"g": device})

    def go(self, *place):
        copy = self.copy(*place)
        copy.start()
        self.started.append(copy)

    def got(self, *place):
        self.copy(*place).wait_recv()

    def start(self):
        group = self.group
        self.go(2, group.me, group.peers[2])
        self.go(1, group.me, group.peers[1])
        self.go(0, group.me, group.sibling)

    def arrive(self, chip):
        group = self.group
        sibling = group.sibling
        if chip == 0:
            self.got(0, sibling, sibling)
        if chip == 1:
            self.got(1, group.peers[1], sibling)
            self.go(3, group.peers[1], group.peers[2], HALF, HALF)
            self.got(2, group.peers[2], sibling)
            self.go(4, group.peers[2], group.peers[1], 0, HALF)
            self.go(5, group.peers[1], sibling)
            self.go(6, group.peers[2], sibling)
            self.got(5, group.others[1], sibling)
        if chip == 2:
            self.got(6, group.others[2], sibling)
        if chip == 3:
            self.got(4, group.peers[3], sibling, 0, HALF)
            self.go(7, group.peers[3], sibling, 0, HALF)
            self.got(3, group.peers[3], sibling, HALF, HALF)
            self.go(8, group.peers[3], sibling, HALF, HALF)
            self.got(7, group.others[3], sibling, 0, HALF)
            self.got(8, group.others[3], sibling, HALF, HALF)

    def finish(self):
        for copy in self.started:
            copy.wait_send()


class Scatter:
    scratch = (
        pltpu.VMEM((4, TOK, 1024), F32),
        pltpu.VMEM((4, TOK, 1024), BF16),
        pltpu.VMEM((4, TOK, 1024), BF16),
        pltpu.VMEM((3, TOK, 1024), BF16),
        pltpu.VMEM((2, HALF, 1024), BF16),
        pltpu.VMEM((2, TOK, 1024), BF16),
        pltpu.SemaphoreType.DMA((10,)),
        pltpu.SemaphoreType.DMA((10,)),
    )

    def __init__(self, group, keep, near_out, near_in, far_out, mid_in, far_in, send, recv):
        self.group, self.keep, self.far_out = group, keep, far_out
        self.near_out, self.near_in, self.mid_in, self.far_in = near_out, near_in, mid_in, far_in
        y, x = ({"g": group.peers[chip]} for chip in (1, 2))
        low, high = pl.ds(0, HALF), pl.ds(HALF, HALF)
        self.copies = [
            *(remote(near_out.at[n], near_in.at[n], send, recv, n, {"g": group.sibling}) for n in range(4)),
            remote(far_out.at[2, low], mid_in.at[0], send, recv, 4, x),
            remote(far_out.at[2, high], mid_in.at[1], send, recv, 5, y),
            remote(far_out.at[0, high], far_in.at[0, high], send, recv, 6, y),
            remote(far_out.at[0, low], far_in.at[0, low], send, recv, 7, y),
            remote(far_out.at[1, low], far_in.at[1, low], send, recv, 8, x),
            remote(far_out.at[1, high], far_in.at[1, high], send, recv, 9, x),
        ]

    def push(self, chip, term):
        self.near_out[chip] = term(self.group.others[chip]).astype(BF16)
        self.copies[chip].start()
        self.keep[chip] = term(self.group.peers[chip])

    def relay(self, chip):
        self.copies[chip].wait_recv()
        total = self.keep[chip] + self.near_in[chip].astype(F32)
        if chip == 0:
            self.keep[0] = total
        if chip == 1:
            self.keep[1] = total
            self.far_out[0, HALF:] = total[HALF:].astype(BF16)
            self.copies[6].start()
        if chip == 2:
            self.keep[2] = total
            self.far_out[1, :HALF] = total[:HALF].astype(BF16)
            self.copies[8].start()
        if chip == 3:
            self.far_out[2] = total.astype(BF16)
            self.copies[4].start()
            self.copies[5].start()

    def across(self):
        self.copies[4].wait_recv()
        self.far_out[0, :HALF] = (self.keep[1, :HALF] + self.mid_in[0].astype(F32)).astype(BF16)
        self.copies[7].start()
        self.copies[5].wait_recv()
        self.far_out[1, HALF:] = (self.keep[2, HALF:] + self.mid_in[1].astype(F32)).astype(BF16)
        self.copies[9].start()

    def result(self):
        for number in (6, 8, 7, 9):
            self.copies[number].wait_recv()
        return self.keep[0] + self.far_in[0].astype(F32) + self.far_in[1].astype(F32)

    def finish(self):
        for copy in self.copies:
            copy.wait_send()


def norm_parts(value):
    average = jnp.mean(value, axis=-1, keepdims=True)
    centered = value - average
    variance = jnp.mean(centered * centered, axis=-1, keepdims=True)
    inverse = lax.rsqrt(variance + 1e-06)
    return centered * inverse, inverse


def norm_back(normal, inverse, grad):
    first = jnp.mean(grad, axis=-1, keepdims=True)
    second = jnp.mean(grad * normal, axis=-1, keepdims=True)
    return (grad - first - normal * second) * inverse


def store_blocks(ref, half, first, value):
    for part in range(8):
        slot = part % 4 * 4 + part // 4 * 2 + half
        ref[slot, first : first + value.shape[0], :] = value[:, part * 128 : part * 128 + 128].astype(ref.dtype)


def column_sum(value):
    return jnp.sum(value, axis=0, keepdims=True)


def attention_forward_stage(
    group, weights, gather, scatter, start,
    hidden, mods, weight, bias, proj, proj_bias,
    middle, branch, full, packed, attended, logsum,
):
    normal, _ = norm_parts(hidden[...])
    full[token_rows(group.me), :] = (normal * (1.0 + mods[1:2]) + mods[0:1]).astype(BF16)
    start()
    gather.start()
    weights.step(0)
    for chip in range(4):
        gather.arrive(chip)
        rows = chip_rows(group.chips[chip])
        packed[rows, :] = (nt(full[rows, :], weight[...]) + bias[...]).astype(BF16)
        if chip == 1:
            weights.step(1)
    weights.step(2)
    order = (3, 2, 1, 0)
    for place, chip in enumerate(order):
        rows = chip_rows(group.chips[chip])
        for head in range(2):
            query = packed[rows, head * 64 : head * 64 + 64] * BF16(HEAD_DIM**-0.5)
            key = packed[:, 128 + head * 64 : 192 + head * 64]
            value = packed[:, 256 + head * 64 : 320 + head * 64]
            scores = nt(key, query)
            top = jnp.max(scores, axis=0, keepdims=True)
            raised = jnp.exp(scores - top)
            total = jnp.sum(raised, axis=0, keepdims=True)
            output = tn(value, raised.astype(BF16)) * (1.0 / total)
            attended[rows, head * 64 : head * 64 + 64] = output.T.astype(BF16)
            logsum[head : head + 1, rows] = top + jnp.log(total)
        scatter.push(chip, lambda device: nn(attended[token_rows(device), :], proj[...]))
        if place:
            scatter.relay(order[place - 1])
    scatter.across()
    scatter.relay(0)
    weights.step(3)
    result = scatter.result() + proj_bias[...]
    branch[...] = result
    middle[...] = hidden[...] + mods[2:3] * result
    gather.finish()
    scatter.finish()


def mlp_forward_stage(
    group, weights, gather, scatter, ready,
    middle, mods, weight, bias, weight_two, bias_two,
    output, branch, full, inner, active,
):
    normal, _ = norm_parts(middle[...])
    full[token_rows(group.me), :] = (normal * (1.0 + mods[4:5]) + mods[3:4]).astype(BF16)
    gather.start()
    ready()
    weights.step(1)
    for chip in range(4):
        gather.arrive(chip)
        rows = chip_rows(group.chips[chip])
        value = nt(full[rows, :], weight[...]) + bias[...]
        inner[rows, :] = value
        bent = jnp.tanh(GELU_COEF * (value + 0.044715 * value * value * value))
        active[rows, :] = (0.5 * value * (1.0 + bent)).astype(BF16)
        scatter.push(chip, lambda device: nn(active[token_rows(device), :], weight_two[...]))
        if chip:
            scatter.relay(chip - 1)
        if chip == 2:
            weights.step(2)
    scatter.relay(3)
    scatter.across()
    weights.step(3)

    def end():
        result = scatter.result() + bias_two[...]
        branch[...] = result
        output[...] = middle[...] + mods[5:6] * result
        gather.finish()
        scatter.finish()

    return end


def mlp_backward_stage(
    group, owned_sum, gather, scatter, start, start_result,
    grad, mods, middle, branch, branch_one, weight, weight_two, full_two, inner, active,
    grad_middle, grad_attn, sums, weight_grads, bias_grad, full, grad_inner,
):
    if gather:
        full[token_rows(group.me), :] = (mods[5:6] * grad[...]).astype(BF16)
        start()
        gather.start()
    owned_sum.step(0)
    sums[1:2, :] = column_sum(full[token_rows(group.me), :].astype(F32))
    total = jnp.zeros((1, inner.shape[1]), F32)
    for chip in range(4):
        if gather:
            gather.arrive(chip)
        rows = chip_rows(group.chips[chip])
        grad_active = nt(full[rows, :], weight_two[...])
        value = inner[rows, :]
        bent = jnp.tanh(GELU_COEF * (value + 0.044715 * value * value * value))
        slope = GELU_COEF * (1.0 + (3 * 0.044715) * value * value)
        low = (grad_active * (0.5 * (1.0 + bent) + 0.5 * value * (1.0 - bent * bent) * slope)).astype(BF16)
        grad_inner[rows, :] = low
        total = total + column_sum(low.astype(F32))
        scatter.push(chip, lambda device: nn(grad_inner[token_rows(device), :], weight[...]))
        if chip:
            scatter.relay(chip - 1)
        if chip == 1:
            owned_sum.step(1)
    scatter.relay(3)
    scatter.across()
    owned_sum.step(2)
    bias_grad[...] = total
    units = weight.shape[0] // 2
    for half in range(2):
        cols = slice(half * units, half * units + units)
        store_blocks(weight_grads, half, 0, tn(grad_inner[:, cols], full_two[...]))
        store_blocks(weight_grads, half, units, tn(active[:, cols], full[...]))
    owned_sum.step(3)
    start_result()
    sums[0:1, :] = column_sum(grad[...] * branch[...])
    result = scatter.result()
    normal, inverse = norm_parts(middle[...])
    sums[2:3, :] = column_sum(result)
    sums[3:4, :] = column_sum(result * normal)
    back = grad[...] + norm_back(normal, inverse, (1.0 + mods[4:5]) * result)
    grad_middle[...] = back
    low = (mods[2:3] * back).astype(BF16)
    grad_attn[...] = low
    sums[4:5, :] = column_sum(back * branch_one[...])
    sums[5:6, :] = column_sum(low.astype(F32))
    owned_sum.step(4)
    if gather:
        gather.finish()
    scatter.finish()


def attention_backward_stage(
    group, owned_sum, gather, scatter,
    grad_middle, grad_attn, mods, hidden, weight, proj, full_one, packed, attended, logsum,
    grad_input, sums, weight_grads, bias_grad, full, grad_packed, key_grad, value_grad,
):
    full[token_rows(group.me), :] = grad_attn[...]
    gather.start()
    owned_sum.step(0)
    scale = HEAD_DIM**-0.5
    for chip in range(4):
        gather.arrive(chip)
        rows = chip_rows(group.chips[chip])
        grad_out = nt(full[rows, :], proj[...]).astype(BF16)
        for head in range(2):
            query = packed[rows, head * 64 : head * 64 + 64] * BF16(scale)
            key = packed[:, 128 + head * 64 : 192 + head * 64]
            value = packed[:, 256 + head * 64 : 320 + head * 64]
            part = grad_out[:, head * 64 : head * 64 + 64]
            probs = jnp.exp(nt(key, query) - logsum[head : head + 1, rows])
            grad_probs = nt(value, part)
            delta = jnp.sum(probs * grad_probs, axis=0, keepdims=True)
            grad_scores = (probs * (grad_probs - delta)).astype(BF16)
            grad_packed[rows, head * 64 : head * 64 + 64] = (tn(grad_scores, key) * scale).astype(BF16)
            key_term = nn(grad_scores, query)
            value_term = nn(probs.astype(BF16), part)
            if chip == 0:
                key_grad[head] = key_term
                value_grad[head] = value_term
            else:
                key_grad[head] += key_term
                value_grad[head] += value_term
        if chip == 1:
            owned_sum.step(1)
    for head in range(2):
        grad_packed[:, 128 + head * 64 : 192 + head * 64] = key_grad[head].astype(BF16)
        grad_packed[:, 256 + head * 64 : 320 + head * 64] = value_grad[head].astype(BF16)
    order = (3, 2, 1, 0)
    for place, chip in enumerate(order):
        scatter.push(chip, lambda device: nn(grad_packed[token_rows(device), :], weight[...]))
        if place:
            scatter.relay(order[place - 1])
    scatter.across()
    scatter.relay(0)
    owned_sum.step(2)
    for part in range(3):
        term = tn(grad_packed[:, part * 128 : part * 128 + 128], full_one[...])
        for half in range(2):
            store_blocks(weight_grads, half, part * 64, term[half * 64 : half * 64 + 64])
    term = tn(attended[...], full[...])
    for half in range(2):
        store_blocks(weight_grads, half, 192, term[half * 64 : half * 64 + 64])
    bias_grad[...] = column_sum(grad_packed[...].astype(F32))
    owned_sum.step(3)
    result = scatter.result()
    normal, inverse = norm_parts(hidden[...])
    sums[6:7, :] = column_sum(result)
    sums[7:8, :] = column_sum(result * normal)
    grad_input[...] = grad_middle[...] + norm_back(normal, inverse, (1.0 + mods[1:2]) * result)
    owned_sum.step(4)
    gather.finish()
    scatter.finish()


class Nothing:
    def step(self, step):
        pass


def forward_kernel(more, *refs):
    hidden, mods, weight, bias, proj, proj_bias, inner_bias, bias_two, mlp_rows, *refs = refs
    if more:
        next_rows, *refs = refs
    middle, branch, full, packed, attended, logsum, fc1, fc2, output, branch_two, full_two, inner, active, *refs = refs
    if more:
        next_qkv, next_proj, *refs = refs
    land, own_send, own_recv, *refs = refs
    if more:
        next_land, next_send, next_recv, *refs = refs
    send, recv, *scatter_refs = refs
    group, owners = Group(), Owners()
    partners = group.near + owners.near
    greet(partners)
    weights = OwnersGather(owners, land, own_send, own_recv)
    land[owners.slot] = mlp_rows[...]
    scatter = Scatter(group, *scatter_refs)
    attention_forward_stage(
        group, weights, Gather(group, full, send, recv), scatter, lambda: met(partners),
        hidden, mods, weight, bias, proj, proj_bias, middle, branch, full, packed, attended, logsum,
    )
    following = Nothing()
    if more:
        following = OwnersGather(owners, next_land, next_send, next_recv)
        next_land[owners.slot] = next_rows[...]
    following.step(0)

    def ready():
        weights.step(4)
        place_mlp(land, fc1, fc2)

    mlp_forward_stage(
        group, following, Gather(group, full_two, send, recv), scatter, ready,
        middle, mods, fc1, inner_bias, fc2, bias_two, output, branch_two, full_two, inner, active,
    )()
    following.step(4)
    if more:
        place_attention(next_land, next_qkv, next_proj)


def backward_kernel(more, *refs):
    grad, mods, middle, branch_two, branch, fc1, fc2, full_two, inner, active, *refs = refs
    hidden, qkv, proj, full_one, packed, attended, logsum, *refs = refs
    if more:
        parts, *refs = refs
    grad_input, sums, attn_parts, qkv_sum, fc1_sum, mlp_owned, *refs = refs
    if more:
        attn_owned, *refs = refs
    grad_middle, grad_attn, mlp_parts, full, full_attn, grad_inner, grad_packed, key_grad, value_grad, *refs = refs
    mlp_refs, refs = refs[:10], refs[10:]
    if more:
        attn_refs, refs = refs[:10], refs[10:]
    send, recv, *scatter_refs = refs
    group, owners = Group(), Owners()
    partners = group.near + owners.near
    greet(partners)
    scatter = Scatter(group, *scatter_refs)
    owned = OwnersScatter(owners, parts, attn_owned, *attn_refs) if more else Nothing()
    mlp_backward_stage(
        group, owned, Gather(group, full, send, recv), scatter, lambda: met(partners), lambda: None,
        grad, mods, middle, branch_two, branch, fc1, fc2, full_two, inner, active,
        grad_middle, grad_attn, sums, mlp_parts, fc1_sum, full, grad_inner,
    )
    owned = OwnersScatter(owners, mlp_parts, mlp_owned, *mlp_refs)
    attention_backward_stage(
        group, owned, Gather(group, full_attn, send, recv), scatter,
        grad_middle, grad_attn, mods, hidden, qkv, proj, full_one, packed, attended, logsum,
        grad_input, sums, attn_parts, qkv_sum, full_attn, grad_packed, key_grad, value_grad,
    )


class Beside:
    def __init__(self, weights, gather):
        self.weights, self.gather = weights, gather

    def step(self, step):
        self.weights.step(step)
        if step == 2:
            self.gather.start()
            self.gather.arrive(0)
        if step == 3:
            self.gather.arrive(1)
            self.gather.arrive(2)
        if step == 4:
            self.gather.arrive(3)
            self.gather.finish()


def turn_kernel(
    hidden, mods, qkv, qkv_bias, proj, proj_bias, inner_bias, bias_two, mlp_rows, grad,
    output, grad_input, sums, attn_parts, qkv_sum, fc1_sum, mlp_owned,
    middle, branch, branch_two, full, packed, attended, logsum, fc1, fc2, full_two, inner, active,
    land, own_send, own_recv,
    grad_middle, grad_attn, mlp_parts, full_grad, full_attn, grad_inner, grad_packed, key_grad, value_grad, *refs,
):
    mlp_refs, refs = refs[:10], refs[10:]
    back_refs, refs = refs[:8], refs[8:]
    grad_send, grad_recv, send, recv, *scatter_refs = refs
    group, owners = Group(), Owners()
    partners = group.near + owners.near
    greet(partners)
    weights = OwnersGather(owners, land, own_send, own_recv)
    land[owners.slot] = mlp_rows[...]
    full_grad[token_rows(group.me), :] = (mods[5:6] * grad[...]).astype(BF16)
    beside = Beside(weights, Gather(group, full_grad, grad_send, grad_recv))
    scatter, back = Scatter(group, *scatter_refs), Scatter(group, *back_refs)
    attention_forward_stage(
        group, beside, Gather(group, full, send, recv), scatter, lambda: met(partners),
        hidden, mods, qkv, qkv_bias, proj, proj_bias, middle, branch, full, packed, attended, logsum,
    )

    def ready():
        beside.step(4)
        place_mlp(land, fc1, fc2)

    end = mlp_forward_stage(
        group, Nothing(), Gather(group, full_two, send, recv), scatter, ready,
        middle, mods, fc1, inner_bias, fc2, bias_two, output, branch_two, full_two, inner, active,
    )
    mlp_backward_stage(
        group, Nothing(), None, back, None, end,
        grad, mods, middle, branch_two, branch, fc1, fc2, full_two, inner, active,
        grad_middle, grad_attn, sums, mlp_parts, fc1_sum, full_grad, grad_inner,
    )
    owned = OwnersScatter(owners, mlp_parts, mlp_owned, *mlp_refs)
    attention_backward_stage(
        group, owned, Gather(group, full_attn, send, recv), back,
        grad_middle, grad_attn, mods, hidden, qkv, proj, full, packed, attended, logsum,
        grad_input, sums, attn_parts, qkv_sum, full_attn, grad_packed, key_grad, value_grad,
    )


def first_kernel(
    rows, terms, bias, qkv, proj, halves, mods,
    land, own_send, own_recv, x_in, y_out, y_in, z_out, z_in, send, recv, all_send, all_recv,
):
    group, owners = Group(), Owners()
    partners = owners.near + (owners.to_across,) + tuple({"g": device} for device in group.everyone)
    greet(partners)
    weights = OwnersGather(owners, land, own_send, own_recv)
    land[owners.slot] = rows[...]
    halves[owners.x] = bias[...]
    met(partners)
    other = 1 - owners.x
    along_x = remote(terms.at[pl.ds(other * 8, 8)], x_in, send, recv, 0, owners.to_x)
    along_x.start()
    bias_there = remote(bias, halves.at[owners.x], send, recv, 1, owners.to_x)
    bias_there.start()
    weights.step(0)
    along_x.wait_recv()
    y_out[owners.x] = terms[pl.ds(owners.x * 8 + (1 - owners.y) * 4, 4)]
    y_out[other] = x_in[pl.ds((1 - owners.y) * 4, 4)]
    along_y = remote(y_out, y_in, send, recv, 2, owners.to_y)
    along_y.start()
    weights.step(1)
    along_y.wait_recv()
    own = terms[pl.ds(owners.x * 8 + owners.y * 4, 4)] + y_in[owners.x]
    far = x_in[pl.ds(owners.y * 4, 4)] + y_in[other]
    for z in range(4):
        z_out[z, owners.x] = own[z]
        z_out[z, other] = far[z]
    along_z = [
        remote(z_out.at[z], z_in.at[number], send, recv, 3 + number, device)
        for number, (z, device) in enumerate(
            ((owners.up, owners.to_up), (owners.across, owners.to_across), (owners.down, owners.to_down))
        )
    ]
    for copy in along_z:
        copy.start()
    weights.step(2)
    total = z_out[owners.z]
    for number, copy in enumerate(along_z):
        copy.wait_recv()
        total = total + z_in[number]
    mods[group.me] = total
    around = [
        remote(mods.at[group.me], mods.at[group.me], all_send, all_recv, number, {"g": device})
        for number, device in enumerate(group.everyone)
    ]
    for copy in around:
        copy.start()
    weights.step(3)
    for number, device in enumerate(group.everyone):
        remote(mods.at[device], mods.at[device], all_send, all_recv, number, {"g": device}).wait_recv()
    remote(bias, halves.at[other], send, recv, 1, owners.to_x).wait_recv()
    weights.step(4)
    place_attention(land, qkv, proj)
    for copy in (along_x, bias_there, along_y, *along_z, *around):
        copy.wait_send()


def last_kernel(
    parts, blocks, own, ada, owned, every, summed, copies, act_grad,
    *refs,
):
    group, owners = Group(), Owners()
    partners = owners.near + tuple({"g": device} for device in group.everyone)
    greet(partners)
    owned_sum = OwnersScatter(owners, parts, owned, *refs[:10])
    own_send, own_recv, inbox, send, recv, all_send, all_recv, *refs = refs[10:]
    act_all, act_out, act_in, act_send, act_recv, x_send, x_recv = refs
    gather = OwnersGather(owners, every, own_send, own_recv)
    met(partners)
    around = [
        remote(blocks.at[device], inbox.at[number], send, recv, number, {"g": device})
        for number, device in enumerate(group.everyone)
    ]
    for copy in around:
        copy.start()
    owned_sum.step(0)
    total = blocks[group.me]
    for number, copy in enumerate(around):
        copy.wait_recv()
        total = total + inbox[number]
    rows = blocks.shape[1]
    every[owners.slot, 0:rows] = total
    every[owners.slot, rows:] = own[...]
    gather.step(0)
    gather.step(1)
    gather.step(2)
    owned_sum.step(1)
    gather.step(3)
    gather.step(4)
    act = jnp.zeros(act_out.shape, F32)
    lines = ada.shape[2] // 128
    for layer in range(ada.shape[0]):
        for line in range(lines):
            place = layer * lines + line
            left = jnp.where(owners.x == 0, every[:, place, :], every[:, ada.shape[0] * lines + place, :])
            right = ada[layer, :, line * 128 : line * 128 + 128].astype(F32)
            act = act + lax.dot_general(
                left, right, (((1,), (1,)), ((), ())), precision=lax.Precision.HIGHEST, preferred_element_type=F32
            )
    act_all[group.me] = act
    acts = [
        remote(act_all.at[group.me], act_all.at[group.me], act_send, act_recv, number, {"g": device})
        for number, device in enumerate(group.everyone)
    ]
    for copy in acts:
        copy.start()
    total = every[0]
    for slot in range(1, 16):
        total = total + every[slot]
    summed[...] = total
    copies[group.me] = total[0:rows]
    spread = [
        remote(copies.at[group.me], copies.at[group.me], all_send, all_recv, number, {"g": device})
        for number, device in enumerate(group.everyone)
    ]
    for copy in spread:
        copy.start()
    owned_sum.step(2)
    for number, device in enumerate(group.everyone):
        remote(act_all.at[device], act_all.at[device], act_send, act_recv, number, {"g": device}).wait_recv()
    act = act_all[0]
    for device in range(1, 8):
        act = act + act_all[device]
    act_out[...] = act
    over = remote(act_out, act_in, x_send, x_recv, 0, owners.to_x)
    over.start()
    owned_sum.step(3)
    for number, device in enumerate(group.everyone):
        remote(copies.at[device], copies.at[device], all_send, all_recv, number, {"g": device}).wait_recv()
    over.wait_recv()
    act_grad[...] = act_out[...] + act_in[...]
    owned_sum.step(4)
    for copy in (*around, *spread, *acts, over):
        copy.wait_send()


def plain_call(kernel, number, outs, scratch, *operands):
    space = pl.BlockSpec(memory_space=pltpu.VMEM)
    return pl.pallas_call(
        kernel,
        out_shape=[jax.ShapeDtypeStruct(shape, kind) for shape, kind in outs],
        in_specs=[space] * len(operands),
        out_specs=[space] * len(outs),
        scratch_shapes=scratch,
        compiler_params=pltpu.CompilerParams(
            collective_id=number, has_side_effects=True, vmem_limit_bytes=VMEM_LIMIT
        ),
        cost_estimate=pl.CostEstimate(flops=10**10, bytes_accessed=8 << 20, transcendentals=1 << 20),
    )(*operands)


def call(kernel, number, outs, scratch, *operands):
    pair = [pltpu.SemaphoreType.DMA((9,)), pltpu.SemaphoreType.DMA((9,))]
    return plain_call(kernel, number, outs, [*scratch, *pair, *Scatter.scratch], *operands)


def first(rows, terms, bias):
    width = 1024
    outs = [
        ((384, width), BF16), ((128, width), BF16), ((2, *bias.shape), F32), ((8, 2, 8, 128), F32),
    ]
    scratch = [
        pltpu.VMEM((16, *rows.shape), BF16), *OwnersGather.scratch,
        pltpu.VMEM((8, 8, 128), F32), pltpu.VMEM((2, 4, 8, 128), F32), pltpu.VMEM((2, 4, 8, 128), F32),
        pltpu.VMEM((4, 2, 8, 128), F32), pltpu.VMEM((3, 2, 8, 128), F32),
        pltpu.SemaphoreType.DMA((6,)), pltpu.SemaphoreType.DMA((6,)),
        pltpu.SemaphoreType.DMA((7,)), pltpu.SemaphoreType.DMA((7,)),
    ]
    return plain_call(first_kernel, 10, outs, scratch, rows, terms, bias)


def last(parts, blocks, own, ada):
    rows = blocks.shape[1]
    outs = [
        (parts.shape[1:], F32), ((16, rows + own.shape[0], 128), F32), ((rows + own.shape[0], 128), F32),
        (blocks.shape, F32), ((16, 128), F32),
    ]
    scratch = [
        *OwnersScatter.scratch(parts.shape[1]), *OwnersGather.scratch, pltpu.VMEM((7, rows, 128), F32),
        *([pltpu.SemaphoreType.DMA((7,))] * 4),
        pltpu.VMEM((8, 16, 128), F32), pltpu.VMEM((16, 128), F32), pltpu.VMEM((16, 128), F32),
        *([pltpu.SemaphoreType.DMA((7,))] * 2), *([pltpu.SemaphoreType.DMA((1,))] * 2),
    ]
    return plain_call(last_kernel, 11, outs, scratch, parts, blocks, own, ada)


def forward(operands, rows=None):
    hidden, weight, proj, mlp_rows = operands[0], operands[2], operands[4], operands[8]
    width, units = hidden.shape[1], mlp_rows.shape[0]
    token, whole = ((TOK, width), F32), ((SEQ_LEN, width), BF16)
    outs = [
        token, token, whole, ((SEQ_LEN, weight.shape[0]), BF16), ((SEQ_LEN, proj.shape[0]), BF16), ((2, SEQ_LEN), F32),
        ((units, width), BF16), ((units, width), BF16),
        token, token, whole, ((SEQ_LEN, units), F32), ((SEQ_LEN, units), BF16),
    ]
    scratch = [pltpu.VMEM((16, *mlp_rows.shape), BF16), *OwnersGather.scratch]
    if rows is None:
        return call(functools.partial(forward_kernel, False), 0, outs, scratch, *operands)
    outs += [(weight.shape, BF16), (proj.shape, BF16)]
    scratch += [pltpu.VMEM((16, *rows.shape), BF16), *OwnersGather.scratch]
    return call(functools.partial(forward_kernel, True), 1, outs, scratch, *operands, rows)


def backward(operands, parts=None):
    grad, fc1, qkv = operands[0], operands[5], operands[11]
    width, units = grad.shape[1], fc1.shape[0]
    outs = [
        ((TOK, width), F32), ((8, width), F32), ((16, 256, 128), BF16),
        ((1, qkv.shape[0]), F32), ((1, units), F32), ((units, 128), F32),
    ]
    if parts is not None:
        outs += [(parts.shape[1:], F32)]
    scratch = [
        pltpu.VMEM((TOK, width), F32),
        pltpu.VMEM((TOK, width), BF16),
        pltpu.VMEM((16, units, 128), BF16),
        pltpu.VMEM((SEQ_LEN, width), BF16),
        pltpu.VMEM((SEQ_LEN, width), BF16),
        pltpu.VMEM((SEQ_LEN, units), BF16),
        pltpu.VMEM((SEQ_LEN, qkv.shape[0]), BF16),
        pltpu.VMEM((2, SEQ_LEN, HEAD_DIM), F32),
        pltpu.VMEM((2, SEQ_LEN, HEAD_DIM), F32),
        *OwnersScatter.scratch(units),
    ]
    if parts is None:
        return call(functools.partial(backward_kernel, False), 2, outs, scratch, *operands)
    scratch += OwnersScatter.scratch(parts.shape[1])
    return call(functools.partial(backward_kernel, True), 3, outs, scratch, *operands, parts)


def turn(*operands):
    hidden, qkv, proj, mlp_rows = operands[0], operands[2], operands[4], operands[8]
    width, units, cols = hidden.shape[1], mlp_rows.shape[0], qkv.shape[0]
    outs = [
        ((TOK, width), F32), ((TOK, width), F32), ((8, width), F32), ((16, 256, 128), BF16),
        ((1, cols), F32), ((1, units), F32), ((units, 128), F32),
    ]
    token, whole = pltpu.VMEM((TOK, width), F32), pltpu.VMEM((SEQ_LEN, width), BF16)
    head = pltpu.VMEM((2, SEQ_LEN, HEAD_DIM), F32)
    scratch = [
        token, token, token, whole, pltpu.VMEM((SEQ_LEN, cols), BF16), pltpu.VMEM((SEQ_LEN, proj.shape[0]), BF16),
        pltpu.VMEM((2, SEQ_LEN), F32), pltpu.VMEM((units, width), BF16), pltpu.VMEM((units, width), BF16),
        whole, pltpu.VMEM((SEQ_LEN, units), F32), pltpu.VMEM((SEQ_LEN, units), BF16),
        pltpu.VMEM((16, units, 128), BF16), *OwnersGather.scratch,
        token, pltpu.VMEM((TOK, width), BF16), pltpu.VMEM((16, units, 128), BF16), whole, whole,
        pltpu.VMEM((SEQ_LEN, units), BF16), pltpu.VMEM((SEQ_LEN, cols), BF16), head, head,
        *OwnersScatter.scratch(units), *Scatter.scratch,
        pltpu.SemaphoreType.DMA((9,)), pltpu.SemaphoreType.DMA((9,)),
    ]
    return call(turn_kernel, 4, outs, scratch, *operands)


RX = ("row", "xh")
ALL = ("row", "xh", "g")


def highest(left, right):
    return jnp.dot(left, right, precision=lax.Precision.HIGHEST, preferred_element_type=F32)


def highest_tn(left, right):
    return lax.dot_general(
        left, right, (((0,), (0,)), ((), ())), precision=lax.Precision.HIGHEST, preferred_element_type=F32
    )


def highest_nt(left, right):
    return lax.dot_general(
        left, right, (((1,), (1,)), ((), ())), precision=lax.Precision.HIGHEST, preferred_element_type=F32
    )


def small_sums(sums, qkv_sum, fc1_sum):
    mod_grad = jnp.concatenate([sums[6:8], sums[4:5], sums[2:4], sums[0:1]])
    return mod_grad, sums[5], sums[1], qkv_sum, fc1_sum


def on_device(
    tokens, cotangent, timestep, class_label, class_table, ada_weight, ada_bias, qkv_weight, qv_bias,
    proj_weight, proj_bias, fc1_weight, fc1_bias, fc2_weight, fc2_bias,
):
    row_index, half_index, _ = (lax.axis_index(axis) for axis in ALL)
    width = tokens.shape[1]
    width_part = class_table.shape[1]
    latent_count = timestep.shape[0]
    layer_count, _, ada_cols = ada_weight.shape
    units = fc1_weight.shape[2]
    attn_rows = [jnp.concatenate([qkv_weight[l].T, proj_weight[l]]) for l in range(layer_count)]
    mlp_rows = [jnp.concatenate([fc1_weight[l].T, fc2_weight[l]]) for l in range(layer_count)]
    column_ids = row_index * width_part + lax.iota(jnp.int32, width_part)
    half_width = width // 2
    frequency = jnp.exp(-LOG_BASE * (column_ids % half_width).astype(F32) / half_width)
    angles = timestep.astype(F32)[:, None] * frequency[None, :]
    waves = jnp.where(column_ids[None, :] < half_width, jnp.cos(angles), jnp.sin(angles))
    class_hot = (class_label[:, None] == lax.iota(jnp.int32, class_table.shape[0])[None, :]).astype(F32)
    condition = waves + highest(class_hot, class_table.astype(F32))
    cond_act = condition * jax.nn.sigmoid(condition)
    ada_float = ada_weight.astype(F32)
    terms = jnp.stack([highest(cond_act, ada_float[l]) for l in range(layer_count)], axis=1)
    terms = terms.reshape(latent_count // 2, 2, -1, 128).swapaxes(0, 1).reshape(latent_count, -1, 128)
    lines = layer_count * ada_cols // 128
    terms = jnp.pad(terms, ((0, 0), (0, 8 - lines), (0, 0)))
    bias_rows = jnp.concatenate([qv_bias.reshape(layer_count, -1), fc1_bias], axis=1).reshape(-1, 128)
    bias_count = bias_rows.shape[0]
    bias_rows = jnp.pad(bias_rows, ((0, 8 - bias_count), (0, 0)))
    qkv, proj, halves, mod_parts = first(attn_rows[0], terms, bias_rows)
    modulation = mod_parts[:, :, :lines].reshape(8, 2, layer_count, ada_cols).transpose(2, 1, 0, 3)
    modulation = modulation.reshape(layer_count, 6 * width) + ada_bias
    mods = jnp.pad(modulation.reshape(layer_count, 6, width), ((0, 0), (0, 2), (0, 0)))
    halves = halves[:, :bias_count].reshape(2, layer_count, -1)

    saved = []
    hidden = tokens
    small = [None] * layer_count
    attn_grads, mlp_grads = [None] * layer_count, [None] * layer_count
    for number in range(layer_count):
        query = halves[:, number, :HEAD_DIM].reshape(1, -1)
        value = halves[:, number, HEAD_DIM : 2 * HEAD_DIM].reshape(1, -1)
        qkv_bias = jnp.concatenate([query, jnp.zeros_like(query), value], axis=1)
        inner_bias = halves[:, number, 2 * HEAD_DIM :].reshape(1, -1)
        operands = (
            hidden, mods[number], qkv, qkv_bias, proj, proj_bias[number : number + 1], inner_bias,
            fc2_bias[number : number + 1], mlp_rows[number],
        )
        if number + 1 < layer_count:
            (
                middle, branch, full, packed, attended, logsum, fc1, fc2, output, branch_two, full_two, inner, active, *later
            ) = forward(operands, attn_rows[number + 1])
            saved.append(
                (middle, branch_two, branch, fc1, fc2, full_two, inner, active, hidden, qkv, proj, full, packed, attended, logsum)
            )
            hidden = output
            qkv, proj = later
        else:
            mixed, grad, sums, attn_parts, qkv_sum, fc1_sum, mlp_grads[number] = turn(*operands, cotangent)
            small[number] = small_sums(sums, qkv_sum, fc1_sum)
    for number in reversed(range(layer_count - 1)):
        grad, sums, attn_parts, qkv_sum, fc1_sum, mlp_grads[number], attn_grads[number + 1] = backward(
            (grad, mods[number], *saved[number]), attn_parts
        )
        small[number] = small_sums(sums, qkv_sum, fc1_sum)
    tokens_grad = grad

    mod_grad, proj_sum, fc2_sum, qkv_sum, fc1_sum = (jnp.stack(parts) for parts in zip(*small))
    mod_send = mod_grad.reshape(layer_count, 2, 8, ada_cols).transpose(2, 1, 0, 3).reshape(8, -1)
    bias_send = jnp.concatenate([proj_sum, fc2_sum]).reshape(2 * layer_count, 8, -1).swapaxes(0, 1).reshape(8, -1)
    mod_size = mod_send.shape[1]
    send = jnp.concatenate([mod_send, bias_send], axis=1).reshape(8, -1, 128)
    qv_sum = qkv_sum.reshape(layer_count, 3, 2, HEAD_DIM)[:, ::2].transpose(2, 0, 1, 3).reshape(2, -1)
    fc1_half = fc1_sum.reshape(layer_count, 2, units).swapaxes(0, 1).reshape(2, -1)
    own = jnp.concatenate([qv_sum, fc1_half], axis=1).reshape(-1, 128)
    own_count = own.shape[0]
    own = jnp.pad(own, ((0, 16 - own_count), (0, 0)))
    attn_grads[0], every, summed, copies, act_grad = last(attn_parts, send, own, ada_weight)
    every = every[:, : mod_size // 128].reshape(4, 2, 2, 2, layer_count, ada_cols)
    mod_cols = lax.dynamic_index_in_dim(every, half_index, axis=3, keepdims=False)
    mod_cols = mod_cols.transpose(1, 0, 2, 3, 4).reshape(latent_count, layer_count, ada_cols)
    copies = copies.reshape(8, -1)
    ada_bias_grad = copies[:, :mod_size].reshape(8, 2, layer_count, ada_cols).transpose(2, 1, 0, 3)
    ada_bias_grad = ada_bias_grad.reshape(layer_count, 6 * width)
    bias_total = copies[:, mod_size:].reshape(8, 2 * layer_count, -1).swapaxes(0, 1).reshape(2, layer_count, width)
    own_total = summed[send.shape[1] :][:own_count].reshape(2, -1)
    own_total = lax.dynamic_index_in_dim(own_total, half_index, keepdims=False)
    qv_bias_grad = own_total[: layer_count * 2 * HEAD_DIM].reshape(layer_count, 2, HEAD_DIM)
    fc1_bias_grad = own_total[layer_count * 2 * HEAD_DIM :].reshape(layer_count, units)
    ada_weight_grad = jnp.stack([highest_tn(cond_act, mod_cols[:, l]) for l in range(layer_count)])
    act_grad = act_grad.reshape(4, 2, 2, width_part).swapaxes(0, 1).reshape(latent_count, width_part)
    gate = jax.nn.sigmoid(condition)
    cond_grad = act_grad * (gate * (1.0 + condition * (1.0 - gate)))
    table_grad = highest_tn(class_hot, cond_grad)
    attn_grads, mlp_grads = jnp.stack(attn_grads), jnp.stack(mlp_grads)
    return (
        mixed,
        tokens_grad,
        cond_grad,
        table_grad,
        ada_weight_grad,
        ada_bias_grad,
        attn_grads[:, :192].swapaxes(1, 2),
        qv_bias_grad,
        attn_grads[:, 192:],
        bias_total[0],
        mlp_grads[:, :units].swapaxes(1, 2),
        fc1_bias_grad,
        mlp_grads[:, units:],
        bias_total[1],
    )


def solution(mesh):
    split = Mesh(mesh.devices.reshape(mesh.shape["row"], 2, 8), ALL)
    col = ("xh", "g")
    in_specs = (
        P(ALL, None), P(ALL, None), P(), P(), P(None, "row"), P(None, "row", col), P(),
        P(None, "row", col), P(None, None, col), P(None, col, "row"), P(), P(None, "row", col),
        P(None, col), P(None, col, "row"), P(),
    )
    out_specs = (
        P(ALL, None), P(ALL, None), P(None, "row"), P(None, "row"), P(None, "row", col), P(),
        P(None, "row", col), P(None, None, col), P(None, col, "row"), P(), P(None, "row", col),
        P(None, col), P(None, col, "row"), P(),
    )
    return jax.shard_map(on_device, mesh=split, in_specs=in_specs, out_specs=out_specs, check_vma=False)
```
